32 devices in a mesh: groups: 2 (over x), ep: 8 (over z, y), sub: 2 (over core).
Axes of the slice: x: 2, y: 2, z: 4, core: 2. Of those that a mesh axis runs over, the one named last changes fastest.
Arguments:
- tokens: bfloat16 [2048, 2048], P(('groups', 'ep', 'sub')), parts along dimension 0, may hold values from -6 to 6
- routes: int32 [2048, 8], P(('groups', 'ep', 'sub')), parts along dimension 0, may hold values from 0 to 15, all different within a row; in each aligned block of 64 rows (0 to 63, 64 to 127, ...) at most 64 rows name the same one
- gates: float32 [2048, 8], P(('groups', 'ep', 'sub')), parts along dimension 0, may hold values from 0.05 to 1
- priority: int32 [2048], P(('groups', 'ep', 'sub')), parts along dimension 0, may hold values from 0 to 15
- capacity: int32 [16], replicated, may hold values from 320 to 640, as said below
- w_gate: bfloat16 [16, 2048, 768], P(('ep', 'sub')), may hold values from -0.125 to 0.125
- w_up: bfloat16 [16, 2048, 768], P(('ep', 'sub')), may hold values from -0.125 to 0.125
- w_down: bfloat16 [16, 768, 2048], P(('ep', 'sub')), may hold values from -0.21875 to 0.21875
Outputs:
- mixed: bfloat16 [2048, 2048], P(('groups', 'ep', 'sub')), parts along dimension 0
The draws below stay inside these ranges and needn't reach their ends.
There are 2 independent parts, one for each index of `groups`. The reference program is written for one: setup_inputs(seed, part) draws one part's arguments, and reference() takes and returns one part's arrays. A program takes and returns all parts, laid end to end along the dimension named above; an argument that names none is the same for every part. Nothing has to cross between parts.
Inputs may be any that keep to these rules, and one draw needn't show every extreme that they name: `capacity`: each expert accepts between 320 and 640 entries; some expert accepts exactly 640.
All inputs are finite; a program needn't handle non-finite values.
Results may differ from the reference program's by a relative error of at most 0.0069.
Values may be sent and summed in bfloat16 or wider, within the bound.
No kernel may reach another device: no remote copies, remote signals or barrier semaphores. Data moves between devices by JAX's collectives and lax.ppermute only.
A program may use at most 64 MiB of HBM per device.

```python
import math
import jax
import jax.numpy as jnp
import numpy as np
from jax import lax

D = 2048
FF = 768
TOP = 8
PRIO = 16
TOK_DEV = 64
EXPERTS = 16
TOKENS = 1024
SLOT = 64
CAP = 640


def draw_capacity(key, part):
    key = jax.random.fold_in(key, 7)
    first, second = jax.random.split(key)
    values = jax.random.randint(first, (EXPERTS,), CAP // 2, CAP + 1)
    where_full = jax.random.randint(second, (), 0, EXPERTS)
    return jnp.where(jnp.arange(EXPERTS) == where_full, CAP, values).astype(jnp.int32)


def touch_ends(values, stream_key, least, high):
    index_at = [jax.random.randint(jax.random.fold_in(stream_key, axis), (), 0, length) for axis, length in enumerate(values.shape)]
    longest = values.shape.index(max(values.shape))
    neighbour = index_at[:longest] + [(index_at[longest] + 1) % values.shape[longest]] + index_at[longest + 1:]
    return values.at[tuple(index_at)].set(least).at[tuple(neighbour)].set(high)


def levels(own_key, extent, pieces, least, top_value):
    factor_of = 1.0
    for dim, blocks in pieces:
        heights = jax.random.uniform(jax.random.fold_in(jax.random.fold_in(own_key, 6), dim), (blocks,), jnp.float32, least / len(pieces), top_value / len(pieces))
        factor_of = factor_of * jnp.repeat(jnp.exp(heights), extent[dim] // blocks).reshape((-1,) + (1,) * (len(extent) - 1 - dim))
    return factor_of


def deal_out(stream_key, own, number, rows, amount, top, bound, slope):
    order = jax.random.permutation(stream_key, amount)
    crowded, ordinary = portions_of(amount, rows * top, bound, slope, True), portions_of(amount, rows * top, bound, slope, False)
    places = jnp.arange(amount)

    def named(sizes, offset_by):
        used = int((sizes > 0).sum())
        fixed = max(1, used // 4)
        moved = fixed + (places - fixed + offset_by * (used - fixed)) % max(1, amount - fixed)
        return jnp.zeros((amount,), jnp.int32).at[order[jnp.where(places < fixed, places, moved)]].set(jnp.asarray(sizes, jnp.int32))

    sizes = jnp.where(number % 4 == 0, named(crowded, number // 4), named(ordinary, number - number // 4 - 1))
    mixed = jax.random.permutation(jax.random.fold_in(own, 3), amount)
    source_of, sink = mixed[0:amount // 2 * 2:2], mixed[1:amount // 2 * 2:2]
    room = jnp.minimum(sizes[source_of] - 1, bound - sizes[sink]) // 2
    room = jnp.where((source_of == order[0]) | (sink == order[0]) | (sizes[sink] == 0), 0, jnp.maximum(room, 0))
    moved = jax.random.randint(jax.random.fold_in(own, 4), (amount // 2,), 0, 1 << 20) % (room + 1)
    sizes = sizes.at[source_of].add(-moved).at[sink].add(moved)
    members = jnp.searchsorted(jnp.cumsum(sizes), jnp.arange(rows * top), side="right").astype(jnp.int32)
    grid = members.reshape(top, rows).T
    grid = grid[jax.random.permutation(jax.random.fold_in(own, 1), rows)]
    offset_by = jax.random.randint(jax.random.fold_in(own, 2), (rows, 1), 0, top)
    return jnp.take_along_axis(grid, (jnp.arange(top)[None, :] + offset_by) % top, axis=1)


def portions_of(amount, total, most, skew, full):
    weights = [(1 << 20) // math.isqrt(grade ** skew) + 1 for grade in range(1, amount + 1)]
    largest = most if full else min(most, max(-(-total // amount), total * weights[0] // sum(weights)))
    least = 1 if total - largest >= amount - 1 else 0
    holding, spare = [largest] + [least] * (amount - 1), total - largest - least * (amount - 1)
    while spare > 0:
        movable = [i for i in range(1, amount) if holding[i] < largest] or [i for i in range(1, amount) if holding[i] < most]
        whole, budget = sum([weights[i] for i in movable]), spare
        for i in movable:
            addition = min(most - holding[i], max(1, budget * weights[i] // whole), spare)
            holding[i] = holding[i] + addition
            spare = spare - addition
    return np.array(holding)


def noise(rng, shape, scale, limit, cuts=(), kind=jnp.bfloat16):
    array = jax.random.normal(rng, shape, jnp.float32) * scale
    if len(cuts) > 0:
        array = levels(rng, shape, cuts, -0.22, 0.18) * array
    return jnp.clip(array, min=-limit, max=limit).astype(kind)


def setup_inputs(seed: int = 0, part: int = 0) -> dict:
    splits = jax.random.split(jax.random.key(seed), 9)
    own_keys = jax.random.split(jax.random.fold_in(splits[8], part), 9)
    tokens = noise(own_keys[0], (TOKENS, D), 1.0, 6.0, ((0, 16),))
    routes_keys = jax.random.split(jax.random.fold_in(own_keys[1], 1), TOKENS // TOK_DEV)
    routes_turns = jax.random.permutation(jax.random.fold_in(own_keys[1], 3), TOKENS // TOK_DEV)
    routes = jax.vmap(lambda own, number: deal_out(jax.random.fold_in(own_keys[1], 2), own, number, TOK_DEV, EXPERTS, TOP, SLOT, 2))(routes_keys, routes_turns).reshape((TOKENS, TOP))
    gates = jnp.clip(jnp.exp(math.log(1.0) - 2.9957323 * jax.random.uniform(own_keys[2], (TOKENS, TOP), jnp.float32) ** levels(own_keys[2], (TOKENS, TOP), ((0, 16),), -0.2, 0.2)), 0.05, 1.0)
    priority = touch_ends(jax.random.randint(own_keys[3], (TOKENS,), 0, PRIO), jax.random.fold_in(own_keys[3], 1), 0, PRIO - 1).astype(jnp.int32)
    capacity = draw_capacity(jax.random.fold_in(splits[8], 71), part)
    w_gate = noise(splits[5], (EXPERTS, D, FF), D ** -0.5, 0.125, ((0, 16),))
    w_up = noise(splits[6], (EXPERTS, D, FF), D ** -0.5, 0.125, ((0, 16),))
    w_down = noise(splits[7], (EXPERTS, FF, D), FF ** -0.5, 0.21875, ((0, 16),))
    return dict(tokens=tokens, routes=routes, gates=gates, priority=priority, capacity=capacity, w_gate=w_gate, w_up=w_up, w_down=w_down)


block_width = 128


def quantize(activations):
    count = activations.shape[0]
    blocks = activations.astype(jnp.float32).reshape(count, -1, block_width)
    largest = jnp.max(jnp.abs(blocks), axis=-1)
    scales = ((largest + 1e-6) / 448.0).astype(jnp.bfloat16)
    quantized = (blocks / scales.astype(jnp.float32)[..., None]).astype(jnp.bfloat16)
    return quantized.reshape(count, -1), scales


def expert_apply(quantized, scales, gate_matrix, up_matrix, down_matrix):
    count = quantized.shape[0]
    restored = quantized.reshape(count, -1, block_width).astype(jnp.float32) * scales.astype(jnp.float32)[..., None]
    restored = restored.astype(jnp.bfloat16).reshape(count, -1)
    gated = jnp.dot(restored, gate_matrix, preferred_element_type=jnp.float32)
    upward = jnp.dot(restored, up_matrix, preferred_element_type=jnp.float32)
    hidden = (jax.nn.silu(gated) * upward).astype(jnp.bfloat16)
    return jnp.dot(hidden, down_matrix, preferred_element_type=jnp.float32).astype(jnp.bfloat16)


def reference(tokens, routes, gates, priority, capacity, w_gate, w_up, w_down):
    quantized, scales = quantize(tokens)
    entries = TOKENS * TOP
    flat_expert = routes.reshape(-1).astype(jnp.int32)
    flat_token = (jnp.arange(entries, dtype=jnp.int32) // TOP).astype(jnp.int32)
    flat_prio = priority[flat_token].astype(jnp.int32)
    classes = (flat_expert * PRIO + flat_prio).astype(jnp.int32)
    totals = jnp.zeros((EXPERTS * PRIO,), jnp.int32).at[classes].add(1).reshape(EXPERTS, PRIO)
    below = (jnp.cumsum(totals, axis=1) - totals).reshape(-1)
    order = jnp.argsort(classes, stable=True).astype(jnp.int32)
    sorted_classes = classes[order]
    starts = jnp.searchsorted(sorted_classes, sorted_classes, side="left").astype(jnp.int32)
    within = jnp.zeros((entries,), jnp.int32).at[order].set(jnp.arange(entries, dtype=jnp.int32) - starts)
    rank = below[classes] + within
    kept = rank < capacity[flat_expert]
    flat_gates = gates.reshape(-1)

    def one_expert(total, expert):
        chosen = kept & (flat_expert == expert)
        picked = jnp.nonzero(chosen, size=CAP, fill_value=entries)[0].astype(jnp.int32)
        present = picked < entries
        safe_entry = jnp.minimum(picked, entries - 1)
        token_rows = jnp.where(present, safe_entry // TOP, 0).astype(jnp.int32)
        outputs = expert_apply(quantized[token_rows], scales[token_rows], w_gate[expert], w_up[expert], w_down[expert])
        weights = jnp.where(present, flat_gates[safe_entry], jnp.zeros_like(flat_gates[safe_entry]))
        total = total.at[token_rows].add(outputs.astype(jnp.float32) * weights[:, None])
        return total, None

    total, unused = lax.scan(one_expert, jnp.zeros((TOKENS, D), jnp.float32), jnp.arange(EXPERTS, dtype=jnp.int32))
    return total.astype(jnp.bfloat16)
```

```python
import functools

import jax
import jax.numpy as jnp
from jax import lax
from jax.experimental import pallas as pl
from jax.experimental.pallas import tpu as pltpu
from jax.sharding import PartitionSpec as P

F32 = jnp.float32
BF16 = jnp.bfloat16
LANES = 128
CHUNKS = 2
BIG = 1e9


def iota(shape, dim):
    return lax.broadcasted_iota(jnp.int32, shape, dim)


def prepare_kernel(me_ref, tokens_ref, routes_ref, gates_ref, prio_ref, *out_refs):
    rows, width = tokens_ref.shape
    part = rows // CHUNKS
    for block in range(width // LANES):
        lanes = slice(block * LANES, (block + 1) * LANES)
        x = tokens_ref[:, lanes].astype(F32)
        largest = jnp.max(jnp.abs(x), axis=1, keepdims=True)
        scale = ((largest + 1e-06) / 448.0).astype(BF16).astype(F32)
        quantized = (x / scale).astype(BF16)
        restored = (quantized.astype(F32) * scale).astype(BF16)
        for c in range(CHUNKS):
            out_refs[c][:, lanes] = restored[c * part : (c + 1) * part]
    top = routes_ref.shape[1]
    gates = gates_ref[...]
    high = gates.astype(BF16)
    middle = (gates - high.astype(F32)).astype(BF16)
    low = (gates - high.astype(F32) - middle.astype(F32)).astype(BF16)
    eye = iota((rows, rows), 0) == iota((rows, rows), 1)
    prio = jnp.sum(jnp.where(eye, prio_ref[...].astype(F32), 0.0), axis=1, keepdims=True)
    fields = [routes_ref[...].astype(F32).astype(BF16), high, middle, low]
    facts = jnp.zeros((part, LANES), F32)
    lane = iota((part, LANES), 1)
    for c in range(CHUNKS):
        first = c * (LANES // CHUNKS)
        held = slice(c * part, (c + 1) * part)
        for k, field in enumerate(fields):
            place = iota((top, LANES), 1) == iota((top, LANES), 0) + (first + k * top)
            facts += jnp.dot(field[held], place.astype(F32).astype(BF16), preferred_element_type=F32)
        facts = jnp.where(lane == first + 4 * top, prio[held], facts)
        facts = jnp.where(lane == first + 4 * top + 1, me_ref[0].astype(F32), facts)
    out_refs[0][:, width:] = facts.astype(BF16)


def prepare(me, tokens, routes, gates, priority):
    rows, width = tokens.shape
    part = rows // CHUNKS
    return pl.pallas_call(
        prepare_kernel,
        in_specs=[pl.BlockSpec(memory_space=pltpu.SMEM)] + [pl.BlockSpec(memory_space=pltpu.VMEM)] * 4,
        out_specs=[pl.BlockSpec(memory_space=pltpu.VMEM)] * CHUNKS,
        out_shape=[
            jax.ShapeDtypeStruct((part, width + (LANES if c == 0 else 0)), BF16) for c in range(CHUNKS)
        ],
    )(me, tokens, routes, gates, priority.reshape(1, rows))


def weigh_kernel(top, tok_rows, me_ref, capacity_ref, *refs):
    fact_refs, out_refs, key_ref, row_ref = refs[:4], refs[4 : 4 + CHUNKS], refs[-2], refs[-1]
    part = tok_rows // CHUNKS
    each = fact_refs[0].shape[0]
    total = 4 * each * CHUNKS
    me = me_ref[0]
    eye = iota((LANES, LANES), 0) == iota((LANES, LANES), 1)
    lane = iota((LANES, LANES), 1)
    row = lax.rem(iota((LANES, LANES), 0), part)[:, :1]
    tiles = each // LANES
    for a in range(4):
        def tile_step(i, _, a=a):
            facts = fact_refs[a][pl.ds(pl.multiple_of(i * LANES, LANES), LANES), :].astype(F32)
            values = (
                pltpu.roll(facts, LANES - top, 1)
                + pltpu.roll(facts, LANES - 2 * top, 1)
                + pltpu.roll(facts, LANES - 3 * top, 1)
            )
            for c in range(CHUNKS):
                first = c * (LANES // CHUNKS)
                named = (lane >= first) & (lane < first + top) & (facts == me.astype(F32))
                has = jnp.sum(named.astype(F32), axis=1, keepdims=True)
                gate = jnp.sum(jnp.where(named, values, 0.0), axis=1, keepdims=True)
                prio = jnp.sum(jnp.where(lane == first + 4 * top, facts, 0.0), axis=1, keepdims=True)
                source = jnp.sum(jnp.where(lane == first + 4 * top + 1, facts, 0.0), axis=1, keepdims=True)
                key = prio * float(total) + source * float(tok_rows) + (row + c * part).astype(F32)
                key = jnp.where(has > 0.0, key, BIG)
                at = (c * 4 + a) * tiles + i
                key_ref[at] = jnp.broadcast_to(key, (LANES, LANES))
                row_ref[pl.ds(at, 1), :] = jnp.sum(jnp.where(eye, key, 0.0), axis=0, keepdims=True)
                out_refs[c][pl.ds(pl.multiple_of((a * tiles + i) * LANES, LANES), LANES), :] = (
                    jnp.broadcast_to(gate, (LANES, LANES))
                )
            return 0

        lax.fori_loop(0, tiles, tile_step, 0, unroll=tiles == 1)
    limit = capacity_ref[me].astype(F32)
    count = 4 * tiles * CHUNKS
    per = 4 * tiles

    for c in range(CHUNKS):
        def rank_step(i, _, c=c):
            key = key_ref[c * per + i]

            def add(j, smaller):
                return smaller + (row_ref[pl.ds(j, 1), :] < key).astype(F32)

            smaller = lax.fori_loop(0, count, add, jnp.zeros((LANES, LANES), F32), unroll=min(count, 8))
            rank = jnp.sum(smaller, axis=1, keepdims=True)
            keep = (rank < limit) & (key < BIG)
            at = pl.ds(pl.multiple_of(i * LANES, LANES), LANES)
            out_refs[c][at, :] = jnp.where(keep, out_refs[c][at, :], 0.0)
            return 0

        lax.fori_loop(0, per, rank_step, 0)


def weigh(me, capacity, rows, top, tok_rows):
    each, wide = rows[0].shape
    last = wide // LANES - 1
    count = 4 * each * CHUNKS // LANES
    return pl.pallas_call(
        functools.partial(weigh_kernel, top, tok_rows),
        grid=(1,),
        in_specs=[pl.BlockSpec(memory_space=pltpu.SMEM)] * 2
        + [pl.BlockSpec((each, LANES), lambda i: (0, last))] * 4,
        out_specs=[pl.BlockSpec((4 * each, LANES), lambda i: (0, 0))] * CHUNKS,
        out_shape=[jax.ShapeDtypeStruct((4 * each, LANES), F32)] * CHUNKS,
        scratch_shapes=[pltpu.VMEM((count, LANES, LANES), F32), pltpu.VMEM((count, LANES), F32)],
        compiler_params=pltpu.CompilerParams(vmem_limit_bytes=32 * 1024 * 1024),
    )(me, capacity, *rows)


def expert_kernel(steps, *refs):
    x_refs, weight_ref, gate_ref, up_ref, down_ref = refs[:4], refs[4], refs[5], refs[6], refs[7]
    own_ref, other_ref, x, hidden, sems = refs[8:]
    each, width = x_refs[0].shape[0], x.shape[1]
    tile = gate_ref.shape[1]
    step = pl.program_id(0)

    @pl.when(step == 0)
    def _():
        copies = [
            pltpu.make_async_copy(
                x_refs[a].at[:, pl.ds(0, width)], x.at[pl.ds(a * each, each), :], sems.at[a]
            )
            for a in range(4)
        ]
        for copy in copies:
            copy.start()
        for copy in copies:
            copy.wait()

    @pl.when(step < steps)
    def _():
        gated = jnp.dot(x[...], gate_ref[...], preferred_element_type=F32)
        upward = jnp.dot(x[...], up_ref[...], preferred_element_type=F32)
        result = (gated / (1.0 + jnp.exp(-gated)) * upward).astype(BF16)
        hidden[:, pl.ds(pl.multiple_of(step * tile, tile), tile)] = result

    @pl.when(step >= steps)
    def _():
        for half, ref in enumerate((own_ref, other_ref)):
            rows = slice(half * 2 * each, (half + 1) * 2 * each)
            out = jnp.dot(hidden[rows, :], down_ref[...], preferred_element_type=F32).astype(BF16)
            ref[...] = (out.astype(F32) * weight_ref[rows, :1]).astype(BF16)


def expert(rows, weight, w_gate, w_up, w_down):
    each = rows[0].shape[0]
    unused, width, ff = w_gate.shape
    tile, out_tile = 256, 512
    steps = ff // tile
    grid = steps + width // out_tile

    def out_at(i):
        return (0, jnp.maximum(i - steps, 0))

    return pl.pallas_call(
        functools.partial(expert_kernel, steps),
        grid=(grid,),
        in_specs=[pl.BlockSpec(memory_space=pl.ANY)] * 4
        + [
            pl.BlockSpec((4 * each, LANES), lambda i: (0, 0)),
            pl.BlockSpec((None, width, tile), lambda i: (0, 0, jnp.minimum(i, steps - 1))),
            pl.BlockSpec((None, width, tile), lambda i: (0, 0, jnp.minimum(i, steps - 1))),
            pl.BlockSpec((None, ff, out_tile), lambda i: (0, 0, jnp.maximum(i - steps, 0))),
        ],
        out_specs=[pl.BlockSpec((2 * each, out_tile), out_at)] * 2,
        out_shape=[jax.ShapeDtypeStruct((2 * each, width), BF16)] * 2,
        scratch_shapes=[
            pltpu.VMEM((4 * each, width), BF16),
            pltpu.VMEM((4 * each, ff), BF16),
            pltpu.SemaphoreType.DMA((4,)),
        ],
        compiler_params=pltpu.CompilerParams(vmem_limit_bytes=40 * 1024 * 1024),
        cost_estimate=pl.CostEstimate(
            flops=24 * each * width * ff, bytes_accessed=6 * width * ff, transcendentals=4 * each * ff
        ),
    )(*rows, weight, w_gate, w_up, w_down)


def orders(ep):
    bits = list(range(ep.bit_length() - 1))[::-1]
    return (bits, bits[:-2] + bits[:-3:-1])


def swap(array, ep, step):
    pairs = [
        (2 * place + core, 2 * (place ^ (1 << order[step])) + core)
        for place in range(ep)
        for core, order in enumerate(orders(ep))
    ]
    return lax.ppermute(array, ("ep", "sub"), pairs)


def cross(array):
    return lax.ppermute(array, "sub", [(0, 1), (1, 0)])


def on_device(ep, tokens, routes, gates, priority, capacity, w_gate, w_up, w_down):
    tok_rows, width = tokens.shape
    top = routes.shape[1]
    part = tok_rows // CHUNKS
    steps = ep.bit_length() - 1
    me = (lax.axis_index("ep") * 2 + lax.axis_index("sub")).astype(jnp.int32).reshape(1)
    chunks = prepare(me, tokens, routes, gates, priority)
    gathered = []
    for chunk in chunks:
        held = chunk
        for step in range(steps - 1):
            held = jnp.concatenate([held, swap(held, ep, step)])
        came = swap(held, ep, steps - 1)
        gathered.append([held, came, cross(held), cross(came)])
    weights = weigh(me, capacity, gathered[0], top, tok_rows)
    results = []
    for c in range(CHUNKS):
        own, other = expert(gathered[c], weights[c], w_gate, w_up, w_down)
        terms = [own, cross(other)]
        count = ep * part
        for step in range(steps)[::-1]:
            count //= 2
            send = sum([t[count : 2 * count].astype(F32) for t in terms]).astype(BF16)
            terms.append(swap(send, ep, step))
        results.append(sum([t[:part].astype(F32) for t in terms]).astype(BF16))
    return jnp.concatenate(results)


def solution(mesh):
    in_specs = (
        P(("groups", "ep", "sub"), None),
        P(("groups", "ep", "sub"), None),
        P(("groups", "ep", "sub"), None),
        P(("groups", "ep", "sub")),
        P(),
        P(("ep", "sub"), None, None),
        P(("ep", "sub"), None, None),
        P(("ep", "sub"), None, None),
    )
    out_specs = P(("groups", "ep", "sub"), None)
    return jax.shard_map(
        functools.partial(on_device, mesh.shape["ep"]),
        mesh=mesh,
        in_specs=in_specs,
        out_specs=out_specs,
        check_vma=False,
    )
```

```python
import functools

import jax
import jax.numpy as jnp
from jax import lax
from jax.experimental import pallas as pl
from jax.experimental.pallas import tpu as pltpu
from jax.sharding import PartitionSpec as P

F32 = jnp.float32
BF16 = jnp.bfloat16
LANES = 128
BIG = 1e9
MIB = 1024 * 1024


def iota(shape, dim):
    return lax.broadcasted_iota(jnp.int32, shape, dim)


def prepare_kernel(me_ref, tokens_ref, routes_ref, gates_ref, prio_ref, rows_ref, facts_ref):
    rows, width = tokens_ref.shape
    top = routes_ref.shape[0]
    for block in range(width // LANES):
        lanes = slice(block * LANES, (block + 1) * LANES)
        x = tokens_ref[:, lanes].astype(F32)
        largest = jnp.max(jnp.abs(x), axis=1, keepdims=True)
        scale = ((largest + 1e-06) / 448.0).astype(BF16).astype(F32)
        quantized = (x / scale).astype(BF16)
        rows_ref[:, lanes] = (quantized.astype(F32) * scale).astype(BF16)
    gates = gates_ref[...]
    high = gates.astype(BF16)
    middle = (gates - high.astype(F32)).astype(BF16)
    low = (gates - high.astype(F32) - middle.astype(F32)).astype(BF16)
    place = iota((top, rows), 0)
    other = jnp.where(place == 0, prio_ref[...].astype(F32), jnp.where(place == 1, me_ref[0].astype(F32), 0.0))
    fields = [routes_ref[...].astype(F32).astype(BF16), high, middle, low, other.astype(BF16)]
    half = rows // 2
    facts = jnp.zeros((half, LANES), F32)
    for c in range(2):
        for k, field in enumerate(fields):
            spot = iota((top, LANES), 1) == iota((top, LANES), 0) + (c * (LANES // 2) + k * top)
            laid = lax.dot_general(
                field,
                spot.astype(F32).astype(BF16),
                (((0,), (0,)), ((), ())),
                preferred_element_type=F32,
            )
            facts += laid[c * half : (c + 1) * half]
    facts_ref[...] = facts.astype(BF16)


def prepare(me, tokens, routes, gates, priority):
    rows, width = tokens.shape
    return pl.pallas_call(
        prepare_kernel,
        in_specs=[pl.BlockSpec(memory_space=pltpu.SMEM)] + [pl.BlockSpec(memory_space=pltpu.VMEM)] * 4,
        out_specs=[pl.BlockSpec(memory_space=pltpu.VMEM)] * 2,
        out_shape=[
            jax.ShapeDtypeStruct((rows, width), BF16),
            jax.ShapeDtypeStruct((rows // 2, LANES), BF16),
        ],
    )(me, tokens, routes.T, gates.T, priority.reshape(1, rows))


def weigh_kernel(top, tok_rows, me_ref, capacity_ref, *refs):
    fact_refs, out_refs, key_ref, row_ref, gate_out = refs[:4], refs[4:6], refs[6], refs[7], refs[8]
    half = tok_rows // 2
    each = fact_refs[0].shape[0]
    total = 8 * each
    me = me_ref[0]
    eye = iota((LANES, LANES), 0) == iota((LANES, LANES), 1)
    lane = iota((LANES, LANES), 1)
    row = lax.rem(iota((LANES, LANES), 0), half)[:, :1]
    tiles = each // LANES
    for a in range(4):

        def tile_step(i, _, a=a):
            facts = fact_refs[a][pl.ds(pl.multiple_of(i * LANES, LANES), LANES), :].astype(F32)
            values = (
                pltpu.roll(facts, LANES - top, 1)
                + pltpu.roll(facts, LANES - 2 * top, 1)
                + pltpu.roll(facts, LANES - 3 * top, 1)
            )
            for c in range(2):
                first = c * (LANES // 2)
                named = (lane >= first) & (lane < first + top) & (facts == me.astype(F32))
                has = jnp.sum(named.astype(F32), axis=1, keepdims=True)
                gate = jnp.sum(jnp.where(named, values, 0.0), axis=1, keepdims=True)
                prio = jnp.sum(jnp.where(lane == first + 4 * top, facts, 0.0), axis=1, keepdims=True)
                source = jnp.sum(jnp.where(lane == first + 4 * top + 1, facts, 0.0), axis=1, keepdims=True)
                key = prio * float(total) + source * float(tok_rows) + (row + c * half).astype(F32)
                key = jnp.where(has > 0.0, key, BIG)
                at = (a * tiles + i) * 2 + c
                key_ref[at] = jnp.broadcast_to(key, (LANES, LANES))
                gate_out[at] = jnp.broadcast_to(gate, (LANES, LANES))
                row_ref[pl.ds(at, 1), :] = jnp.sum(jnp.where(eye, key, 0.0), axis=0, keepdims=True)
            return 0

        lax.fori_loop(0, tiles, tile_step, 0, unroll=tiles == 1)
    limit = capacity_ref[me].astype(F32)
    count = 8 * tiles
    owners = LANES // half

    for side in range(2):

        def rank_step(i, _, side=side):
            for c in range(2):
                at = side * (count // 2) + 2 * i + c
                key = key_ref[at]

                def add(j, smaller):
                    return smaller + (row_ref[pl.ds(j, 1), :] < key).astype(F32)

                smaller = lax.fori_loop(0, count, add, jnp.zeros((LANES, LANES), F32), unroll=min(count, 8))
                rank = jnp.sum(smaller, axis=1, keepdims=True)
                weight = jnp.where((rank < limit) & (key < BIG), gate_out[at], 0.0)
                for owner in range(owners):
                    to = pl.multiple_of((i * owners + owner) * tok_rows + c * half, half)
                    out_refs[side][pl.ds(to, half), :] = weight[owner * half : (owner + 1) * half]
            return 0

        lax.fori_loop(0, count // 4, rank_step, 0)


def weigh(me, capacity, facts, top, tok_rows):
    each = facts[0].shape[0]
    count = 8 * each // LANES
    return pl.pallas_call(
        functools.partial(weigh_kernel, top, tok_rows),
        in_specs=[pl.BlockSpec(memory_space=pltpu.SMEM)] * 2 + [pl.BlockSpec(memory_space=pltpu.VMEM)] * 4,
        out_specs=[pl.BlockSpec(memory_space=pltpu.VMEM)] * 2,
        out_shape=[jax.ShapeDtypeStruct((4 * each, LANES), F32)] * 2,
        scratch_shapes=[
            pltpu.VMEM((count, LANES, LANES), F32),
            pltpu.VMEM((count, LANES), F32),
            pltpu.VMEM((count, LANES, LANES), F32),
        ],
        compiler_params=pltpu.CompilerParams(vmem_limit_bytes=24 * MIB),
        cost_estimate=pl.CostEstimate(flops=2000000, bytes_accessed=5000000, transcendentals=0),
    )(me, capacity, *facts)


FF_TILE, OUT_TILE = 256, 512


def expert_kernel(blocks, *refs):
    count = 2 * len(blocks)
    x_refs, weight_refs, gate_ref, up_ref, down_ref = refs[:count], refs[count : count + 2], *refs[count + 2 : count + 5]
    out_refs = refs[count + 5 : count + 7]
    x, gate_w, up_w, down_w, hidden, out, x_sem, w_sem, out_sem = refs[count + 7 :]
    base, width = x_refs[0].shape
    ff = hidden.shape[1]
    rows = count // 2 * base
    ff_tiles, out_tiles = ff // FF_TILE, width // OUT_TILE
    copies = []
    for a, ref in enumerate(x_refs):
        copies.append(pltpu.make_async_copy(ref, x.at[pl.ds(a * base, base), :], x_sem.at[a]))
    first = []
    for k in range(ff_tiles):
        lanes = pl.ds(k * FF_TILE, FF_TILE)
        first.append(pltpu.make_async_copy(gate_ref.at[0, :, lanes], gate_w.at[k], w_sem.at[2 * k]))
        first.append(pltpu.make_async_copy(up_ref.at[0, :, lanes], up_w.at[k], w_sem.at[2 * k + 1]))
    last = []
    for k in range(out_tiles):
        lanes = pl.ds(k * OUT_TILE, OUT_TILE)
        last.append(pltpu.make_async_copy(down_ref.at[0, :, lanes], down_w.at[k], w_sem.at[2 * ff_tiles + k]))
    for copy in copies + first + last:
        copy.start()
    for copy in copies:
        copy.wait()
    for k in range(ff_tiles):
        first[2 * k].wait()
        gated = jnp.dot(x[...], gate_w[k], preferred_element_type=F32)
        first[2 * k + 1].wait()
        upward = jnp.dot(x[...], up_w[k], preferred_element_type=F32)
        result = gated / (1.0 + jnp.exp(-gated)) * upward
        hidden[:, k * FF_TILE : (k + 1) * FF_TILE] = result.astype(BF16)
    sent = []
    for k in range(out_tiles):
        last[k].wait()
        lanes = slice(k * OUT_TILE, (k + 1) * OUT_TILE)
        made = jnp.dot(hidden[...], down_w[k], preferred_element_type=F32).astype(BF16).astype(F32)
        for a in range(count):
            side, block = divmod(a, count // 2)
            held = slice(a * base, (a + 1) * base)
            weight = weight_refs[side][blocks[block] * base : (blocks[block] + 1) * base, :1]
            out[held, lanes] = (made[held] * weight).astype(BF16)
        for side in range(2):
            copy = pltpu.make_async_copy(
                out.at[pl.ds(side * rows, rows), pl.ds(k * OUT_TILE, OUT_TILE)],
                out_refs[side].at[:, pl.ds(k * OUT_TILE, OUT_TILE)],
                out_sem.at[2 * k + side],
            )
            copy.start()
            sent.append(copy)
    for copy in sent:
        copy.wait()


def expert(blocks, own, other, weights, w_gate, w_up, w_down):
    count = 2 * len(blocks)
    base, width = own[blocks[0]].shape
    ff = w_gate.shape[2]
    rows = len(blocks) * base
    ff_tiles, out_tiles = ff // FF_TILE, width // OUT_TILE
    held = 2 * rows * (4 * width + 2 * ff) + 6 * width * ff + 4 * rows * 2 * (2 * FF_TILE + OUT_TILE)
    return pl.pallas_call(
        functools.partial(expert_kernel, blocks),
        in_specs=[pl.BlockSpec(memory_space=pl.ANY)] * count
        + [pl.BlockSpec(memory_space=pltpu.VMEM)] * 2
        + [pl.BlockSpec(memory_space=pltpu.HBM)] * 3,
        out_specs=[pl.BlockSpec(memory_space=pl.ANY)] * 2,
        out_shape=[jax.ShapeDtypeStruct((rows, width), BF16)] * 2,
        scratch_shapes=[
            pltpu.VMEM((2 * rows, width), BF16),
            pltpu.VMEM((ff_tiles, width, FF_TILE), BF16),
            pltpu.VMEM((ff_tiles, width, FF_TILE), BF16),
            pltpu.VMEM((out_tiles, ff, OUT_TILE), BF16),
            pltpu.VMEM((2 * rows, ff), BF16),
            pltpu.VMEM((2 * rows, width), BF16),
            pltpu.SemaphoreType.DMA((count,)),
            pltpu.SemaphoreType.DMA((2 * ff_tiles + out_tiles,)),
            pltpu.SemaphoreType.DMA((2 * out_tiles,)),
        ],
        compiler_params=pltpu.CompilerParams(vmem_limit_bytes=held + 6 * MIB),
        cost_estimate=pl.CostEstimate(
            flops=12 * rows * width * ff, bytes_accessed=6 * width * ff, transcendentals=2 * rows * ff
        ),
    )(*[own[b] for b in blocks], *[other[b] for b in blocks], *weights, w_gate, w_up, w_down)


def orders(ep):
    bits = list(range(ep.bit_length() - 1))[::-1]
    return (bits, bits[:-2] + bits[:-3:-1])


def send(array, ep, flips):
    pairs = []
    for place in range(ep):
        for core, order in enumerate(orders(ep)):
            to = place
            for flip in flips:
                to ^= 1 << order[flip]
            pairs.append((2 * place + core, 2 * to + core))
    return lax.ppermute(array, ("ep", "sub"), pairs)


def cross(array):
    return lax.ppermute(array, "sub", [(0, 1), (1, 0)])


def add(*terms):
    return sum([t.astype(F32) for t in terms]).astype(BF16)


def on_device(ep, tokens, routes, gates, priority, capacity, w_gate, w_up, w_down):
    tok_rows, width = tokens.shape
    top = routes.shape[1]
    steps = ep.bit_length() - 1
    me = (lax.axis_index("ep") * 2 + lax.axis_index("sub")).astype(jnp.int32).reshape(1)
    held, facts = prepare(me, tokens, routes, gates, priority)
    for step in range(steps - 1):
        facts = jnp.concatenate([facts, send(facts, ep, [step])])
    came = send(facts, ep, [steps - 1])
    weights = weigh(me, capacity, [facts, came, cross(facts), cross(came)], top, tok_rows)
    for step in range(steps - 3):
        held = jnp.concatenate([held, send(held, ep, [step])])
    base = held.shape[0]
    own = {0: held}
    own[1] = send(held, ep, [-3])
    own[2] = send(held, ep, [-2])
    own[4] = send(held, ep, [-1])
    own[3] = send(own[1], ep, [-2])
    own[5] = send(own[1], ep, [-1])
    own[7] = send(own[1], ep, [-2, -1])
    own[6] = send(own[2], ep, [-1])
    other = {b: cross(own[b]) for b in own}
    parts = {}
    for blocks in ((0, 1, 2, 4), (3, 5), (7, 6)):
        mine, theirs = expert(blocks, own, other, weights, w_gate, w_up, w_down)
        theirs = cross(theirs)
        for k, b in enumerate(blocks):
            parts[b] = (mine[k * base : (k + 1) * base], theirs[k * base : (k + 1) * base])
    back4 = send(add(*parts[4]), ep, [-1])
    back3 = send(add(*parts[3]), ep, [-2])
    back5 = send(add(*parts[5]), ep, [-1])
    back7 = send(add(*parts[7]), ep, [-2, -1])
    back6 = send(add(*parts[6]), ep, [-1])
    back1 = send(add(*parts[1], back3, back5, back7), ep, [-3])
    back2 = send(add(*parts[2], back6), ep, [-2])
    terms = [*parts[0], back1, back2, back4]
    count = base
    for step in range(steps - 3)[::-1]:
        count //= 2
        terms.append(send(add(*[t[count : 2 * count] for t in terms]), ep, [step]))
    return add(*[t[:tok_rows] for t in terms])


def solution(mesh):
    in_specs = (
        P(("groups", "ep", "sub"), None),
        P(("groups", "ep", "sub"), None),
        P(("groups", "ep", "sub"), None),
        P(("groups", "ep", "sub")),
        P(),
        P(("ep", "sub"), None, None),
        P(("ep", "sub"), None, None),
        P(("ep", "sub"), None, None),
    )
    out_specs = P(("groups", "ep", "sub"), None)
    return jax.shard_map(
        functools.partial(on_device, mesh.shape["ep"]),
        mesh=mesh,
        in_specs=in_specs,
        out_specs=out_specs,
        check_vma=False,
    )
```

```python
import functools

import jax
import jax.numpy as jnp
from jax import lax
from jax.experimental import pallas as pl
from jax.experimental.pallas import tpu as pltpu
from jax.sharding import PartitionSpec as P

F32 = jnp.float32
BF16 = jnp.bfloat16
LANES = 128
BIG = 1e9
MIB = 1024 * 1024


def iota(shape, dim):
    return lax.broadcasted_iota(jnp.int32, shape, dim)


def prepare_kernel(me_ref, tokens_ref, routes_ref, gates_ref, prio_ref, rows_ref):
    rows, width = tokens_ref.shape
    top = routes_ref.shape[0]
    for block in range(width // LANES):
        lanes = slice(block * LANES, (block + 1) * LANES)
        x = tokens_ref[:, lanes].astype(F32)
        largest = jnp.max(jnp.abs(x), axis=1, keepdims=True)
        scale = ((largest + 1e-06) / 448.0).astype(BF16).astype(F32)
        quantized = (x / scale).astype(BF16)
        rows_ref[:, lanes] = (quantized.astype(F32) * scale).astype(BF16)
    gates = gates_ref[...]
    high = gates.astype(BF16)
    middle = (gates - high.astype(F32)).astype(BF16)
    low = (gates - high.astype(F32) - middle.astype(F32)).astype(BF16)
    place, token = iota((top, rows), 0), iota((top, rows), 1)
    other = jnp.where(place == 0, prio_ref[...], jnp.where(place == 1, me_ref[0], token))
    fields = [routes_ref[...].astype(F32), high.astype(F32), middle.astype(F32), low.astype(F32), other.astype(F32)]
    facts = jnp.zeros((rows, LANES), F32)
    for k, field in enumerate(fields):
        spot = iota((top, LANES), 1) == iota((top, LANES), 0) + k * top
        facts += lax.dot_general(
            field.astype(BF16),
            spot.astype(F32).astype(BF16),
            (((0,), (0,)), ((), ())),
            preferred_element_type=F32,
        )
    rows_ref[:, width:] = facts.astype(BF16)


def prepare(me, tokens, routes, gates, priority):
    rows, width = tokens.shape
    return pl.pallas_call(
        prepare_kernel,
        in_specs=[pl.BlockSpec(memory_space=pltpu.SMEM)] + [pl.BlockSpec(memory_space=pltpu.VMEM)] * 4,
        out_specs=pl.BlockSpec(memory_space=pltpu.VMEM),
        out_shape=jax.ShapeDtypeStruct((rows, width + LANES), BF16),
    )(me, tokens, routes.T, gates.T, priority.reshape(1, rows))


def weigh_kernel(top, tok_rows, me_ref, capacity_ref, *refs):
    fact_refs, out_ref, (all_ref, key_ref, row_ref) = refs[:5], refs[5], refs[6:]
    total = out_ref.shape[0]
    at = 0
    for ref in fact_refs:
        rows, wide = ref.shape
        all_ref[at : at + rows, :] = ref[:, wide - LANES :]
        at += rows
    me = me_ref[0].astype(F32)
    limit = capacity_ref[me_ref[0]].astype(F32)
    eye = iota((LANES, LANES), 0) == iota((LANES, LANES), 1)
    lane = iota((LANES, LANES), 1)
    tiles = total // LANES
    worth = jnp.where(lane == 4 * top, float(total), 0.0)
    worth = jnp.where(lane == 4 * top + 1, float(tok_rows), jnp.where(lane == 4 * top + 2, 1.0, worth))

    def read(i, _):
        held = pl.ds(pl.multiple_of(i * LANES, LANES), LANES)
        facts = all_ref[held, :].astype(F32)
        values = (
            pltpu.roll(facts, LANES - top, 1)
            + pltpu.roll(facts, LANES - 2 * top, 1)
            + pltpu.roll(facts, LANES - 3 * top, 1)
        )
        named = (lane < top) & (facts == me)
        gate = jnp.sum(jnp.where(named, values, 0.0), axis=1, keepdims=True)
        key = jnp.sum(facts * worth, axis=1, keepdims=True)
        key = jnp.where(gate > 0.0, key, BIG)
        key_ref[i] = jnp.broadcast_to(key, (LANES, LANES))
        out_ref[held, :] = jnp.broadcast_to(gate, (LANES, LANES))
        row_ref[pl.ds(i, 1), :] = jnp.sum(jnp.where(eye, key, 0.0), axis=0, keepdims=True)
        return 0

    lax.fori_loop(0, tiles, read, 0, unroll=2)

    def judge(i, _):
        held = pl.ds(pl.multiple_of(i * LANES, LANES), LANES)
        key = key_ref[i]

        def count(j, smaller):
            return smaller + (row_ref[pl.ds(j, 1), :] < key).astype(F32)

        smaller = lax.fori_loop(0, tiles, count, jnp.zeros((LANES, LANES), F32), unroll=min(tiles, 8))
        rank = jnp.sum(smaller, axis=1, keepdims=True)
        out_ref[held, :] = jnp.where(rank < limit, out_ref[held, :], 0.0)
        return 0

    lax.fori_loop(0, tiles, judge, 0)


def weigh(me, capacity, facts, top, tok_rows):
    total = sum(f.shape[0] for f in facts)
    return pl.pallas_call(
        functools.partial(weigh_kernel, top, tok_rows),
        in_specs=[pl.BlockSpec(memory_space=pltpu.SMEM)] * 2 + [pl.BlockSpec(memory_space=pltpu.VMEM)] * 5,
        out_specs=pl.BlockSpec(memory_space=pltpu.VMEM),
        out_shape=jax.ShapeDtypeStruct((total, LANES), F32),
        scratch_shapes=[
            pltpu.VMEM((total, LANES), BF16),
            pltpu.VMEM((total // LANES, LANES, LANES), F32),
            pltpu.VMEM((total // LANES, LANES), F32),
        ],
        compiler_params=pltpu.CompilerParams(vmem_limit_bytes=24 * MIB),
        cost_estimate=pl.CostEstimate(flops=1, bytes_accessed=1, transcendentals=0),
    )(me, capacity, *facts)


def pack_kernel(*refs):
    ins, packed, facts, first, second = refs[:4], *refs[4:]
    rows, width = first.shape
    for k, ref in enumerate(ins):
        facts[k * rows : (k + 1) * rows, :] = ref[:, width:]
        if k > 0:
            packed[(k - 1) * rows : k * rows, :] = ref[...]
    first[...] = ins[1][:, :width]
    second[...] = ins[2][:, :width]


def pack(blocks):
    rows, wide = blocks[0].shape
    return pl.pallas_call(
        pack_kernel,
        in_specs=[pl.BlockSpec(memory_space=pltpu.VMEM)] * 4,
        out_specs=[pl.BlockSpec(memory_space=pltpu.VMEM)] * 4,
        out_shape=[
            jax.ShapeDtypeStruct((3 * rows, wide), BF16),
            jax.ShapeDtypeStruct((4 * rows, LANES), BF16),
            jax.ShapeDtypeStruct((rows, wide - LANES), BF16),
            jax.ShapeDtypeStruct((rows, wide - LANES), BF16),
        ],
        compiler_params=pltpu.CompilerParams(vmem_limit_bytes=24 * MIB),
        cost_estimate=pl.CostEstimate(flops=1, bytes_accessed=1, transcendentals=0),
    )(*blocks)


def load_kernel(*refs):
    count = len(refs) // 2
    sems = refs[-1]
    copies = [pltpu.make_async_copy(refs[k], refs[count + k], sems.at[k]) for k in range(count)]
    for copy in copies:
        copy.start()
    for copy in copies:
        copy.wait()


def load(*arrays):
    size = sum(a.size * 2 for a in arrays)
    return pl.pallas_call(
        load_kernel,
        in_specs=[pl.BlockSpec(memory_space=pl.ANY)] * len(arrays),
        out_specs=[pl.BlockSpec(memory_space=pltpu.VMEM)] * len(arrays),
        out_shape=[jax.ShapeDtypeStruct(a.shape, a.dtype) for a in arrays],
        scratch_shapes=[pltpu.SemaphoreType.DMA((len(arrays),))],
        compiler_params=pltpu.CompilerParams(vmem_limit_bytes=size + 4 * MIB),
    )(*arrays)


FF_TILE, OUT_TILE = 256, 512


def expert_kernel(places, base, split, *refs):
    count = len(refs) - 8
    x_refs, (weight_ref, gate_ref, up_ref, down_ref) = refs[:count], refs[count : count + 4]
    out_refs, (x, hidden) = refs[count + 4 : count + 6], refs[count + 6 :]
    width, ff = x.shape[1], hidden.shape[1]
    at = 0
    for ref in x_refs:
        x[at : at + ref.shape[0], :] = ref[:, :width]
        at += ref.shape[0]
    for k in range(ff // FF_TILE):
        lanes = slice(k * FF_TILE, (k + 1) * FF_TILE)
        gated = jnp.dot(x[...], gate_ref[0, :, lanes], preferred_element_type=F32)
        upward = jnp.dot(x[...], up_ref[0, :, lanes], preferred_element_type=F32)
        hidden[:, lanes] = (gated / (1.0 + jnp.exp(-gated)) * upward).astype(BF16)
    for k in range(width // OUT_TILE):
        lanes = slice(k * OUT_TILE, (k + 1) * OUT_TILE)
        made = jnp.dot(hidden[...], down_ref[0, :, lanes], preferred_element_type=F32).astype(BF16).astype(F32)
        for side in range(2):
            for k, place in enumerate(places[side]):
                first = side * split + k * base
                weight = weight_ref[place * base : (place + 1) * base, :1]
                out_refs[side][k * base : (k + 1) * base, lanes] = (made[first : first + base] * weight).astype(BF16)


def expert(own, other, places, weights, matrices):
    ff, width = matrices[2].shape[1:]
    rows = sum(a.shape[0] for a in own)
    held = 2 * rows * 2 * (width + ff) + 4 * 2 * rows * (2 * FF_TILE + OUT_TILE)
    return pl.pallas_call(
        functools.partial(expert_kernel, places, rows // len(places[0]), rows),
        in_specs=[pl.BlockSpec(memory_space=pltpu.VMEM)] * (len(own) + len(other) + 4),
        out_specs=[pl.BlockSpec(memory_space=pltpu.VMEM)] * 2,
        out_shape=[jax.ShapeDtypeStruct((rows, width), BF16)] * 2,
        scratch_shapes=[pltpu.VMEM((2 * rows, width), BF16), pltpu.VMEM((2 * rows, ff), BF16)],
        compiler_params=pltpu.CompilerParams(vmem_limit_bytes=held + 20 * MIB),
        cost_estimate=pl.CostEstimate(flops=1, bytes_accessed=1, transcendentals=0),
    )(*own, *other, weights, *matrices)


def orders(ep):
    bits = list(range(ep.bit_length() - 1))[::-1]
    return (bits, bits[:-2] + bits[:-3:-1])


def send(array, ep, flips):
    pairs = []
    for place in range(ep):
        for core, order in enumerate(orders(ep)):
            to = place
            for flip in flips:
                to ^= 1 << order[flip]
            pairs.append((2 * place + core, 2 * to + core))
    return lax.ppermute(array, ("ep", "sub"), pairs)


def cross(array):
    return lax.ppermute(array, "sub", [(0, 1), (1, 0)])


def add(*terms):
    return sum([t.astype(F32) for t in terms]).astype(BF16)


def on_device(ep, tokens, routes, gates, priority, capacity, w_gate, w_up, w_down):
    tok_rows, width = tokens.shape
    top = routes.shape[1]
    steps = ep.bit_length() - 1
    me = (lax.axis_index("ep") * 2 + lax.axis_index("sub")).astype(jnp.int32).reshape(1)
    held = prepare(me, tokens, routes, gates, priority)
    for step in range(steps - 3):
        held = jnp.concatenate([held, send(held, ep, [step])])
    base = held.shape[0]
    own1, own2, own4 = send(held, ep, [-3]), send(held, ep, [-2]), send(held, ep, [-1])
    first = cross(held)
    matrices = load(w_gate, w_up, w_down)
    own1, own2, own4, first, matrices = lax.optimization_barrier((own1, own2, own4, first, matrices))
    packed, facts, rows1, rows2 = pack([held, own1, own2, own4])
    own3 = send(rows1, ep, [-2])
    own5 = send(rows1, ep, [-1])
    own7 = send(rows1, ep, [-2, -1])
    own6 = send(rows2, ep, [-1])
    crossed = cross(packed)
    far_facts = send(facts, ep, [-3, -2, -1])
    weights = weigh(me, capacity, [facts, first, crossed, far_facts, cross(far_facts)], top, tok_rows)
    parts = {}

    def work(blocks, mine, others, places):
        places = (places, tuple(p + 4 for p in places))
        made, theirs = expert(mine, others, places, weights, matrices)
        back = cross(theirs)
        for k, b in enumerate(blocks):
            parts[b] = (made[k * base : (k + 1) * base], back[k * base : (k + 1) * base])
        return made

    made = work((0, 1, 2, 4), [held, own1, own2, own4], [first, crossed], (0, 1, 2, 3))
    own3, own5, own7, own6, unused = lax.optimization_barrier((own3, own5, own7, own6, made))
    work((3, 5), [own3, own5], [cross(own3), cross(own5)], (11, 10))
    work((7, 6), [own7, own6], [cross(own7), cross(own6)], (8, 9))
    back4 = send(add(*parts[4]), ep, [-1])
    back3 = send(add(*parts[3]), ep, [-2])
    back5 = send(add(*parts[5]), ep, [-1])
    back7 = send(add(*parts[7]), ep, [-2, -1])
    back6 = send(add(*parts[6]), ep, [-1])
    back1 = send(add(*parts[1], back3, back5, back7), ep, [-3])
    back2 = send(add(*parts[2], back6), ep, [-2])
    terms = [*parts[0], back1, back2, back4]
    count = base
    for step in range(steps - 3)[::-1]:
        count //= 2
        terms.append(send(add(*[t[count : 2 * count] for t in terms]), ep, [step]))
    return add(*[t[:tok_rows] for t in terms])


def solution(mesh):
    in_specs = (
        P(("groups", "ep", "sub"), None),
        P(("groups", "ep", "sub"), None),
        P(("groups", "ep", "sub"), None),
        P(("groups", "ep", "sub")),
        P(),
        P(("ep", "sub"), None, None),
        P(("ep", "sub"), None, None),
        P(("ep", "sub"), None, None),
    )
    out_specs = P(("groups", "ep", "sub"), None)
    return jax.shard_map(
        functools.partial(on_device, mesh.shape["ep"]),
        mesh=mesh,
        in_specs=in_specs,
        out_specs=out_specs,
        check_vma=False,
    )
```

```python
import functools

import jax
import jax.numpy as jnp
from jax import lax
from jax.experimental import pallas as pl
from jax.experimental.pallas import tpu as pltpu
from jax.sharding import PartitionSpec as P

F32 = jnp.float32
BF16 = jnp.bfloat16
LANES = 128
BIG = 1e9
MIB = 1024 * 1024


def iota(shape, dim):
    return lax.broadcasted_iota(jnp.int32, shape, dim)


def prepare_kernel(me_ref, tokens_ref, routes_ref, gates_ref, prio_ref, rows_ref):
    rows, width = tokens_ref.shape
    top = routes_ref.shape[0]
    for block in range(width // LANES):
        lanes = slice(block * LANES, (block + 1) * LANES)
        x = tokens_ref[:, lanes].astype(F32)
        largest = jnp.max(jnp.abs(x), axis=1, keepdims=True)
        scale = ((largest + 1e-06) / 448.0).astype(BF16).astype(F32)
        quantized = (x / scale).astype(BF16)
        rows_ref[:, lanes] = (quantized.astype(F32) * scale).astype(BF16)
    gates = gates_ref[...]
    high = gates.astype(BF16)
    middle = (gates - high.astype(F32)).astype(BF16)
    low = (gates - high.astype(F32) - middle.astype(F32)).astype(BF16)
    place, token = iota((top, rows), 0), iota((top, rows), 1)
    other = jnp.where(place == 0, prio_ref[...], jnp.where(place == 1, me_ref[0], token))
    fields = [routes_ref[...].astype(F32), high.astype(F32), middle.astype(F32), low.astype(F32), other.astype(F32)]
    facts = jnp.zeros((rows, LANES), F32)
    for k, field in enumerate(fields):
        spot = iota((top, LANES), 1) == iota((top, LANES), 0) + k * top
        facts += lax.dot_general(
            field.astype(BF16),
            spot.astype(F32).astype(BF16),
            (((0,), (0,)), ((), ())),
            preferred_element_type=F32,
        )
    rows_ref[:, width:] = facts.astype(BF16)


def prepare(me, tokens, routes, gates, priority):
    rows, width = tokens.shape
    return pl.pallas_call(
        prepare_kernel,
        in_specs=[pl.BlockSpec(memory_space=pltpu.SMEM)] + [pl.BlockSpec(memory_space=pltpu.VMEM)] * 4,
        out_specs=pl.BlockSpec(memory_space=pltpu.VMEM),
        out_shape=jax.ShapeDtypeStruct((rows, width + LANES), BF16),
    )(me, tokens, routes.T, gates.T, priority.reshape(1, rows))


def weigh_kernel(top, tok_rows, me_ref, capacity_ref, *refs):
    fact_refs, out_ref, (all_ref, key_ref, row_ref) = refs[:5], refs[5], refs[6:]
    total = out_ref.shape[0]
    at = 0
    for ref in fact_refs:
        rows, wide = ref.shape
        all_ref[at : at + rows, :] = ref[:, wide - LANES :]
        at += rows
    me = me_ref[0].astype(F32)
    limit = capacity_ref[me_ref[0]].astype(F32)
    eye = iota((LANES, LANES), 0) == iota((LANES, LANES), 1)
    lane = iota((LANES, LANES), 1)
    tiles = total // LANES
    worth = jnp.where(lane == 4 * top, float(total), 0.0)
    worth = jnp.where(lane == 4 * top + 1, float(tok_rows), jnp.where(lane == 4 * top + 2, 1.0, worth))

    def read(i, _):
        held = pl.ds(pl.multiple_of(i * LANES, LANES), LANES)
        facts = all_ref[held, :].astype(F32)
        values = (
            pltpu.roll(facts, LANES - top, 1)
            + pltpu.roll(facts, LANES - 2 * top, 1)
            + pltpu.roll(facts, LANES - 3 * top, 1)
        )
        named = (lane < top) & (facts == me)
        gate = jnp.sum(jnp.where(named, values, 0.0), axis=1, keepdims=True)
        key = jnp.sum(facts * worth, axis=1, keepdims=True)
        key = jnp.where(gate > 0.0, key, BIG)
        key_ref[i] = jnp.broadcast_to(key, (LANES, LANES))
        out_ref[held, :] = jnp.broadcast_to(gate, (LANES, LANES))
        row_ref[pl.ds(i, 1), :] = jnp.sum(jnp.where(eye, key, 0.0), axis=0, keepdims=True)
        return 0

    lax.fori_loop(0, tiles, read, 0, unroll=min(tiles, 8))

    def judge(i, _):
        held = pl.ds(pl.multiple_of(i * LANES, LANES), LANES)
        key = key_ref[i]

        def count(j, smaller):
            return smaller + (row_ref[pl.ds(j, 1), :] < key).astype(F32)

        smaller = lax.fori_loop(0, tiles, count, jnp.zeros((LANES, LANES), F32), unroll=min(tiles, 8))
        rank = jnp.sum(smaller, axis=1, keepdims=True)
        out_ref[held, :] = jnp.where(rank < limit, out_ref[held, :], 0.0)
        return 0

    lax.fori_loop(0, tiles, judge, 0, unroll=min(tiles, 8))


def weigh(me, capacity, facts, top, tok_rows):
    total = sum(f.shape[0] for f in facts)
    return pl.pallas_call(
        functools.partial(weigh_kernel, top, tok_rows),
        in_specs=[pl.BlockSpec(memory_space=pltpu.SMEM)] * 2 + [pl.BlockSpec(memory_space=pltpu.VMEM)] * 5,
        out_specs=pl.BlockSpec(memory_space=pltpu.VMEM),
        out_shape=jax.ShapeDtypeStruct((total, LANES), F32),
        scratch_shapes=[
            pltpu.VMEM((total, LANES), BF16),
            pltpu.VMEM((total // LANES, LANES, LANES), F32),
            pltpu.VMEM((total // LANES, LANES), F32),
        ],
        compiler_params=pltpu.CompilerParams(vmem_limit_bytes=24 * MIB),
        cost_estimate=pl.CostEstimate(flops=1, bytes_accessed=1, transcendentals=0),
    )(me, capacity, *facts)


def pack_kernel(*refs):
    ins, packed, facts, first, second = refs[:4], *refs[4:]
    rows, width = first.shape
    for k, ref in enumerate(ins):
        facts[k * rows : (k + 1) * rows, :] = ref[:, width:]
        if k > 0:
            packed[(k - 1) * rows : k * rows, :] = ref[...]
    first[...] = ins[1][:, :width]
    second[...] = ins[2][:, :width]


def pack(blocks):
    rows, wide = blocks[0].shape
    return pl.pallas_call(
        pack_kernel,
        in_specs=[pl.BlockSpec(memory_space=pltpu.VMEM)] * 4,
        out_specs=[pl.BlockSpec(memory_space=pltpu.VMEM)] * 4,
        out_shape=[
            jax.ShapeDtypeStruct((3 * rows, wide), BF16),
            jax.ShapeDtypeStruct((4 * rows, LANES), BF16),
            jax.ShapeDtypeStruct((rows, wide - LANES), BF16),
            jax.ShapeDtypeStruct((rows, wide - LANES), BF16),
        ],
        compiler_params=pltpu.CompilerParams(vmem_limit_bytes=24 * MIB),
        cost_estimate=pl.CostEstimate(flops=1, bytes_accessed=1, transcendentals=0),
    )(*blocks)


def load_kernel(*refs):
    count = len(refs) // 2
    sems = refs[-1]
    copies = [pltpu.make_async_copy(refs[k], refs[count + k], sems.at[k]) for k in range(count)]
    for copy in copies:
        copy.start()
    for copy in copies:
        copy.wait()


def load(*arrays):
    size = sum(a.size * 2 for a in arrays)
    return pl.pallas_call(
        load_kernel,
        in_specs=[pl.BlockSpec(memory_space=pl.ANY)] * len(arrays),
        out_specs=[pl.BlockSpec(memory_space=pltpu.VMEM)] * len(arrays),
        out_shape=[jax.ShapeDtypeStruct(a.shape, a.dtype) for a in arrays],
        scratch_shapes=[pltpu.SemaphoreType.DMA((len(arrays),))],
        compiler_params=pltpu.CompilerParams(vmem_limit_bytes=size + 4 * MIB),
    )(*arrays)


FF_TILE, OUT_TILE = 256, 512


def expert_kernel(places, base, splits, *refs):
    count = len(refs) - 6 - len(splits)
    x_refs, (weight_ref, gate_ref, up_ref, down_ref) = refs[:count], refs[count : count + 4]
    out_refs, (x, hidden) = refs[count + 4 : -2], refs[-2:]
    width, ff = x.shape[1], hidden.shape[1]
    at = 0
    for ref in x_refs:
        x[at : at + ref.shape[0], :] = ref[:, :width]
        at += ref.shape[0]
    for k in range(ff // FF_TILE):
        lanes = slice(k * FF_TILE, (k + 1) * FF_TILE)
        gated = jnp.dot(x[...], gate_ref[0, :, lanes], preferred_element_type=F32)
        upward = jnp.dot(x[...], up_ref[0, :, lanes], preferred_element_type=F32)
        hidden[:, lanes] = (gated / (1.0 + jnp.exp(-gated)) * upward).astype(BF16)
    for k in range(width // OUT_TILE):
        lanes = slice(k * OUT_TILE, (k + 1) * OUT_TILE)
        made = jnp.dot(hidden[...], down_ref[0, :, lanes], preferred_element_type=F32).astype(BF16).astype(F32)
        block = 0
        for out_ref, blocks in zip(out_refs, splits):
            for to in range(blocks):
                place = places[block]
                weight = weight_ref[place * base : (place + 1) * base, :1]
                out_ref[to * base : (to + 1) * base, lanes] = (
                    made[block * base : (block + 1) * base] * weight
                ).astype(BF16)
                block += 1


def expert(arrays, places, splits, weights, matrices):
    ff, width = matrices[2].shape[1:]
    rows = sum(a.shape[0] for a in arrays)
    base = rows // len(places)
    held = rows * 2 * (width + ff) + 4 * rows * (2 * FF_TILE + OUT_TILE)
    return pl.pallas_call(
        functools.partial(expert_kernel, places, base, splits),
        in_specs=[pl.BlockSpec(memory_space=pltpu.VMEM)] * (len(arrays) + 4),
        out_specs=[pl.BlockSpec(memory_space=pltpu.VMEM)] * len(splits),
        out_shape=[jax.ShapeDtypeStruct((blocks * base, width), BF16) for blocks in splits],
        scratch_shapes=[pltpu.VMEM((rows, width), BF16), pltpu.VMEM((rows, ff), BF16)],
        compiler_params=pltpu.CompilerParams(vmem_limit_bytes=held + 20 * MIB),
        cost_estimate=pl.CostEstimate(flops=1, bytes_accessed=1, transcendentals=0),
    )(*arrays, weights, *matrices)


def orders(ep):
    bits = list(range(ep.bit_length() - 1))[::-1]
    return (bits, bits[:-2] + bits[:-3:-1])


def send(array, ep, flips):
    pairs = []
    for place in range(ep):
        for core, order in enumerate(orders(ep)):
            to = place
            for flip in flips:
                to ^= 1 << order[flip]
            pairs.append((2 * place + core, 2 * to + core))
    return lax.ppermute(array, ("ep", "sub"), pairs)


def cross(array):
    return lax.ppermute(array, "sub", [(0, 1), (1, 0)])


def add(*terms):
    return sum([t.astype(F32) for t in terms]).astype(BF16)


def on_device(ep, tokens, routes, gates, priority, capacity, w_gate, w_up, w_down):
    tok_rows, width = tokens.shape
    top = routes.shape[1]
    steps = ep.bit_length() - 1
    me = (lax.axis_index("ep") * 2 + lax.axis_index("sub")).astype(jnp.int32).reshape(1)
    held = prepare(me, tokens, routes, gates, priority)
    for step in range(steps - 3):
        held = jnp.concatenate([held, send(held, ep, [step])])
    base = held.shape[0]
    own1, own2, own4 = send(held, ep, [-3]), send(held, ep, [-2]), send(held, ep, [-1])
    first = cross(held)
    matrices = load(w_gate, w_up, w_down)
    own1, own2, own4, first, matrices = lax.optimization_barrier((own1, own2, own4, first, matrices))
    packed, facts, rows1, rows2 = pack([held, own1, own2, own4])
    own3 = send(rows1, ep, [-2])
    own5 = send(rows1, ep, [-1])
    far_facts = send(facts, ep, [-3, -2, -1])
    crossed = cross(packed)
    rows1, rows2, far_facts = lax.optimization_barrier((rows1, rows2, far_facts))
    own7 = send(rows1, ep, [-2, -1])
    own6 = send(rows2, ep, [-1])
    far_crossed = cross(far_facts)
    own3, own5, far_crossed = lax.optimization_barrier((own3, own5, far_crossed))
    weights = weigh(me, capacity, [facts, first, crossed, far_facts, far_crossed], top, tok_rows)
    parts = {}

    def pair(blocks, arrays, places):
        made, theirs = expert(
            arrays + [cross(a) for a in arrays], places + [p + 4 for p in places], (2, 2), weights, matrices
        )
        back = cross(theirs)
        for k, b in enumerate(blocks):
            parts[b] = (made[k * base : (k + 1) * base], back[k * base : (k + 1) * base])
        return made

    made = pair((3, 5), [own3, own5], [11, 10])
    first, made = lax.optimization_barrier((first, made))
    (theirs,) = expert([first, crossed], [4, 5, 6, 7], (4,), weights, matrices)
    own7, own6, theirs = lax.optimization_barrier((own7, own6, theirs))
    back3 = send(add(*parts[3]), ep, [-2])
    back5 = send(add(*parts[5]), ep, [-1])
    pair((7, 6), [own7, own6], [8, 9])
    back7 = send(add(*parts[7]), ep, [-2, -1])
    back6 = send(add(*parts[6]), ep, [-1])
    (made,) = expert([held, own1, own2, own4], [0, 1, 2, 3], (4,), weights, matrices)
    back = cross(theirs)
    for k, b in enumerate((0, 1, 2, 4)):
        parts[b] = (made[k * base : (k + 1) * base], back[k * base : (k + 1) * base])
    back1 = send(add(*parts[1], back3, back5, back7), ep, [-3])
    back2 = send(add(*parts[2], back6), ep, [-2])
    back4 = send(add(*parts[4]), ep, [-1])
    terms = [*parts[0], back1, back2, back4]
    count = base
    for step in range(steps - 3)[::-1]:
        count //= 2
        terms.append(send(add(*[t[count : 2 * count] for t in terms]), ep, [step]))
    return add(*[t[:tok_rows] for t in terms])


def solution(mesh):
    in_specs = (
        P(("groups", "ep", "sub"), None),
        P(("groups", "ep", "sub"), None),
        P(("groups", "ep", "sub"), None),
        P(("groups", "ep", "sub")),
        P(),
        P(("ep", "sub"), None, None),
        P(("ep", "sub"), None, None),
        P(("ep", "sub"), None, None),
    )
    out_specs = P(("groups", "ep", "sub"), None)
    return jax.shard_map(
        functools.partial(on_device, mesh.shape["ep"]),
        mesh=mesh,
        in_specs=in_specs,
        out_specs=out_specs,
        check_vma=False,
    )
```

```python
import functools

import jax
import jax.numpy as jnp
from jax import lax
from jax.experimental import pallas as pl
from jax.experimental.pallas import tpu as pltpu
from jax.sharding import PartitionSpec as P

F32 = jnp.float32
BF16 = jnp.bfloat16
LANES = 128
BIG = 1e9
MIB = 1024 * 1024


def iota(shape, dim):
    return lax.broadcasted_iota(jnp.int32, shape, dim)


def prepare_kernel(me_ref, tokens_ref, routes_ref, gates_ref, prio_ref, rows_ref):
    rows, width = tokens_ref.shape
    top = routes_ref.shape[0]
    for block in range(width // LANES):
        lanes = slice(block * LANES, (block + 1) * LANES)
        x = tokens_ref[:, lanes].astype(F32)
        largest = jnp.max(jnp.abs(x), axis=1, keepdims=True)
        scale = ((largest + 1e-06) / 448.0).astype(BF16).astype(F32)
        quantized = (x / scale).astype(BF16)
        rows_ref[:, lanes] = (quantized.astype(F32) * scale).astype(BF16)
    gates = gates_ref[...]
    high = gates.astype(BF16)
    middle = (gates - high.astype(F32)).astype(BF16)
    low = (gates - high.astype(F32) - middle.astype(F32)).astype(BF16)
    place, token = iota((top, rows), 0), iota((top, rows), 1)
    other = jnp.where(place == 0, prio_ref[...], jnp.where(place == 1, me_ref[0], token))
    fields = [routes_ref[...].astype(F32), high.astype(F32), middle.astype(F32), low.astype(F32), other.astype(F32)]
    facts = jnp.zeros((rows, LANES), F32)
    for k, field in enumerate(fields):
        spot = iota((top, LANES), 1) == iota((top, LANES), 0) + k * top
        facts += lax.dot_general(
            field.astype(BF16),
            spot.astype(F32).astype(BF16),
            (((0,), (0,)), ((), ())),
            preferred_element_type=F32,
        )
    rows_ref[:, width:] = facts.astype(BF16)


def prepare(me, tokens, routes, gates, priority):
    rows, width = tokens.shape
    return pl.pallas_call(
        prepare_kernel,
        in_specs=[pl.BlockSpec(memory_space=pltpu.SMEM)] + [pl.BlockSpec(memory_space=pltpu.VMEM)] * 4,
        out_specs=pl.BlockSpec(memory_space=pltpu.VMEM),
        out_shape=jax.ShapeDtypeStruct((rows, width + LANES), BF16),
    )(me, tokens, routes.T, gates.T, priority.reshape(1, rows))


def weigh_kernel(top, tok_rows, me_ref, capacity_ref, *refs):
    fact_refs, out_ref, (all_ref, key_ref, row_ref) = refs[:-4], refs[-4], refs[-3:]
    total = all_ref.shape[0]
    at = 0
    for ref in fact_refs:
        rows, wide = ref.shape
        all_ref[at : at + rows, :] = ref[:, wide - LANES :]
        at += rows
    eye = iota((LANES, LANES), 0) == iota((LANES, LANES), 1)
    lane = iota((LANES, LANES), 1)
    tiles = total // LANES
    mine = tiles // 2
    experts = (me_ref[0], me_ref[0] + 1 - 2 * lax.rem(me_ref[0], 2))
    worth = jnp.where(lane == 4 * top, float(total), 0.0)
    worth = jnp.where(lane == 4 * top + 1, float(tok_rows), jnp.where(lane == 4 * top + 2, 1.0, worth))

    def read(i, _, own):
        facts = all_ref[pl.ds(pl.multiple_of(i * LANES, LANES), LANES), :].astype(F32)
        values = (
            pltpu.roll(facts, LANES - top, 1)
            + pltpu.roll(facts, LANES - 2 * top, 1)
            + pltpu.roll(facts, LANES - 3 * top, 1)
        )
        order = jnp.sum(facts * worth, axis=1, keepdims=True)
        for e, expert in enumerate(experts):
            named = (lane < top) & (facts == expert.astype(F32))
            gate = jnp.sum(jnp.where(named, values, 0.0), axis=1, keepdims=True)
            key = jnp.where(gate > 0.0, order, BIG)
            row_ref[e, pl.ds(i, 1), :] = jnp.sum(jnp.where(eye, key, 0.0), axis=0, keepdims=True)
            if own:
                key_ref[e, i] = jnp.broadcast_to(key, (LANES, LANES))
                held = pl.ds(pl.multiple_of((e * mine + i) * LANES, LANES), LANES)
                out_ref[held, :] = jnp.broadcast_to(gate, (LANES, LANES))
        return 0

    lax.fori_loop(0, mine, functools.partial(read, own=True), 0, unroll=min(mine, 4))
    lax.fori_loop(mine, tiles, functools.partial(read, own=False), 0, unroll=min(mine, 4))
    for e, expert in enumerate(experts):
        limit = capacity_ref[expert].astype(F32)

        def judge(i, _, e=e, limit=limit):
            held = pl.ds(pl.multiple_of((e * mine + i) * LANES, LANES), LANES)
            key = key_ref[e, i]

            def count(j, smaller):
                return smaller + (row_ref[e, pl.ds(j, 1), :] < key).astype(F32)

            smaller = lax.fori_loop(0, tiles, count, jnp.zeros((LANES, LANES), F32), unroll=min(tiles, 8))
            rank = jnp.sum(smaller, axis=1, keepdims=True)
            out_ref[held, :] = jnp.where(rank < limit, out_ref[held, :], 0.0)
            return 0

        lax.fori_loop(0, mine, judge, 0, unroll=min(mine, 4))


def weigh(me, capacity, facts, top, tok_rows):
    total = sum(f.shape[0] for f in facts)
    tiles = total // LANES
    return pl.pallas_call(
        functools.partial(weigh_kernel, top, tok_rows),
        in_specs=[pl.BlockSpec(memory_space=pltpu.SMEM)] * 2
        + [pl.BlockSpec(memory_space=pltpu.VMEM)] * len(facts),
        out_specs=pl.BlockSpec(memory_space=pltpu.VMEM),
        out_shape=jax.ShapeDtypeStruct((total, LANES), F32),
        scratch_shapes=[
            pltpu.VMEM((total, LANES), BF16),
            pltpu.VMEM((2, tiles // 2, LANES, LANES), F32),
            pltpu.VMEM((2, tiles, LANES), F32),
        ],
        compiler_params=pltpu.CompilerParams(vmem_limit_bytes=24 * MIB),
        cost_estimate=pl.CostEstimate(flops=1, bytes_accessed=1, transcendentals=0),
    )(me, capacity, *facts)


def pack_kernel(*refs):
    rows = refs[0].shape[0]
    for k, ref in enumerate(refs[:-1]):
        refs[-1][k * rows : (k + 1) * rows, :] = ref[...]


def pack(blocks):
    rows, wide = blocks[0].shape
    return pl.pallas_call(
        pack_kernel,
        in_specs=[pl.BlockSpec(memory_space=pltpu.VMEM)] * len(blocks),
        out_specs=pl.BlockSpec(memory_space=pltpu.VMEM),
        out_shape=jax.ShapeDtypeStruct((len(blocks) * rows, wide), BF16),
        compiler_params=pltpu.CompilerParams(vmem_limit_bytes=24 * MIB),
        cost_estimate=pl.CostEstimate(flops=1, bytes_accessed=1, transcendentals=0),
    )(*blocks)


def combine_kernel(rows, sums, weighted, *refs):
    ins, outs = refs[: -len(sums)], refs[-len(sums) :]
    width = outs[0].shape[1]
    for lanes in range(0, width, 256):
        for terms, out in zip(sums, outs):
            total = None
            for which, first, place in terms:
                value = ins[which][first : first + rows, lanes : lanes + 256].astype(F32)
                if place is not None:
                    value = value * ins[weighted][place : place + rows, :1]
                total = value if total is None else total + value
            out[:, lanes : lanes + 256] = total.astype(BF16)


def combine(arrays, weights, sums):
    rows = weights.shape[0] // 16
    width = arrays[0].shape[1]
    sums = [[(a, b * rows, None if p is None else p * rows) for a, b, p in terms] for terms in sums]
    return pl.pallas_call(
        functools.partial(combine_kernel, rows, sums, len(arrays)),
        in_specs=[pl.BlockSpec(memory_space=pltpu.VMEM)] * (len(arrays) + 1),
        out_specs=[pl.BlockSpec(memory_space=pltpu.VMEM)] * len(sums),
        out_shape=[jax.ShapeDtypeStruct((rows, width), BF16)] * len(sums),
        compiler_params=pltpu.CompilerParams(vmem_limit_bytes=24 * MIB),
        cost_estimate=pl.CostEstimate(flops=1, bytes_accessed=1, transcendentals=0),
    )(*arrays, weights)


def load_kernel(*refs):
    count = len(refs) // 2
    sems = refs[-1]
    copies = [pltpu.make_async_copy(refs[k], refs[count + k], sems.at[k]) for k in range(count)]
    for copy in copies:
        copy.start()
    for copy in copies:
        copy.wait()


def load(*arrays):
    size = sum(a.size * 2 for a in arrays)
    return pl.pallas_call(
        load_kernel,
        in_specs=[pl.BlockSpec(memory_space=pl.ANY)] * len(arrays),
        out_specs=[pl.BlockSpec(memory_space=pltpu.VMEM)] * len(arrays),
        out_shape=[jax.ShapeDtypeStruct(a.shape, a.dtype) for a in arrays],
        scratch_shapes=[pltpu.SemaphoreType.DMA((len(arrays),))],
        compiler_params=pltpu.CompilerParams(vmem_limit_bytes=size + 4 * MIB),
    )(*arrays)


FF_TILE, OUT_TILE = 256, 512


def expert_kernel(*refs):
    x_refs, (gate_ref, up_ref, down_ref, out_ref, x, hidden) = refs[:-6], refs[-6:]
    width, ff = x.shape[1], hidden.shape[1]
    at = 0
    for ref in x_refs:
        x[at : at + ref.shape[0], :] = ref[:, :width]
        at += ref.shape[0]
    for k in range(ff // FF_TILE):
        lanes = slice(k * FF_TILE, (k + 1) * FF_TILE)
        gated = jnp.dot(x[...], gate_ref[0, :, lanes], preferred_element_type=F32)
        upward = jnp.dot(x[...], up_ref[0, :, lanes], preferred_element_type=F32)
        hidden[:, lanes] = (gated / (1.0 + jnp.exp(-gated)) * upward).astype(BF16)
    for k in range(width // OUT_TILE):
        lanes = slice(k * OUT_TILE, (k + 1) * OUT_TILE)
        out_ref[:, lanes] = jnp.dot(hidden[...], down_ref[0, :, lanes], preferred_element_type=F32).astype(BF16)


def expert(arrays, matrices):
    ff, width = matrices[2].shape[1:]
    rows = sum(a.shape[0] for a in arrays)
    held = rows * 2 * (width + ff) + 4 * rows * (2 * FF_TILE + OUT_TILE)
    return pl.pallas_call(
        expert_kernel,
        in_specs=[pl.BlockSpec(memory_space=pltpu.VMEM)] * (len(arrays) + 3),
        out_specs=pl.BlockSpec(memory_space=pltpu.VMEM),
        out_shape=jax.ShapeDtypeStruct((rows, width), BF16),
        scratch_shapes=[pltpu.VMEM((rows, width), BF16), pltpu.VMEM((rows, ff), BF16)],
        compiler_params=pltpu.CompilerParams(vmem_limit_bytes=held + 20 * MIB),
        cost_estimate=pl.CostEstimate(flops=1, bytes_accessed=1, transcendentals=0),
    )(*arrays, *matrices)


def orders(ep):
    bits = list(range(ep.bit_length() - 1))[::-1]
    return (bits, bits[:-2] + bits[:-3:-1])


def send(array, ep, flips):
    pairs = []
    for place in range(ep):
        for core, order in enumerate(orders(ep)):
            to = place
            for flip in flips:
                to ^= 1 << order[flip]
            pairs.append((2 * place + core, 2 * to + core))
    return lax.ppermute(array, ("ep", "sub"), pairs)


def cross(array):
    return lax.ppermute(array, "sub", [(0, 1), (1, 0)])


def add(*terms):
    return sum([t.astype(F32) for t in terms]).astype(BF16)


def on_device(ep, tokens, routes, gates, priority, capacity, w_gate, w_up, w_down):
    tok_rows, width = tokens.shape
    top = routes.shape[1]
    steps = ep.bit_length() - 1
    me = (lax.axis_index("ep") * 2 + lax.axis_index("sub")).astype(jnp.int32).reshape(1)
    held = prepare(me, tokens, routes, gates, priority)
    for step in range(steps - 3):
        held = jnp.concatenate([held, send(held, ep, [step])])
    base = held.shape[0]
    own1, own2, own4 = send(held, ep, [-3]), send(held, ep, [-2]), send(held, ep, [-1])
    first = cross(held)
    matrices = load(w_gate, w_up, w_down)
    own1, own2, own4, first, matrices = lax.optimization_barrier((own1, own2, own4, first, matrices))
    crossed = cross(pack([own1, own2, own4]))
    own3 = send(own1, ep, [-2])
    own5 = send(own1, ep, [-1])
    own6 = send(own2, ep, [-1])
    own7 = send(own3, ep, [-1])
    theirs = expert([first, crossed], matrices)
    own3, own5, own6, own7, theirs = lax.optimization_barrier((own3, own5, own6, own7, theirs))
    far = [own3, own5, own6, own7]
    far_crossed = cross(pack(far))
    far_made = expert(far, matrices)
    far_crossed, far_made = lax.optimization_barrier((far_crossed, far_made))
    far_back = cross(expert([far_crossed], matrices))
    near = [held, own1, own2, own4]
    weights = weigh(me, capacity, near + far + [first, crossed, far_crossed], top, tok_rows)

    def part(mine, back, block, place):
        return [(mine, block, place), (back, block, 8 + place)]

    send5, send6, send7 = combine(
        [far_made, far_back], weights, [part(0, 1, 1, 5), part(0, 1, 2, 6), part(0, 1, 3, 7)]
    )
    back7 = send(send7, ep, [-1])
    back5 = send(send5, ep, [-1])
    back6 = send(send6, ep, [-1])
    (send3,) = combine([far_made, far_back, back7], weights, [part(0, 1, 0, 4) + [(2, 0, None)]])
    back3 = send(send3, ep, [-2])
    near_made = expert(near, matrices)
    near_back = cross(theirs)
    send1, send2, send4 = combine(
        [near_made, near_back, back3, back5, back6],
        weights,
        [
            part(0, 1, 1, 1) + [(2, 0, None), (3, 0, None)],
            part(0, 1, 2, 2) + [(4, 0, None)],
            part(0, 1, 3, 3),
        ],
    )
    back1 = send(send1, ep, [-3])
    back2 = send(send2, ep, [-2])
    back4 = send(send4, ep, [-1])
    (total,) = combine(
        [near_made, near_back, back1, back2, back4],
        weights,
        [part(0, 1, 0, 0) + [(2, 0, None), (3, 0, None), (4, 0, None)]],
    )
    for step in range(steps - 3)[::-1]:
        half = total.shape[0] // 2
        total = add(total[:half], send(total[half:], ep, [step]))
    return total


def solution(mesh):
    in_specs = (
        P(("groups", "ep", "sub"), None),
        P(("groups", "ep", "sub"), None),
        P(("groups", "ep", "sub"), None),
        P(("groups", "ep", "sub")),
        P(),
        P(("ep", "sub"), None, None),
        P(("ep", "sub"), None, None),
        P(("ep", "sub"), None, None),
    )
    out_specs = P(("groups", "ep", "sub"), None)
    return jax.shard_map(
        functools.partial(on_device, mesh.shape["ep"]),
        mesh=mesh,
        in_specs=in_specs,
        out_specs=out_specs,
        check_vma=False,
    )
```

```python
import functools

import jax
import jax.numpy as jnp
from jax import lax
from jax.experimental import pallas as pl
from jax.experimental.pallas import tpu as pltpu
from jax.sharding import PartitionSpec as P

F32 = jnp.float32
BF16 = jnp.bfloat16
LANES = 128
BIG = 1e9
MIB = 1024 * 1024


def iota(shape, dim):
    return lax.broadcasted_iota(jnp.int32, shape, dim)


def prepare_kernel(me_ref, tokens_ref, routes_ref, gates_ref, prio_ref, rows_ref):
    rows, width = tokens_ref.shape
    top = routes_ref.shape[0]
    for block in range(width // LANES):
        lanes = slice(block * LANES, (block + 1) * LANES)
        x = tokens_ref[:, lanes].astype(F32)
        largest = jnp.max(jnp.abs(x), axis=1, keepdims=True)
        scale = ((largest + 1e-06) / 448.0).astype(BF16).astype(F32)
        quantized = (x / scale).astype(BF16)
        rows_ref[:, lanes] = (quantized.astype(F32) * scale).astype(BF16)
    gates = gates_ref[...]
    high = gates.astype(BF16)
    middle = (gates - high.astype(F32)).astype(BF16)
    low = (gates - high.astype(F32) - middle.astype(F32)).astype(BF16)
    place, token = iota((top, rows), 0), iota((top, rows), 1)
    other = jnp.where(place == 0, prio_ref[...], jnp.where(place == 1, me_ref[0], token))
    fields = [routes_ref[...].astype(F32), high.astype(F32), middle.astype(F32), low.astype(F32), other.astype(F32)]
    facts = jnp.zeros((rows, LANES), F32)
    for k, field in enumerate(fields):
        spot = iota((top, LANES), 1) == iota((top, LANES), 0) + k * top
        facts += lax.dot_general(
            field.astype(BF16),
            spot.astype(F32).astype(BF16),
            (((0,), (0,)), ((), ())),
            preferred_element_type=F32,
        )
    rows_ref[:, width:] = facts.astype(BF16)


def prepare(me, tokens, routes, gates, priority):
    rows, width = tokens.shape
    return pl.pallas_call(
        prepare_kernel,
        in_specs=[pl.BlockSpec(memory_space=pltpu.SMEM)] + [pl.BlockSpec(memory_space=pltpu.VMEM)] * 4,
        out_specs=pl.BlockSpec(memory_space=pltpu.VMEM),
        out_shape=jax.ShapeDtypeStruct((rows, width + LANES), BF16),
    )(me, tokens, routes.T, gates.T, priority.reshape(1, rows))


def weigh_kernel(top, tok_rows, me_ref, capacity_ref, *refs):
    fact_refs, out_ref, (all_ref, key_ref, row_ref) = refs[:-4], refs[-4], refs[-3:]
    total = all_ref.shape[0]
    at = 0
    for ref in fact_refs:
        rows, wide = ref.shape
        all_ref[at : at + rows, :] = ref[:, wide - LANES :]
        at += rows
    eye = iota((LANES, LANES), 0) == iota((LANES, LANES), 1)
    lane = iota((LANES, LANES), 1)
    tiles = total // LANES
    mine = tiles // 2
    experts = (me_ref[0], me_ref[0] + 1 - 2 * lax.rem(me_ref[0], 2))
    worth = jnp.where(lane == 4 * top, float(total), 0.0)
    worth = jnp.where(lane == 4 * top + 1, float(tok_rows), jnp.where(lane == 4 * top + 2, 1.0, worth))

    def read(i, _, own):
        facts = all_ref[pl.ds(pl.multiple_of(i * LANES, LANES), LANES), :].astype(F32)
        values = (
            pltpu.roll(facts, LANES - top, 1)
            + pltpu.roll(facts, LANES - 2 * top, 1)
            + pltpu.roll(facts, LANES - 3 * top, 1)
        )
        order = jnp.sum(facts * worth, axis=1, keepdims=True)
        for e, expert in enumerate(experts):
            named = (lane < top) & (facts == expert.astype(F32))
            gate = jnp.sum(jnp.where(named, values, 0.0), axis=1, keepdims=True)
            key = jnp.where(gate > 0.0, order, BIG)
            row_ref[e, pl.ds(i, 1), :] = jnp.sum(jnp.where(eye, key, 0.0), axis=0, keepdims=True)
            if own:
                key_ref[e, i] = jnp.broadcast_to(key, (LANES, LANES))
                held = pl.ds(pl.multiple_of((e * mine + i) * LANES, LANES), LANES)
                out_ref[held, :] = jnp.broadcast_to(gate, (LANES, LANES))
        return 0

    lax.fori_loop(0, mine, functools.partial(read, own=True), 0, unroll=min(mine, 4))
    lax.fori_loop(mine, tiles, functools.partial(read, own=False), 0, unroll=min(mine, 4))
    for e, expert in enumerate(experts):
        limit = capacity_ref[expert].astype(F32)

        def judge(i, _, e=e, limit=limit):
            held = pl.ds(pl.multiple_of((e * mine + i) * LANES, LANES), LANES)
            key = key_ref[e, i]

            def count(j, smaller):
                return smaller + (row_ref[e, pl.ds(j, 1), :] < key).astype(F32)

            smaller = lax.fori_loop(0, tiles, count, jnp.zeros((LANES, LANES), F32), unroll=min(tiles, 8))
            rank = jnp.sum(smaller, axis=1, keepdims=True)
            out_ref[held, :] = jnp.where(rank < limit, out_ref[held, :], 0.0)
            return 0

        lax.fori_loop(0, mine, judge, 0, unroll=min(mine, 4))


def weigh(me, capacity, facts, top, tok_rows):
    total = sum(f.shape[0] for f in facts)
    tiles = total // LANES
    return pl.pallas_call(
        functools.partial(weigh_kernel, top, tok_rows),
        in_specs=[pl.BlockSpec(memory_space=pltpu.SMEM)] * 2
        + [pl.BlockSpec(memory_space=pltpu.VMEM)] * len(facts),
        out_specs=pl.BlockSpec(memory_space=pltpu.VMEM),
        out_shape=jax.ShapeDtypeStruct((total, LANES), F32),
        scratch_shapes=[
            pltpu.VMEM((total, LANES), BF16),
            pltpu.VMEM((2, tiles // 2, LANES, LANES), F32),
            pltpu.VMEM((2, tiles, LANES), F32),
        ],
        compiler_params=pltpu.CompilerParams(vmem_limit_bytes=24 * MIB),
        cost_estimate=pl.CostEstimate(flops=1, bytes_accessed=1, transcendentals=0),
    )(me, capacity, *facts)


def pack_kernel(*refs):
    rows = refs[0].shape[0]
    for k, ref in enumerate(refs[:-1]):
        refs[-1][k * rows : (k + 1) * rows, :] = ref[...]


def pack(blocks):
    rows, wide = blocks[0].shape
    return pl.pallas_call(
        pack_kernel,
        in_specs=[pl.BlockSpec(memory_space=pltpu.VMEM)] * len(blocks),
        out_specs=pl.BlockSpec(memory_space=pltpu.VMEM),
        out_shape=jax.ShapeDtypeStruct((len(blocks) * rows, wide), BF16),
        compiler_params=pltpu.CompilerParams(vmem_limit_bytes=24 * MIB),
        cost_estimate=pl.CostEstimate(flops=1, bytes_accessed=1, transcendentals=0),
    )(*blocks)


def combine_kernel(rows, sums, weighted, *refs):
    ins, outs = refs[: -len(sums)], refs[-len(sums) :]
    width = outs[0].shape[1]
    for lanes in range(0, width, 256):
        for terms, out in zip(sums, outs):
            total = None
            for which, first, place in terms:
                value = ins[which][first : first + rows, lanes : lanes + 256].astype(F32)
                if place is not None:
                    value = value * ins[weighted][place : place + rows, :1]
                total = value if total is None else total + value
            out[:, lanes : lanes + 256] = total.astype(out.dtype)


def combine(arrays, weights, sums, kind=BF16):
    rows = weights.shape[0] // 16
    width = arrays[0].shape[1]
    sums = [[(a, b * rows, None if p is None else p * rows) for a, b, p in terms] for terms in sums]
    return pl.pallas_call(
        functools.partial(combine_kernel, rows, sums, len(arrays)),
        in_specs=[pl.BlockSpec(memory_space=pltpu.VMEM)] * (len(arrays) + 1),
        out_specs=[pl.BlockSpec(memory_space=pltpu.VMEM)] * len(sums),
        out_shape=[jax.ShapeDtypeStruct((rows, width), kind)] * len(sums),
        compiler_params=pltpu.CompilerParams(vmem_limit_bytes=24 * MIB),
        cost_estimate=pl.CostEstimate(flops=1, bytes_accessed=1, transcendentals=0),
    )(*arrays, weights)


def load_kernel(*refs):
    count = len(refs) // 2
    sems = refs[-1]
    copies = [pltpu.make_async_copy(refs[k], refs[count + k], sems.at[k]) for k in range(count)]
    for copy in copies:
        copy.start()
    for copy in copies:
        copy.wait()


def load(*arrays):
    size = sum(a.size * 2 for a in arrays)
    return pl.pallas_call(
        load_kernel,
        in_specs=[pl.BlockSpec(memory_space=pl.ANY)] * len(arrays),
        out_specs=[pl.BlockSpec(memory_space=pltpu.VMEM)] * len(arrays),
        out_shape=[jax.ShapeDtypeStruct(a.shape, a.dtype) for a in arrays],
        scratch_shapes=[pltpu.SemaphoreType.DMA((len(arrays),))],
        compiler_params=pltpu.CompilerParams(vmem_limit_bytes=size + 4 * MIB),
    )(*arrays)


FF_TILE, OUT_TILE = 256, 512


def expert_kernel(*refs):
    x_refs, (gate_ref, up_ref, down_ref, out_ref, x, hidden) = refs[:-6], refs[-6:]
    width, ff = x.shape[1], hidden.shape[1]
    at = 0
    for ref in x_refs:
        x[at : at + ref.shape[0], :] = ref[:, :width]
        at += ref.shape[0]
    for k in range(ff // FF_TILE):
        lanes = slice(k * FF_TILE, (k + 1) * FF_TILE)
        gated = jnp.dot(x[...], gate_ref[0, :, lanes], preferred_element_type=F32)
        upward = jnp.dot(x[...], up_ref[0, :, lanes], preferred_element_type=F32)
        hidden[:, lanes] = (gated / (1.0 + jnp.exp(-gated)) * upward).astype(BF16)
    for k in range(width // OUT_TILE):
        lanes = slice(k * OUT_TILE, (k + 1) * OUT_TILE)
        out_ref[:, lanes] = jnp.dot(hidden[...], down_ref[0, :, lanes], preferred_element_type=F32).astype(BF16)


def expert(arrays, matrices):
    ff, width = matrices[2].shape[1:]
    rows = sum(a.shape[0] for a in arrays)
    held = rows * 2 * (width + ff) + 4 * rows * (2 * FF_TILE + OUT_TILE)
    return pl.pallas_call(
        expert_kernel,
        in_specs=[pl.BlockSpec(memory_space=pltpu.VMEM)] * (len(arrays) + 3),
        out_specs=pl.BlockSpec(memory_space=pltpu.VMEM),
        out_shape=jax.ShapeDtypeStruct((rows, width), BF16),
        scratch_shapes=[pltpu.VMEM((rows, width), BF16), pltpu.VMEM((rows, ff), BF16)],
        compiler_params=pltpu.CompilerParams(vmem_limit_bytes=held + 20 * MIB),
        cost_estimate=pl.CostEstimate(flops=1, bytes_accessed=1, transcendentals=0),
    )(*arrays, *matrices)


def orders(ep):
    bits = list(range(ep.bit_length() - 1))[::-1]
    return (bits, bits[:-2] + bits[:-3:-1])


def send(array, ep, flips):
    pairs = []
    for place in range(ep):
        for core, order in enumerate(orders(ep)):
            to = place
            for flip in flips:
                to ^= 1 << order[flip]
            pairs.append((2 * place + core, 2 * to + core))
    return lax.ppermute(array, ("ep", "sub"), pairs)


def cross(array):
    return lax.ppermute(array, "sub", [(0, 1), (1, 0)])


def add(*terms):
    return sum([t.astype(F32) for t in terms]).astype(BF16)


def on_device(ep, tokens, routes, gates, priority, capacity, w_gate, w_up, w_down):
    tok_rows, width = tokens.shape
    top = routes.shape[1]
    steps = ep.bit_length() - 1
    me = (lax.axis_index("ep") * 2 + lax.axis_index("sub")).astype(jnp.int32).reshape(1)
    held = prepare(me, tokens, routes, gates, priority)
    for step in range(steps - 3):
        held = jnp.concatenate([held, send(held, ep, [step])])
    base = held.shape[0]
    own1, own2, own4 = send(held, ep, [-3]), send(held, ep, [-2]), send(held, ep, [-1])
    first = cross(held)
    matrices = load(w_gate, w_up, w_down)
    own1, first, matrices = lax.optimization_barrier((own1, first, matrices))
    crossed = cross(pack([own1, own2, own4]))
    own3 = send(own1, ep, [-2])
    own5 = send(own1, ep, [-1])
    own6 = send(own2, ep, [-1])
    own7 = send(own3, ep, [-1])
    theirs = expert([first, crossed], matrices)
    own3, own5, own6, own7, theirs = lax.optimization_barrier((own3, own5, own6, own7, theirs))
    far = [own3, own5, own6, own7]
    far_crossed = cross(pack(far))
    far_made = expert(far, matrices)
    far_crossed, far_made = lax.optimization_barrier((far_crossed, far_made))
    far_back = cross(expert([far_crossed], matrices))
    near = [held, own1, own2, own4]
    weights = weigh(me, capacity, near + far + [first, crossed, far_crossed], top, tok_rows)

    def part(mine, back, block, place):
        return [(mine, block, place), (back, block, 8 + place)]

    send7, send5 = combine([far_made, far_back], weights, [part(0, 1, 3, 7), part(0, 1, 1, 5)])
    back7 = send(send7, ep, [-1])
    back5 = send(send5, ep, [-1])
    send3, send6 = combine(
        [far_made, far_back, back7], weights, [part(0, 1, 0, 4) + [(2, 0, None)], part(0, 1, 2, 6)]
    )
    back3 = send(send3, ep, [-2])
    back6 = send(send6, ep, [-1])
    near_made = expert(near, matrices)
    near_back = cross(theirs)
    near_made, back3, back5 = lax.optimization_barrier((near_made, back3, back5))
    (send1,) = combine([near_made, near_back, back3, back5], weights, [part(0, 1, 1, 1) + [(2, 0, None), (3, 0, None)]])
    back1 = send(send1, ep, [-3])
    back6, send1 = lax.optimization_barrier((back6, send1))
    send2, send4 = combine(
        [near_made, near_back, back6], weights, [part(0, 1, 2, 2) + [(2, 0, None)], part(0, 1, 3, 3)]
    )
    back2 = send(send2, ep, [-2])
    back4 = send(send4, ep, [-1])
    (total,) = combine([near_made, near_back, back1], weights, [part(0, 1, 0, 0) + [(2, 0, None)]], F32)
    back2, back4, total = lax.optimization_barrier((back2, back4, total))
    (total,) = combine([total, back2, back4], weights, [[(0, 0, None), (1, 0, None), (2, 0, None)]])
    for step in range(steps - 3)[::-1]:
        half = total.shape[0] // 2
        total = add(total[:half], send(total[half:], ep, [step]))
    return total


def solution(mesh):
    in_specs = (
        P(("groups", "ep", "sub"), None),
        P(("groups", "ep", "sub"), None),
        P(("groups", "ep", "sub"), None),
        P(("groups", "ep", "sub")),
        P(),
        P(("ep", "sub"), None, None),
        P(("ep", "sub"), None, None),
        P(("ep", "sub"), None, None),
    )
    out_specs = P(("groups", "ep", "sub"), None)
    return jax.shard_map(
        functools.partial(on_device, mesh.shape["ep"]),
        mesh=mesh,
        in_specs=in_specs,
        out_specs=out_specs,
        check_vma=False,
    )
```

```python
import functools

import jax
import jax.numpy as jnp
from jax import lax
from jax.experimental import pallas as pl
from jax.experimental.pallas import tpu as pltpu
from jax.sharding import PartitionSpec as P

F32 = jnp.float32
BF16 = jnp.bfloat16
LANES = 128
BIG = 1e9
MIB = 1024 * 1024


def iota(shape, dim):
    return lax.broadcasted_iota(jnp.int32, shape, dim)


def prepare_kernel(me_ref, tokens_ref, routes_ref, gates_ref, prio_ref, rows_ref):
    rows, width = tokens_ref.shape
    top = routes_ref.shape[0]
    for block in range(width // LANES):
        lanes = slice(block * LANES, (block + 1) * LANES)
        x = tokens_ref[:, lanes].astype(F32)
        largest = jnp.max(jnp.abs(x), axis=1, keepdims=True)
        scale = ((largest + 1e-06) / 448.0).astype(BF16).astype(F32)
        quantized = (x / scale).astype(BF16)
        rows_ref[:, lanes] = (quantized.astype(F32) * scale).astype(BF16)
    gates = gates_ref[...]
    high = gates.astype(BF16)
    middle = (gates - high.astype(F32)).astype(BF16)
    low = (gates - high.astype(F32) - middle.astype(F32)).astype(BF16)
    place, token = iota((top, rows), 0), iota((top, rows), 1)
    other = jnp.where(place == 0, prio_ref[...], jnp.where(place == 1, me_ref[0], token))
    fields = [routes_ref[...].astype(F32), high.astype(F32), middle.astype(F32), low.astype(F32), other.astype(F32)]
    facts = jnp.zeros((rows, LANES), F32)
    for k, field in enumerate(fields):
        spot = iota((top, LANES), 1) == iota((top, LANES), 0) + k * top
        facts += lax.dot_general(
            field.astype(BF16),
            spot.astype(F32).astype(BF16),
            (((0,), (0,)), ((), ())),
            preferred_element_type=F32,
        )
    rows_ref[:, width:] = facts.astype(BF16)


def prepare(me, tokens, routes, gates, priority):
    rows, width = tokens.shape
    return pl.pallas_call(
        prepare_kernel,
        in_specs=[pl.BlockSpec(memory_space=pltpu.SMEM)] + [pl.BlockSpec(memory_space=pltpu.VMEM)] * 4,
        out_specs=pl.BlockSpec(memory_space=pltpu.VMEM),
        out_shape=jax.ShapeDtypeStruct((rows, width + LANES), BF16),
    )(me, tokens, routes.T, gates.T, priority.reshape(1, rows))


def weigh_kernel(top, tok_rows, me_ref, capacity_ref, *refs):
    fact_refs, out_ref, (all_ref, key_ref, row_ref) = refs[:-4], refs[-4], refs[-3:]
    total = all_ref.shape[0]
    at = 0
    for ref in fact_refs:
        rows, wide = ref.shape
        all_ref[at : at + rows, :] = ref[:, wide - LANES :]
        at += rows
    eye = iota((LANES, LANES), 0) == iota((LANES, LANES), 1)
    lane = iota((LANES, LANES), 1)
    tiles = total // LANES
    mine = tiles // 2
    experts = (me_ref[0], me_ref[0] + 1 - 2 * lax.rem(me_ref[0], 2))
    worth = jnp.where(lane == 4 * top, float(total), 0.0)
    worth = jnp.where(lane == 4 * top + 1, float(tok_rows), jnp.where(lane == 4 * top + 2, 1.0, worth))

    def read(i, _, own):
        facts = all_ref[pl.ds(pl.multiple_of(i * LANES, LANES), LANES), :].astype(F32)
        values = (
            pltpu.roll(facts, LANES - top, 1)
            + pltpu.roll(facts, LANES - 2 * top, 1)
            + pltpu.roll(facts, LANES - 3 * top, 1)
        )
        order = jnp.sum(facts * worth, axis=1, keepdims=True)
        for e, expert in enumerate(experts):
            named = (lane < top) & (facts == expert.astype(F32))
            gate = jnp.sum(jnp.where(named, values, 0.0), axis=1, keepdims=True)
            key = jnp.where(gate > 0.0, order, BIG)
            row_ref[e, pl.ds(i, 1), :] = jnp.sum(jnp.where(eye, key, 0.0), axis=0, keepdims=True)
            if own:
                key_ref[e, i] = jnp.broadcast_to(key, (LANES, LANES))
                held = pl.ds(pl.multiple_of((e * mine + i) * LANES, LANES), LANES)
                out_ref[held, :] = jnp.broadcast_to(gate, (LANES, LANES))
        return 0

    lax.fori_loop(0, mine, functools.partial(read, own=True), 0, unroll=min(mine, 4))
    lax.fori_loop(mine, tiles, functools.partial(read, own=False), 0, unroll=min(mine, 4))
    for e, expert in enumerate(experts):
        limit = capacity_ref[expert].astype(F32)

        def judge(i, _, e=e, limit=limit):
            held = pl.ds(pl.multiple_of((e * mine + i) * LANES, LANES), LANES)
            key = key_ref[e, i]

            def count(j, smaller):
                return smaller + (row_ref[e, pl.ds(j, 1), :] < key).astype(F32)

            smaller = lax.fori_loop(0, tiles, count, jnp.zeros((LANES, LANES), F32), unroll=min(tiles, 8))
            rank = jnp.sum(smaller, axis=1, keepdims=True)
            out_ref[held, :] = jnp.where(rank < limit, out_ref[held, :], 0.0)
            return 0

        lax.fori_loop(0, mine, judge, 0, unroll=min(mine, 4))


def weigh(me, capacity, facts, top, tok_rows):
    total = sum(f.shape[0] for f in facts)
    tiles = total // LANES
    return pl.pallas_call(
        functools.partial(weigh_kernel, top, tok_rows),
        in_specs=[pl.BlockSpec(memory_space=pltpu.SMEM)] * 2
        + [pl.BlockSpec(memory_space=pltpu.VMEM)] * len(facts),
        out_specs=pl.BlockSpec(memory_space=pltpu.VMEM),
        out_shape=jax.ShapeDtypeStruct((total, LANES), F32),
        scratch_shapes=[
            pltpu.VMEM((total, LANES), BF16),
            pltpu.VMEM((2, tiles // 2, LANES, LANES), F32),
            pltpu.VMEM((2, tiles, LANES), F32),
        ],
        compiler_params=pltpu.CompilerParams(vmem_limit_bytes=24 * MIB),
        cost_estimate=pl.CostEstimate(flops=1, bytes_accessed=1, transcendentals=0),
    )(me, capacity, *facts)


def pack_kernel(*refs):
    rows = refs[0].shape[0]
    for k, ref in enumerate(refs[:-1]):
        refs[-1][k * rows : (k + 1) * rows, :] = ref[...]


def pack(blocks):
    rows, wide = blocks[0].shape
    return pl.pallas_call(
        pack_kernel,
        in_specs=[pl.BlockSpec(memory_space=pltpu.VMEM)] * len(blocks),
        out_specs=pl.BlockSpec(memory_space=pltpu.VMEM),
        out_shape=jax.ShapeDtypeStruct((len(blocks) * rows, wide), BF16),
        compiler_params=pltpu.CompilerParams(vmem_limit_bytes=24 * MIB),
        cost_estimate=pl.CostEstimate(flops=1, bytes_accessed=1, transcendentals=0),
    )(*blocks)


def combine_kernel(rows, sums, weighted, *refs):
    ins, outs = refs[: -len(sums)], refs[-len(sums) :]
    width = outs[0].shape[1]
    for lanes in range(0, width, 256):
        for terms, out in zip(sums, outs):
            total = None
            for which, first, place in terms:
                value = ins[which][first : first + rows, lanes : lanes + 256].astype(F32)
                if place is not None:
                    value = value * ins[weighted][place : place + rows, :1]
                total = value if total is None else total + value
            out[:, lanes : lanes + 256] = total.astype(out.dtype)


def combine(arrays, weights, sums, kind=BF16):
    rows = weights.shape[0] // 16
    width = arrays[0].shape[1]
    sums = [[(a, b * rows, None if p is None else p * rows) for a, b, p in terms] for terms in sums]
    return pl.pallas_call(
        functools.partial(combine_kernel, rows, sums, len(arrays)),
        in_specs=[pl.BlockSpec(memory_space=pltpu.VMEM)] * (len(arrays) + 1),
        out_specs=[pl.BlockSpec(memory_space=pltpu.VMEM)] * len(sums),
        out_shape=[jax.ShapeDtypeStruct((rows, width), kind)] * len(sums),
        compiler_params=pltpu.CompilerParams(vmem_limit_bytes=24 * MIB),
        cost_estimate=pl.CostEstimate(flops=1, bytes_accessed=1, transcendentals=0),
    )(*arrays, weights)


def load_kernel(*refs):
    count = len(refs) // 2
    sems = refs[-1]
    copies = [pltpu.make_async_copy(refs[k], refs[count + k], sems.at[k]) for k in range(count)]
    for copy in copies:
        copy.start()
    for copy in copies:
        copy.wait()


def load(*arrays):
    size = sum(a.size * 2 for a in arrays)
    return pl.pallas_call(
        load_kernel,
        in_specs=[pl.BlockSpec(memory_space=pl.ANY)] * len(arrays),
        out_specs=[pl.BlockSpec(memory_space=pltpu.VMEM)] * len(arrays),
        out_shape=[jax.ShapeDtypeStruct(a.shape, a.dtype) for a in arrays],
        scratch_shapes=[pltpu.SemaphoreType.DMA((len(arrays),))],
        compiler_params=pltpu.CompilerParams(vmem_limit_bytes=size + 4 * MIB),
    )(*arrays)


FF_TILE, OUT_TILE = 256, 512


def expert_kernel(*refs):
    x_refs, (gate_ref, up_ref, down_ref, out_ref, x, hidden) = refs[:-6], refs[-6:]
    width, ff = x.shape[1], hidden.shape[1]
    at = 0
    for ref in x_refs:
        x[at : at + ref.shape[0], :] = ref[:, :width]
        at += ref.shape[0]
    for k in range(ff // FF_TILE):
        lanes = slice(k * FF_TILE, (k + 1) * FF_TILE)
        gated = jnp.dot(x[...], gate_ref[0, :, lanes], preferred_element_type=F32)
        upward = jnp.dot(x[...], up_ref[0, :, lanes], preferred_element_type=F32)
        hidden[:, lanes] = (gated / (1.0 + jnp.exp(-gated)) * upward).astype(BF16)
    for k in range(width // OUT_TILE):
        lanes = slice(k * OUT_TILE, (k + 1) * OUT_TILE)
        out_ref[:, lanes] = jnp.dot(hidden[...], down_ref[0, :, lanes], preferred_element_type=F32).astype(BF16)


def expert(arrays, matrices):
    ff, width = matrices[2].shape[1:]
    rows = sum(a.shape[0] for a in arrays)
    held = rows * 2 * (width + ff) + 4 * rows * (2 * FF_TILE + OUT_TILE)
    return pl.pallas_call(
        expert_kernel,
        in_specs=[pl.BlockSpec(memory_space=pltpu.VMEM)] * (len(arrays) + 3),
        out_specs=pl.BlockSpec(memory_space=pltpu.VMEM),
        out_shape=jax.ShapeDtypeStruct((rows, width), BF16),
        scratch_shapes=[pltpu.VMEM((rows, width), BF16), pltpu.VMEM((rows, ff), BF16)],
        compiler_params=pltpu.CompilerParams(vmem_limit_bytes=held + 20 * MIB),
        cost_estimate=pl.CostEstimate(flops=1, bytes_accessed=1, transcendentals=0),
    )(*arrays, *matrices)


def orders(ep):
    bits = list(range(ep.bit_length() - 1))[::-1]
    return (bits, bits[:-2] + bits[:-3:-1])


def send(array, ep, flips):
    pairs = []
    for place in range(ep):
        for core, order in enumerate(orders(ep)):
            to = place
            for flip in flips:
                to ^= 1 << order[flip]
            pairs.append((2 * place + core, 2 * to + core))
    return lax.ppermute(array, ("ep", "sub"), pairs)


def cross(array):
    return lax.ppermute(array, "sub", [(0, 1), (1, 0)])


def add(*terms):
    return sum([t.astype(F32) for t in terms]).astype(BF16)


def on_device(ep, tokens, routes, gates, priority, capacity, w_gate, w_up, w_down):
    tok_rows, width = tokens.shape
    top = routes.shape[1]
    steps = ep.bit_length() - 1
    me = (lax.axis_index("ep") * 2 + lax.axis_index("sub")).astype(jnp.int32).reshape(1)
    held = prepare(me, tokens, routes, gates, priority)
    for step in range(steps - 3):
        held = jnp.concatenate([held, send(held, ep, [step])])
    base = held.shape[0]
    own1, own2, own4 = send(held, ep, [-3]), send(held, ep, [-2]), send(held, ep, [-1])
    first = cross(held)
    matrices = load(w_gate, w_up, w_down)
    own1, first, matrices = lax.optimization_barrier((own1, first, matrices))
    crossed = cross(pack([own1, own2, own4]))
    own3 = send(own1, ep, [-2])
    own5 = send(own1, ep, [-1])
    own6 = send(own2, ep, [-1])
    theirs = expert([first, crossed], matrices)
    own3, theirs = lax.optimization_barrier((own3, theirs))
    own7 = send(own3, ep, [-1])
    own3, own5, own6, own7, theirs = lax.optimization_barrier((own3, own5, own6, own7, theirs))
    far = [own3, own5, own6, own7]
    far_crossed = cross(pack(far))
    far_made = expert(far, matrices)
    far_crossed, far_made = lax.optimization_barrier((far_crossed, far_made))
    far_back = cross(expert([far_crossed], matrices))
    near = [held, own1, own2, own4]
    weights = weigh(me, capacity, near + far + [first, crossed, far_crossed], top, tok_rows)

    def part(mine, back, block, place):
        return [(mine, block, place), (back, block, 8 + place)]

    send7, send5 = combine([far_made, far_back], weights, [part(0, 1, 3, 7), part(0, 1, 1, 5)])
    back7 = send(send7, ep, [-1])
    back5 = send(send5, ep, [-1])
    send3, send6 = combine(
        [far_made, far_back, back7], weights, [part(0, 1, 0, 4) + [(2, 0, None)], part(0, 1, 2, 6)]
    )
    back3 = send(send3, ep, [-2])
    near_made = expert(near, matrices)
    near_made, send6 = lax.optimization_barrier((near_made, send6))
    back6 = send(send6, ep, [-1])
    near_back = cross(theirs)
    near_made, back3, back5 = lax.optimization_barrier((near_made, back3, back5))
    (send1,) = combine([near_made, near_back, back3, back5], weights, [part(0, 1, 1, 1) + [(2, 0, None), (3, 0, None)]])
    back1 = send(send1, ep, [-3])
    back6, send1 = lax.optimization_barrier((back6, send1))
    send2, send4 = combine(
        [near_made, near_back, back6], weights, [part(0, 1, 2, 2) + [(2, 0, None)], part(0, 1, 3, 3)]
    )
    back2 = send(send2, ep, [-2])
    back4 = send(send4, ep, [-1])
    (total,) = combine([near_made, near_back, back1], weights, [part(0, 1, 0, 0) + [(2, 0, None)]], F32)
    back2, back4, total = lax.optimization_barrier((back2, back4, total))
    (total,) = combine([total, back2, back4], weights, [[(0, 0, None), (1, 0, None), (2, 0, None)]])
    for step in range(steps - 3)[::-1]:
        half = total.shape[0] // 2
        total = add(total[:half], send(total[half:], ep, [step]))
    return total


def solution(mesh):
    in_specs = (
        P(("groups", "ep", "sub"), None),
        P(("groups", "ep", "sub"), None),
        P(("groups", "ep", "sub"), None),
        P(("groups", "ep", "sub")),
        P(),
        P(("ep", "sub"), None, None),
        P(("ep", "sub"), None, None),
        P(("ep", "sub"), None, None),
    )
    out_specs = P(("groups", "ep", "sub"), None)
    return jax.shard_map(
        functools.partial(on_device, mesh.shape["ep"]),
        mesh=mesh,
        in_specs=in_specs,
        out_specs=out_specs,
        check_vma=False,
    )
```

```python
import functools

import jax
import jax.numpy as jnp
from jax import lax
from jax.experimental import pallas as pl
from jax.experimental.pallas import tpu as pltpu
from jax.sharding import PartitionSpec as P

F32 = jnp.float32
BF16 = jnp.bfloat16
LANES = 128
BIG = 1e9
MIB = 1024 * 1024


def iota(shape, dim):
    return lax.broadcasted_iota(jnp.int32, shape, dim)


def prepare_kernel(me_ref, tokens_ref, routes_ref, gates_ref, prio_ref, rows_ref):
    rows, width = tokens_ref.shape
    top = routes_ref.shape[0]
    for block in range(width // LANES):
        lanes = slice(block * LANES, (block + 1) * LANES)
        x = tokens_ref[:, lanes].astype(F32)
        largest = jnp.max(jnp.abs(x), axis=1, keepdims=True)
        scale = ((largest + 1e-06) / 448.0).astype(BF16).astype(F32)
        quantized = (x / scale).astype(BF16)
        rows_ref[:, lanes] = (quantized.astype(F32) * scale).astype(BF16)
    gates = gates_ref[...]
    high = gates.astype(BF16)
    middle = (gates - high.astype(F32)).astype(BF16)
    low = (gates - high.astype(F32) - middle.astype(F32)).astype(BF16)
    place, token = iota((top, rows), 0), iota((top, rows), 1)
    other = jnp.where(place == 0, prio_ref[...], jnp.where(place == 1, me_ref[0], token))
    fields = [routes_ref[...].astype(F32), high.astype(F32), middle.astype(F32), low.astype(F32), other.astype(F32)]
    facts = jnp.zeros((rows, LANES), F32)
    for k, field in enumerate(fields):
        spot = iota((top, LANES), 1) == iota((top, LANES), 0) + k * top
        facts += lax.dot_general(
            field.astype(BF16),
            spot.astype(F32).astype(BF16),
            (((0,), (0,)), ((), ())),
            preferred_element_type=F32,
        )
    rows_ref[:, width:] = facts.astype(BF16)


def prepare(me, tokens, routes, gates, priority):
    rows, width = tokens.shape
    return pl.pallas_call(
        prepare_kernel,
        in_specs=[pl.BlockSpec(memory_space=pltpu.SMEM)] + [pl.BlockSpec(memory_space=pltpu.VMEM)] * 4,
        out_specs=pl.BlockSpec(memory_space=pltpu.VMEM),
        out_shape=jax.ShapeDtypeStruct((rows, width + LANES), BF16),
    )(me, tokens, routes.T, gates.T, priority.reshape(1, rows))


def weigh_kernel(top, tok_rows, me_ref, capacity_ref, *refs):
    fact_refs, out_ref, (all_ref, key_ref, row_ref) = refs[:-4], refs[-4], refs[-3:]
    total = all_ref.shape[0]
    at = 0
    for ref in fact_refs:
        rows, wide = ref.shape
        all_ref[at : at + rows, :] = ref[:, wide - LANES :]
        at += rows
    eye = iota((LANES, LANES), 0) == iota((LANES, LANES), 1)
    lane = iota((LANES, LANES), 1)
    tiles = total // LANES
    mine = tiles // 2
    experts = (me_ref[0], me_ref[0] + 1 - 2 * lax.rem(me_ref[0], 2))
    worth = jnp.where(lane == 4 * top, float(total), 0.0)
    worth = jnp.where(lane == 4 * top + 1, float(tok_rows), jnp.where(lane == 4 * top + 2, 1.0, worth))

    def read(i, _, own):
        facts = all_ref[pl.ds(pl.multiple_of(i * LANES, LANES), LANES), :].astype(F32)
        values = (
            pltpu.roll(facts, LANES - top, 1)
            + pltpu.roll(facts, LANES - 2 * top, 1)
            + pltpu.roll(facts, LANES - 3 * top, 1)
        )
        order = jnp.sum(facts * worth, axis=1, keepdims=True)
        for e, expert in enumerate(experts):
            named = (lane < top) & (facts == expert.astype(F32))
            gate = jnp.sum(jnp.where(named, values, 0.0), axis=1, keepdims=True)
            key = jnp.where(gate > 0.0, order, BIG)
            row_ref[e, pl.ds(i, 1), :] = jnp.sum(jnp.where(eye, key, 0.0), axis=0, keepdims=True)
            if own:
                key_ref[e, i] = jnp.broadcast_to(key, (LANES, LANES))
                held = pl.ds(pl.multiple_of((e * mine + i) * LANES, LANES), LANES)
                out_ref[held, :] = jnp.broadcast_to(gate, (LANES, LANES))
        return 0

    lax.fori_loop(0, mine, functools.partial(read, own=True), 0, unroll=min(mine, 4))
    lax.fori_loop(mine, tiles, functools.partial(read, own=False), 0, unroll=min(mine, 4))
    for e, expert in enumerate(experts):
        limit = capacity_ref[expert].astype(F32)

        def judge(i, _, e=e, limit=limit):
            held = pl.ds(pl.multiple_of((e * mine + i) * LANES, LANES), LANES)
            key = key_ref[e, i]

            def count(j, smaller):
                return smaller + (row_ref[e, pl.ds(j, 1), :] < key).astype(F32)

            smaller = lax.fori_loop(0, tiles, count, jnp.zeros((LANES, LANES), F32), unroll=min(tiles, 8))
            rank = jnp.sum(smaller, axis=1, keepdims=True)
            out_ref[held, :] = jnp.where(rank < limit, out_ref[held, :], 0.0)
            return 0

        lax.fori_loop(0, mine, judge, 0, unroll=min(mine, 4))


def weigh(me, capacity, facts, top, tok_rows):
    total = sum(f.shape[0] for f in facts)
    tiles = total // LANES
    return pl.pallas_call(
        functools.partial(weigh_kernel, top, tok_rows),
        in_specs=[pl.BlockSpec(memory_space=pltpu.SMEM)] * 2
        + [pl.BlockSpec(memory_space=pltpu.VMEM)] * len(facts),
        out_specs=pl.BlockSpec(memory_space=pltpu.VMEM),
        out_shape=jax.ShapeDtypeStruct((total, LANES), F32),
        scratch_shapes=[
            pltpu.VMEM((total, LANES), BF16),
            pltpu.VMEM((2, tiles // 2, LANES, LANES), F32),
            pltpu.VMEM((2, tiles, LANES), F32),
        ],
        compiler_params=pltpu.CompilerParams(vmem_limit_bytes=24 * MIB),
        cost_estimate=pl.CostEstimate(flops=1, bytes_accessed=1, transcendentals=0),
    )(me, capacity, *facts)


def pack_kernel(*refs):
    rows = refs[0].shape[0]
    for k, ref in enumerate(refs[:-1]):
        refs[-1][k * rows : (k + 1) * rows, :] = ref[...]


def pack(blocks):
    rows, wide = blocks[0].shape
    return pl.pallas_call(
        pack_kernel,
        in_specs=[pl.BlockSpec(memory_space=pltpu.VMEM)] * len(blocks),
        out_specs=pl.BlockSpec(memory_space=pltpu.VMEM),
        out_shape=jax.ShapeDtypeStruct((len(blocks) * rows, wide), BF16),
        compiler_params=pltpu.CompilerParams(vmem_limit_bytes=24 * MIB),
        cost_estimate=pl.CostEstimate(flops=1, bytes_accessed=1, transcendentals=0),
    )(*blocks)


def combine_kernel(rows, sums, weighted, *refs):
    ins, outs = refs[: -len(sums)], refs[-len(sums) :]
    width = outs[0].shape[1]
    for lanes in range(0, width, 256):
        for terms, out in zip(sums, outs):
            total = None
            for which, first, place in terms:
                value = ins[which][first : first + rows, lanes : lanes + 256].astype(F32)
                if place is not None:
                    value = value * ins[weighted][place : place + rows, :1]
                total = value if total is None else total + value
            out[:, lanes : lanes + 256] = total.astype(out.dtype)


def combine(arrays, weights, sums, kind=BF16):
    rows = weights.shape[0] // 16
    width = arrays[0].shape[1]
    sums = [[(a, b * rows, None if p is None else p * rows) for a, b, p in terms] for terms in sums]
    return pl.pallas_call(
        functools.partial(combine_kernel, rows, sums, len(arrays)),
        in_specs=[pl.BlockSpec(memory_space=pltpu.VMEM)] * (len(arrays) + 1),
        out_specs=[pl.BlockSpec(memory_space=pltpu.VMEM)] * len(sums),
        out_shape=[jax.ShapeDtypeStruct((rows, width), kind)] * len(sums),
        compiler_params=pltpu.CompilerParams(vmem_limit_bytes=24 * MIB),
        cost_estimate=pl.CostEstimate(flops=1, bytes_accessed=1, transcendentals=0),
    )(*arrays, weights)


def load_kernel(*refs):
    count = len(refs) // 2
    sems = refs[-1]
    copies = [pltpu.make_async_copy(refs[k], refs[count + k], sems.at[k]) for k in range(count)]
    for copy in copies:
        copy.start()
    for copy in copies:
        copy.wait()


def load(*arrays):
    size = sum(a.size * 2 for a in arrays)
    return pl.pallas_call(
        load_kernel,
        in_specs=[pl.BlockSpec(memory_space=pl.ANY)] * len(arrays),
        out_specs=[pl.BlockSpec(memory_space=pltpu.VMEM)] * len(arrays),
        out_shape=[jax.ShapeDtypeStruct(a.shape, a.dtype) for a in arrays],
        scratch_shapes=[pltpu.SemaphoreType.DMA((len(arrays),))],
        compiler_params=pltpu.CompilerParams(vmem_limit_bytes=size + 4 * MIB),
    )(*arrays)


FF_TILE, OUT_TILE = 256, 512


def expert_kernel(*refs):
    x_refs, (gate_ref, up_ref, down_ref, out_ref, x, hidden) = refs[:-6], refs[-6:]
    width, ff = x.shape[1], hidden.shape[1]
    at = 0
    for ref in x_refs:
        x[at : at + ref.shape[0], :] = ref[:, :width]
        at += ref.shape[0]
    for k in range(ff // FF_TILE):
        lanes = slice(k * FF_TILE, (k + 1) * FF_TILE)
        gated = jnp.dot(x[...], gate_ref[0, :, lanes], preferred_element_type=F32)
        upward = jnp.dot(x[...], up_ref[0, :, lanes], preferred_element_type=F32)
        hidden[:, lanes] = (gated / (1.0 + jnp.exp(-gated)) * upward).astype(BF16)
    for k in range(width // OUT_TILE):
        lanes = slice(k * OUT_TILE, (k + 1) * OUT_TILE)
        out_ref[:, lanes] = jnp.dot(hidden[...], down_ref[0, :, lanes], preferred_element_type=F32).astype(BF16)


def expert(arrays, matrices):
    ff, width = matrices[2].shape[1:]
    rows = sum(a.shape[0] for a in arrays)
    held = rows * 2 * (width + ff) + 4 * rows * (2 * FF_TILE + OUT_TILE)
    return pl.pallas_call(
        expert_kernel,
        in_specs=[pl.BlockSpec(memory_space=pltpu.VMEM)] * (len(arrays) + 3),
        out_specs=pl.BlockSpec(memory_space=pltpu.VMEM),
        out_shape=jax.ShapeDtypeStruct((rows, width), BF16),
        scratch_shapes=[pltpu.VMEM((rows, width), BF16), pltpu.VMEM((rows, ff), BF16)],
        compiler_params=pltpu.CompilerParams(vmem_limit_bytes=held + 20 * MIB),
        cost_estimate=pl.CostEstimate(flops=1, bytes_accessed=1, transcendentals=0),
    )(*arrays, *matrices)


def orders(ep):
    bits = list(range(ep.bit_length() - 1))[::-1]
    return (bits, bits[:-2] + bits[:-3:-1])


def send(array, ep, flips):
    pairs = []
    for place in range(ep):
        for core, order in enumerate(orders(ep)):
            to = place
            for flip in flips:
                to ^= 1 << order[flip]
            pairs.append((2 * place + core, 2 * to + core))
    return lax.ppermute(array, ("ep", "sub"), pairs)


def cross(array):
    return lax.ppermute(array, "sub", [(0, 1), (1, 0)])


def add(*terms):
    return sum([t.astype(F32) for t in terms]).astype(BF16)


def on_device(ep, tokens, routes, gates, priority, capacity, w_gate, w_up, w_down):
    tok_rows, width = tokens.shape
    top = routes.shape[1]
    steps = ep.bit_length() - 1
    me = (lax.axis_index("ep") * 2 + lax.axis_index("sub")).astype(jnp.int32).reshape(1)
    held = prepare(me, tokens, routes, gates, priority)
    for step in range(steps - 3):
        held = jnp.concatenate([held, send(held, ep, [step])])
    base = held.shape[0]
    own1, own2, own4 = send(held, ep, [-3]), send(held, ep, [-2]), send(held, ep, [-1])
    first = cross(held)
    matrices = load(w_gate, w_up, w_down)
    own1, first, matrices = lax.optimization_barrier((own1, first, matrices))
    crossed = cross(pack([own1, own2, own4]))
    own3 = send(own1, ep, [-2])
    own5 = send(own1, ep, [-1])
    own6 = send(own2, ep, [-1])
    theirs = expert([first, crossed], matrices)
    own3, theirs = lax.optimization_barrier((own3, theirs))
    own7 = send(own3, ep, [-1])
    own3, own5, own6, own7, theirs = lax.optimization_barrier((own3, own5, own6, own7, theirs))
    far = [own3, own5, own6, own7]
    far_crossed = cross(pack(far))
    far_made = expert(far, matrices)
    far_crossed, far_made = lax.optimization_barrier((far_crossed, far_made))
    far_back = cross(expert([far_crossed], matrices))
    near = [held, own1, own2, own4]
    weights = weigh(me, capacity, near + far + [first, crossed, far_crossed], top, tok_rows)

    def part(mine, back, block, place):
        return [(mine, block, place), (back, block, 8 + place)]

    send7, send5 = combine([far_made, far_back], weights, [part(0, 1, 3, 7), part(0, 1, 1, 5)])
    back7 = send(send7, ep, [-1])
    back5 = send(send5, ep, [-1])
    send3, send6 = combine(
        [far_made, far_back, back7], weights, [part(0, 1, 0, 4) + [(2, 0, None)], part(0, 1, 2, 6)]
    )
    back3 = send(send3, ep, [-2])
    near_made = expert(near, matrices)
    near_made, send6 = lax.optimization_barrier((near_made, send6))
    back6 = send(send6, ep, [-1])
    near_back = cross(theirs)
    (send4,) = combine([near_made, near_back], weights, [part(0, 1, 3, 3)])
    back4 = send(send4, ep, [-1])
    back3, back5, send4 = lax.optimization_barrier((back3, back5, send4))
    (send1,) = combine([near_made, near_back, back3, back5], weights, [part(0, 1, 1, 1) + [(2, 0, None), (3, 0, None)]])
    back1 = send(send1, ep, [-3])
    back6, send1 = lax.optimization_barrier((back6, send1))
    (send2,) = combine([near_made, near_back, back6], weights, [part(0, 1, 2, 2) + [(2, 0, None)]])
    back2 = send(send2, ep, [-2])
    (total,) = combine([near_made, near_back, back4], weights, [part(0, 1, 0, 0) + [(2, 0, None)]], F32)
    back1, total = lax.optimization_barrier((back1, total))
    (total,) = combine([total, back1], weights, [[(0, 0, None), (1, 0, None)]], F32)
    back2, total = lax.optimization_barrier((back2, total))
    (total,) = combine([total, back2], weights, [[(0, 0, None), (1, 0, None)]])
    for step in range(steps - 3)[::-1]:
        half = total.shape[0] // 2
        total = add(total[:half], send(total[half:], ep, [step]))
    return total


def solution(mesh):
    in_specs = (
        P(("groups", "ep", "sub"), None),
        P(("groups", "ep", "sub"), None),
        P(("groups", "ep", "sub"), None),
        P(("groups", "ep", "sub")),
        P(),
        P(("ep", "sub"), None, None),
        P(("ep", "sub"), None, None),
        P(("ep", "sub"), None, None),
    )
    out_specs = P(("groups", "ep", "sub"), None)
    return jax.shard_map(
        functools.partial(on_device, mesh.shape["ep"]),
        mesh=mesh,
        in_specs=in_specs,
        out_specs=out_specs,
        check_vma=False,
    )
```

```python
import functools

import jax
import jax.numpy as jnp
from jax import lax
from jax.experimental import pallas as pl
from jax.experimental.pallas import tpu as pltpu
from jax.sharding import PartitionSpec as P

F32 = jnp.float32
BF16 = jnp.bfloat16
LANES = 128
BIG = 1e9
MIB = 1024 * 1024


def iota(shape, dim):
    return lax.broadcasted_iota(jnp.int32, shape, dim)


def prepare_kernel(me_ref, tokens_ref, routes_ref, gates_ref, prio_ref, rows_ref):
    rows, width = tokens_ref.shape
    top = routes_ref.shape[0]
    for block in range(width // LANES):
        lanes = slice(block * LANES, (block + 1) * LANES)
        x = tokens_ref[:, lanes].astype(F32)
        largest = jnp.max(jnp.abs(x), axis=1, keepdims=True)
        scale = ((largest + 1e-06) / 448.0).astype(BF16).astype(F32)
        quantized = (x / scale).astype(BF16)
        rows_ref[:, lanes] = (quantized.astype(F32) * scale).astype(BF16)
    gates = gates_ref[...]
    high = gates.astype(BF16)
    middle = (gates - high.astype(F32)).astype(BF16)
    low = (gates - high.astype(F32) - middle.astype(F32)).astype(BF16)
    place, token = iota((top, rows), 0), iota((top, rows), 1)
    other = jnp.where(place == 0, prio_ref[...], jnp.where(place == 1, me_ref[0], token))
    fields = [routes_ref[...].astype(F32), high.astype(F32), middle.astype(F32), low.astype(F32), other.astype(F32)]
    facts = jnp.zeros((rows, LANES), F32)
    for k, field in enumerate(fields):
        spot = iota((top, LANES), 1) == iota((top, LANES), 0) + k * top
        facts += lax.dot_general(
            field.astype(BF16),
            spot.astype(F32).astype(BF16),
            (((0,), (0,)), ((), ())),
            preferred_element_type=F32,
        )
    rows_ref[:, width:] = facts.astype(BF16)


def prepare(me, tokens, routes, gates, priority):
    rows, width = tokens.shape
    return pl.pallas_call(
        prepare_kernel,
        in_specs=[pl.BlockSpec(memory_space=pltpu.SMEM)] + [pl.BlockSpec(memory_space=pltpu.VMEM)] * 4,
        out_specs=pl.BlockSpec(memory_space=pltpu.VMEM),
        out_shape=jax.ShapeDtypeStruct((rows, width + LANES), BF16),
    )(me, tokens, routes.T, gates.T, priority.reshape(1, rows))


def weigh_kernel(top, tok_rows, me_ref, capacity_ref, *refs):
    fact_refs, out_ref, (all_ref, key_ref, row_ref) = refs[:-4], refs[-4], refs[-3:]
    total = all_ref.shape[0]
    at = 0
    for ref in fact_refs:
        rows, wide = ref.shape
        all_ref[at : at + rows, :] = ref[:, wide - LANES :]
        at += rows
    eye = iota((LANES, LANES), 0) == iota((LANES, LANES), 1)
    lane, line = iota((LANES, LANES), 1), iota((LANES, LANES), 0)
    tiles = total // LANES
    mine = tiles // 2
    experts = (me_ref[0], me_ref[0] + 1 - 2 * lax.rem(me_ref[0], 2))

    def table(values):
        return values.astype(F32).astype(BF16)

    def times(left, right):
        return jnp.dot(left, right, preferred_element_type=F32)

    ones = jnp.ones((LANES, LANES), BF16)
    worth = jnp.where(line == 4 * top, float(total), 0.0)
    worth = jnp.where(line == 4 * top + 1, float(tok_rows), jnp.where(line == 4 * top + 2, 1.0, worth))
    worth = table(worth)
    shift = lane - line
    spread = table((line < top) & ((shift == top) | (shift == 2 * top) | (shift == 3 * top)))

    def read(i, _, own):
        facts = all_ref[pl.ds(pl.multiple_of(i * LANES, LANES), LANES), :]
        order = times(facts, worth)
        for e, expert in enumerate(experts):
            named = table((lane < top) & (facts.astype(F32) == expert.astype(F32)))
            parts = (times(named, spread) * facts.astype(F32)).astype(BF16)
            gate = times(parts, ones)
            key = jnp.where(gate > 0.0, order, BIG)
            row_ref[e, pl.ds(i, 1), :] = jnp.sum(jnp.where(eye, key, 0.0), axis=0, keepdims=True)
            if own:
                key_ref[e, i] = key
                held = pl.ds(pl.multiple_of((e * mine + i) * LANES, LANES), LANES)
                out_ref[held, :] = gate
        return 0

    lax.fori_loop(0, mine, functools.partial(read, own=True), 0, unroll=min(mine, 4))
    lax.fori_loop(mine, tiles, functools.partial(read, own=False), 0, unroll=min(mine, 4))
    for e, expert in enumerate(experts):
        limit = capacity_ref[expert].astype(F32)

        def judge(i, _, e=e, limit=limit):
            held = pl.ds(pl.multiple_of((e * mine + i) * LANES, LANES), LANES)
            key = key_ref[e, i]

            def count(j, smaller):
                return smaller + (row_ref[e, pl.ds(j, 1), :] < key).astype(F32)

            smaller = lax.fori_loop(0, tiles, count, jnp.zeros((LANES, LANES), F32), unroll=min(tiles, 8))
            rank = times(smaller.astype(BF16), ones)
            out_ref[held, :] = jnp.where(rank < limit, out_ref[held, :], 0.0)
            return 0

        lax.fori_loop(0, mine, judge, 0, unroll=min(mine, 4))


def weigh(me, capacity, facts, top, tok_rows):
    total = sum(f.shape[0] for f in facts)
    tiles = total // LANES
    return pl.pallas_call(
        functools.partial(weigh_kernel, top, tok_rows),
        in_specs=[pl.BlockSpec(memory_space=pltpu.SMEM)] * 2
        + [pl.BlockSpec(memory_space=pltpu.VMEM)] * len(facts),
        out_specs=pl.BlockSpec(memory_space=pltpu.VMEM),
        out_shape=jax.ShapeDtypeStruct((total, LANES), F32),
        scratch_shapes=[
            pltpu.VMEM((total, LANES), BF16),
            pltpu.VMEM((2, tiles // 2, LANES, LANES), F32),
            pltpu.VMEM((2, tiles, LANES), F32),
        ],
        compiler_params=pltpu.CompilerParams(vmem_limit_bytes=24 * MIB),
        cost_estimate=pl.CostEstimate(flops=1, bytes_accessed=1, transcendentals=0),
    )(me, capacity, *facts)


def pack_kernel(*refs):
    rows = refs[0].shape[0]
    for k, ref in enumerate(refs[:-1]):
        refs[-1][k * rows : (k + 1) * rows, :] = ref[...]


def pack(blocks):
    rows, wide = blocks[0].shape
    return pl.pallas_call(
        pack_kernel,
        in_specs=[pl.BlockSpec(memory_space=pltpu.VMEM)] * len(blocks),
        out_specs=pl.BlockSpec(memory_space=pltpu.VMEM),
        out_shape=jax.ShapeDtypeStruct((len(blocks) * rows, wide), BF16),
        compiler_params=pltpu.CompilerParams(vmem_limit_bytes=24 * MIB),
        cost_estimate=pl.CostEstimate(flops=1, bytes_accessed=1, transcendentals=0),
    )(*blocks)


def combine_kernel(rows, sums, weighted, *refs):
    ins, outs = refs[: -len(sums)], refs[-len(sums) :]
    width = outs[0].shape[1]
    for lanes in range(0, width, 256):
        for terms, out in zip(sums, outs):
            total = None
            for which, first, place in terms:
                value = ins[which][first : first + rows, lanes : lanes + 256].astype(F32)
                if place is not None:
                    value = value * ins[weighted][place : place + rows, :1]
                total = value if total is None else total + value
            out[:, lanes : lanes + 256] = total.astype(out.dtype)


def combine(arrays, weights, sums, kind=BF16):
    rows = weights.shape[0] // 16
    width = arrays[0].shape[1]
    sums = [[(a, b * rows, None if p is None else p * rows) for a, b, p in terms] for terms in sums]
    return pl.pallas_call(
        functools.partial(combine_kernel, rows, sums, len(arrays)),
        in_specs=[pl.BlockSpec(memory_space=pltpu.VMEM)] * (len(arrays) + 1),
        out_specs=[pl.BlockSpec(memory_space=pltpu.VMEM)] * len(sums),
        out_shape=[jax.ShapeDtypeStruct((rows, width), kind)] * len(sums),
        compiler_params=pltpu.CompilerParams(vmem_limit_bytes=24 * MIB),
        cost_estimate=pl.CostEstimate(flops=1, bytes_accessed=1, transcendentals=0),
    )(*arrays, weights)


def load_kernel(*refs):
    count = len(refs) // 2
    sems = refs[-1]
    copies = [pltpu.make_async_copy(refs[k], refs[count + k], sems.at[k]) for k in range(count)]
    for copy in copies:
        copy.start()
    for copy in copies:
        copy.wait()


def load(*arrays):
    size = sum(a.size * 2 for a in arrays)
    return pl.pallas_call(
        load_kernel,
        in_specs=[pl.BlockSpec(memory_space=pl.ANY)] * len(arrays),
        out_specs=[pl.BlockSpec(memory_space=pltpu.VMEM)] * len(arrays),
        out_shape=[jax.ShapeDtypeStruct(a.shape, a.dtype) for a in arrays],
        scratch_shapes=[pltpu.SemaphoreType.DMA((len(arrays),))],
        compiler_params=pltpu.CompilerParams(vmem_limit_bytes=size + 4 * MIB),
    )(*arrays)


FF_TILE, OUT_TILE = 256, 512


def expert_kernel(pieces, *refs):
    x_refs, (gate_ref, up_ref, down_ref) = refs[: -5 - pieces], refs[-5 - pieces : -2 - pieces]
    out_refs, (x, hidden) = refs[-2 - pieces : -2], refs[-2:]
    width, ff = x.shape[1], hidden.shape[1]
    at = 0
    for ref in x_refs:
        x[at : at + ref.shape[0], :] = ref[:, :width]
        at += ref.shape[0]
    for k in range(ff // FF_TILE):
        lanes = slice(k * FF_TILE, (k + 1) * FF_TILE)
        gated = jnp.dot(x[...], gate_ref[0, :, lanes], preferred_element_type=F32)
        upward = jnp.dot(x[...], up_ref[0, :, lanes], preferred_element_type=F32)
        hidden[:, lanes] = (gated / (1.0 + jnp.exp(-gated)) * upward).astype(BF16)
    for k in range(width // OUT_TILE):
        lanes = slice(k * OUT_TILE, (k + 1) * OUT_TILE)
        made = jnp.dot(hidden[...], down_ref[0, :, lanes], preferred_element_type=F32).astype(BF16)
        rows = made.shape[0] // pieces
        for k, out_ref in enumerate(out_refs):
            out_ref[:, lanes] = made[k * rows : (k + 1) * rows]


def expert(arrays, matrices, pieces=1):
    ff, width = matrices[2].shape[1:]
    rows = sum(a.shape[0] for a in arrays)
    held = rows * 2 * (width + ff) + 4 * rows * (2 * FF_TILE + OUT_TILE)
    made = pl.pallas_call(
        functools.partial(expert_kernel, pieces),
        in_specs=[pl.BlockSpec(memory_space=pltpu.VMEM)] * (len(arrays) + 3),
        out_specs=[pl.BlockSpec(memory_space=pltpu.VMEM)] * pieces,
        out_shape=[jax.ShapeDtypeStruct((rows // pieces, width), BF16)] * pieces,
        scratch_shapes=[pltpu.VMEM((rows, width), BF16), pltpu.VMEM((rows, ff), BF16)],
        compiler_params=pltpu.CompilerParams(vmem_limit_bytes=held + 20 * MIB),
        cost_estimate=pl.CostEstimate(flops=1, bytes_accessed=1, transcendentals=0),
    )(*arrays, *matrices)
    return made if pieces > 1 else made[0]


def orders(ep):
    bits = list(range(ep.bit_length() - 1))[::-1]
    return (bits, bits[:-2] + bits[:-3:-1])


def send(array, ep, flips):
    pairs = []
    for place in range(ep):
        for core, order in enumerate(orders(ep)):
            to = place
            for flip in flips:
                to ^= 1 << order[flip]
            pairs.append((2 * place + core, 2 * to + core))
    return lax.ppermute(array, ("ep", "sub"), pairs)


def cross(array):
    return lax.ppermute(array, "sub", [(0, 1), (1, 0)])


def add(*terms):
    return sum([t.astype(F32) for t in terms]).astype(BF16)


def on_device(ep, tokens, routes, gates, priority, capacity, w_gate, w_up, w_down):
    tok_rows, width = tokens.shape
    top = routes.shape[1]
    steps = ep.bit_length() - 1
    me = (lax.axis_index("ep") * 2 + lax.axis_index("sub")).astype(jnp.int32).reshape(1)
    held = prepare(me, tokens, routes, gates, priority)
    for step in range(steps - 3):
        held = jnp.concatenate([held, send(held, ep, [step])])
    base = held.shape[0]
    own1, own2, own4 = send(held, ep, [-3]), send(held, ep, [-2]), send(held, ep, [-1])
    first = cross(held)
    matrices = load(w_gate, w_up, w_down)
    own1, first, matrices = lax.optimization_barrier((own1, first, matrices))
    crossed = cross(pack([own1, own2, own4]))
    own3 = send(own1, ep, [-2])
    own5 = send(own1, ep, [-1])
    own6 = send(own2, ep, [-1])
    theirs = expert([first, crossed], matrices)
    own3, theirs = lax.optimization_barrier((own3, theirs))
    own7 = send(own3, ep, [-1])
    own3, own5, own6, own7, theirs = lax.optimization_barrier((own3, own5, own6, own7, theirs))
    far = [own5, own7, own3, own6]
    far_crossed = cross(pack(far))
    far_made = expert(far, matrices)
    far_crossed, far_made = lax.optimization_barrier((far_crossed, far_made))
    first_back, last_back = expert([far_crossed], matrices, 2)
    first_back = cross(first_back)
    near = [held, own1, own2, own4]
    weights = weigh(me, capacity, near + far + [first, crossed, far_crossed], top, tok_rows)
    weights, theirs, last_back = lax.optimization_barrier((weights, theirs, last_back))
    last_back = cross(last_back)

    def part(mine, back, block, place):
        return [(mine, block, place), (back, block, 8 + place)]

    send5, send7 = combine(
        [far_made, first_back], weights, [[(0, 0, 4), (1, 0, 12)], [(0, 1, 5), (1, 1, 13)]]
    )
    back7 = send(send7, ep, [-1])
    back5 = send(send5, ep, [-1])
    send3, send6 = combine(
        [far_made, last_back, back7],
        weights,
        [[(0, 2, 6), (1, 0, 14), (2, 0, None)], [(0, 3, 7), (1, 1, 15)]],
    )
    back3 = send(send3, ep, [-2])
    near_made = expert(near, matrices)
    near_made, send6 = lax.optimization_barrier((near_made, send6))
    back6 = send(send6, ep, [-1])
    near_back = cross(theirs)
    (send4,) = combine([near_made, near_back], weights, [part(0, 1, 3, 3)])
    back4 = send(send4, ep, [-1])
    back3, back5, send4 = lax.optimization_barrier((back3, back5, send4))
    (send1,) = combine([near_made, near_back, back3, back5], weights, [part(0, 1, 1, 1) + [(2, 0, None), (3, 0, None)]])
    back1 = send(send1, ep, [-3])
    back6, send1 = lax.optimization_barrier((back6, send1))
    (send2,) = combine([near_made, near_back, back6], weights, [part(0, 1, 2, 2) + [(2, 0, None)]])
    back2 = send(send2, ep, [-2])
    (total,) = combine([near_made, near_back, back4], weights, [part(0, 1, 0, 0) + [(2, 0, None)]], F32)
    back1, total = lax.optimization_barrier((back1, total))
    (total,) = combine([total, back1], weights, [[(0, 0, None), (1, 0, None)]], F32)
    back2, total = lax.optimization_barrier((back2, total))
    (total,) = combine([total, back2], weights, [[(0, 0, None), (1, 0, None)]])
    for step in range(steps - 3)[::-1]:
        half = total.shape[0] // 2
        total = add(total[:half], send(total[half:], ep, [step]))
    return total


def solution(mesh):
    in_specs = (
        P(("groups", "ep", "sub"), None),
        P(("groups", "ep", "sub"), None),
        P(("groups", "ep", "sub"), None),
        P(("groups", "ep", "sub")),
        P(),
        P(("ep", "sub"), None, None),
        P(("ep", "sub"), None, None),
        P(("ep", "sub"), None, None),
    )
    out_specs = P(("groups", "ep", "sub"), None)
    return jax.shard_map(
        functools.partial(on_device, mesh.shape["ep"]),
        mesh=mesh,
        in_specs=in_specs,
        out_specs=out_specs,
        check_vma=False,
    )
```

```python
import functools

import jax
import jax.numpy as jnp
from jax import lax
from jax.experimental import pallas as pl
from jax.experimental.pallas import tpu as pltpu
from jax.sharding import PartitionSpec as P

F32 = jnp.float32
BF16 = jnp.bfloat16
LANES = 128
BIG = 1e9
MIB = 1024 * 1024


def iota(shape, dim):
    return lax.broadcasted_iota(jnp.int32, shape, dim)


def prepare_kernel(me_ref, tokens_ref, routes_ref, gates_ref, prio_ref, rows_ref):
    rows, width = tokens_ref.shape
    top = routes_ref.shape[0]
    for block in range(width // LANES):
        lanes = slice(block * LANES, (block + 1) * LANES)
        x = tokens_ref[:, lanes].astype(F32)
        largest = jnp.max(jnp.abs(x), axis=1, keepdims=True)
        scale = ((largest + 1e-06) / 448.0).astype(BF16).astype(F32)
        quantized = (x / scale).astype(BF16)
        rows_ref[:, lanes] = (quantized.astype(F32) * scale).astype(BF16)
    gates = gates_ref[...]
    high = gates.astype(BF16)
    middle = (gates - high.astype(F32)).astype(BF16)
    low = (gates - high.astype(F32) - middle.astype(F32)).astype(BF16)
    place, token = iota((top, rows), 0), iota((top, rows), 1)
    other = jnp.where(place == 0, prio_ref[...], jnp.where(place == 1, me_ref[0], token))
    fields = [routes_ref[...].astype(F32), high.astype(F32), middle.astype(F32), low.astype(F32), other.astype(F32)]
    facts = jnp.zeros((rows, LANES), F32)
    for k, field in enumerate(fields):
        spot = iota((top, LANES), 1) == iota((top, LANES), 0) + k * top
        facts += lax.dot_general(
            field.astype(BF16),
            spot.astype(F32).astype(BF16),
            (((0,), (0,)), ((), ())),
            preferred_element_type=F32,
        )
    rows_ref[:, width:] = facts.astype(BF16)


def prepare(me, tokens, routes, gates, priority):
    rows, width = tokens.shape
    return pl.pallas_call(
        prepare_kernel,
        in_specs=[pl.BlockSpec(memory_space=pltpu.SMEM)] + [pl.BlockSpec(memory_space=pltpu.VMEM)] * 4,
        out_specs=pl.BlockSpec(memory_space=pltpu.VMEM),
        out_shape=jax.ShapeDtypeStruct((rows, width + LANES), BF16),
    )(me, tokens, routes.T, gates.T, priority.reshape(1, rows))


def weigh_kernel(top, tok_rows, me_ref, capacity_ref, *refs):
    fact_refs, out_ref, (all_ref, key_ref, row_ref) = refs[:-4], refs[-4], refs[-3:]
    total = all_ref.shape[0]
    at = 0
    for ref in fact_refs:
        rows, wide = ref.shape
        all_ref[at : at + rows, :] = ref[:, wide - LANES :]
        at += rows
    eye = iota((LANES, LANES), 0) == iota((LANES, LANES), 1)
    lane = iota((LANES, LANES), 1)
    tiles = total // LANES
    mine = tiles // 2
    experts = (me_ref[0], me_ref[0] + 1 - 2 * lax.rem(me_ref[0], 2))
    worth = jnp.where(lane == 4 * top, float(total), 0.0)
    worth = jnp.where(lane == 4 * top + 1, float(tok_rows), jnp.where(lane == 4 * top + 2, 1.0, worth))

    def read(i, _, own):
        facts = all_ref[pl.ds(pl.multiple_of(i * LANES, LANES), LANES), :].astype(F32)
        values = (
            pltpu.roll(facts, LANES - top, 1)
            + pltpu.roll(facts, LANES - 2 * top, 1)
            + pltpu.roll(facts, LANES - 3 * top, 1)
        )
        order = jnp.sum(facts * worth, axis=1, keepdims=True)
        for e, expert in enumerate(experts):
            named = (lane < top) & (facts == expert.astype(F32))
            gate = jnp.sum(jnp.where(named, values, 0.0), axis=1, keepdims=True)
            key = jnp.where(gate > 0.0, order, BIG)
            row_ref[e, pl.ds(i, 1), :] = jnp.sum(jnp.where(eye, key, 0.0), axis=0, keepdims=True)
            if own:
                key_ref[e, i] = jnp.broadcast_to(key, (LANES, LANES))
                held = pl.ds(pl.multiple_of((e * mine + i) * LANES, LANES), LANES)
                out_ref[held, :] = jnp.broadcast_to(gate, (LANES, LANES))
        return 0

    lax.fori_loop(0, mine, functools.partial(read, own=True), 0, unroll=min(mine, 4))
    lax.fori_loop(mine, tiles, functools.partial(read, own=False), 0, unroll=min(mine, 4))
    for e, expert in enumerate(experts):
        limit = capacity_ref[expert].astype(F32)

        def judge(i, _, e=e, limit=limit):
            held = pl.ds(pl.multiple_of((e * mine + i) * LANES, LANES), LANES)
            key = key_ref[e, i]

            def count(j, smaller):
                return smaller + (row_ref[e, pl.ds(j, 1), :] < key).astype(F32)

            smaller = lax.fori_loop(0, tiles, count, jnp.zeros((LANES, LANES), F32), unroll=min(tiles, 8))
            rank = jnp.sum(smaller, axis=1, keepdims=True)
            out_ref[held, :] = jnp.where(rank < limit, out_ref[held, :], 0.0)
            return 0

        lax.fori_loop(0, mine, judge, 0, unroll=min(mine, 4))


def weigh(me, capacity, facts, top, tok_rows):
    total = sum(f.shape[0] for f in facts)
    tiles = total // LANES
    return pl.pallas_call(
        functools.partial(weigh_kernel, top, tok_rows),
        in_specs=[pl.BlockSpec(memory_space=pltpu.SMEM)] * 2
        + [pl.BlockSpec(memory_space=pltpu.VMEM)] * len(facts),
        out_specs=pl.BlockSpec(memory_space=pltpu.VMEM),
        out_shape=jax.ShapeDtypeStruct((total, LANES), F32),
        scratch_shapes=[
            pltpu.VMEM((total, LANES), BF16),
            pltpu.VMEM((2, tiles // 2, LANES, LANES), F32),
            pltpu.VMEM((2, tiles, LANES), F32),
        ],
        compiler_params=pltpu.CompilerParams(vmem_limit_bytes=24 * MIB),
        cost_estimate=pl.CostEstimate(flops=1, bytes_accessed=1, transcendentals=0),
    )(me, capacity, *facts)


def pack_kernel(*refs):
    rows = refs[0].shape[0]
    for k, ref in enumerate(refs[:-1]):
        refs[-1][k * rows : (k + 1) * rows, :] = ref[...]


def pack(blocks):
    rows, wide = blocks[0].shape
    return pl.pallas_call(
        pack_kernel,
        in_specs=[pl.BlockSpec(memory_space=pltpu.VMEM)] * len(blocks),
        out_specs=pl.BlockSpec(memory_space=pltpu.VMEM),
        out_shape=jax.ShapeDtypeStruct((len(blocks) * rows, wide), BF16),
        compiler_params=pltpu.CompilerParams(vmem_limit_bytes=24 * MIB),
        cost_estimate=pl.CostEstimate(flops=1, bytes_accessed=1, transcendentals=0),
    )(*blocks)


def combine_kernel(rows, sums, weighted, *refs):
    ins, outs = refs[: -len(sums)], refs[-len(sums) :]
    width = outs[0].shape[1]
    for lanes in range(0, width, 256):
        for terms, out in zip(sums, outs):
            total = None
            for which, first, place in terms:
                value = ins[which][first : first + rows, lanes : lanes + 256].astype(F32)
                if place is not None:
                    value = value * ins[weighted][place : place + rows, :1]
                total = value if total is None else total + value
            out[:, lanes : lanes + 256] = total.astype(out.dtype)


def combine(arrays, weights, sums, kind=BF16):
    rows = weights.shape[0] // 16
    width = arrays[0].shape[1]
    sums = [[(a, b * rows, None if p is None else p * rows) for a, b, p in terms] for terms in sums]
    return pl.pallas_call(
        functools.partial(combine_kernel, rows, sums, len(arrays)),
        in_specs=[pl.BlockSpec(memory_space=pltpu.VMEM)] * (len(arrays) + 1),
        out_specs=[pl.BlockSpec(memory_space=pltpu.VMEM)] * len(sums),
        out_shape=[jax.ShapeDtypeStruct((rows, width), kind)] * len(sums),
        compiler_params=pltpu.CompilerParams(vmem_limit_bytes=24 * MIB),
        cost_estimate=pl.CostEstimate(flops=1, bytes_accessed=1, transcendentals=0),
    )(*arrays, weights)


def load_kernel(*refs):
    count = len(refs) // 2
    sems = refs[-1]
    copies = [pltpu.make_async_copy(refs[k], refs[count + k], sems.at[k]) for k in range(count)]
    for copy in copies:
        copy.start()
    for copy in copies:
        copy.wait()


def load(*arrays):
    size = sum(a.size * 2 for a in arrays)
    return pl.pallas_call(
        load_kernel,
        in_specs=[pl.BlockSpec(memory_space=pl.ANY)] * len(arrays),
        out_specs=[pl.BlockSpec(memory_space=pltpu.VMEM)] * len(arrays),
        out_shape=[jax.ShapeDtypeStruct(a.shape, a.dtype) for a in arrays],
        scratch_shapes=[pltpu.SemaphoreType.DMA((len(arrays),))],
        compiler_params=pltpu.CompilerParams(vmem_limit_bytes=size + 4 * MIB),
    )(*arrays)


FF_TILE, OUT_TILE = 256, 512


def expert_kernel(pieces, *refs):
    x_refs, (gate_ref, up_ref, down_ref) = refs[: -5 - pieces], refs[-5 - pieces : -2 - pieces]
    out_refs, (x, hidden) = refs[-2 - pieces : -2], refs[-2:]
    width, ff = x.shape[1], hidden.shape[1]
    at = 0
    for ref in x_refs:
        x[at : at + ref.shape[0], :] = ref[:, :width]
        at += ref.shape[0]
    for k in range(ff // FF_TILE):
        lanes = slice(k * FF_TILE, (k + 1) * FF_TILE)
        gated = jnp.dot(x[...], gate_ref[0, :, lanes], preferred_element_type=F32)
        upward = jnp.dot(x[...], up_ref[0, :, lanes], preferred_element_type=F32)
        hidden[:, lanes] = (gated / (1.0 + jnp.exp(-gated)) * upward).astype(BF16)
    for k in range(width // OUT_TILE):
        lanes = slice(k * OUT_TILE, (k + 1) * OUT_TILE)
        made = jnp.dot(hidden[...], down_ref[0, :, lanes], preferred_element_type=F32).astype(BF16)
        rows = made.shape[0] // pieces
        for k, out_ref in enumerate(out_refs):
            out_ref[:, lanes] = made[k * rows : (k + 1) * rows]


def expert(arrays, matrices, pieces=1):
    ff, width = matrices[2].shape[1:]
    rows = sum(a.shape[0] for a in arrays)
    held = rows * 2 * (width + ff) + 4 * rows * (2 * FF_TILE + OUT_TILE)
    made = pl.pallas_call(
        functools.partial(expert_kernel, pieces),
        in_specs=[pl.BlockSpec(memory_space=pltpu.VMEM)] * (len(arrays) + 3),
        out_specs=[pl.BlockSpec(memory_space=pltpu.VMEM)] * pieces,
        out_shape=[jax.ShapeDtypeStruct((rows // pieces, width), BF16)] * pieces,
        scratch_shapes=[pltpu.VMEM((rows, width), BF16), pltpu.VMEM((rows, ff), BF16)],
        compiler_params=pltpu.CompilerParams(vmem_limit_bytes=held + 20 * MIB),
        cost_estimate=pl.CostEstimate(flops=1, bytes_accessed=1, transcendentals=0),
    )(*arrays, *matrices)
    return made if pieces > 1 else made[0]


def orders(ep):
    bits = list(range(ep.bit_length() - 1))[::-1]
    return (bits, bits[:-2] + bits[:-3:-1])


def send(array, ep, flips):
    pairs = []
    for place in range(ep):
        for core, order in enumerate(orders(ep)):
            to = place
            for flip in flips:
                to ^= 1 << order[flip]
            pairs.append((2 * place + core, 2 * to + core))
    return lax.ppermute(array, ("ep", "sub"), pairs)


def cross(array):
    return lax.ppermute(array, "sub", [(0, 1), (1, 0)])


def add(*terms):
    return sum([t.astype(F32) for t in terms]).astype(BF16)


def on_device(ep, tokens, routes, gates, priority, capacity, w_gate, w_up, w_down):
    tok_rows, width = tokens.shape
    top = routes.shape[1]
    steps = ep.bit_length() - 1
    me = (lax.axis_index("ep") * 2 + lax.axis_index("sub")).astype(jnp.int32).reshape(1)
    held = prepare(me, tokens, routes, gates, priority)
    for step in range(steps - 3):
        held = jnp.concatenate([held, send(held, ep, [step])])
    base = held.shape[0]
    own1, own2, own4 = send(held, ep, [-3]), send(held, ep, [-2]), send(held, ep, [-1])
    first = cross(held)
    matrices = load(w_gate, w_up, w_down)
    own1, first, matrices = lax.optimization_barrier((own1, first, matrices))
    crossed = cross(pack([own1, own2, own4]))
    own3 = send(own1, ep, [-2])
    own5 = send(own1, ep, [-1])
    own6 = send(own2, ep, [-1])
    theirs = expert([first, crossed], matrices)
    own3, theirs = lax.optimization_barrier((own3, theirs))
    own7 = send(own3, ep, [-1])
    far_made = expert([own3, own5, own6], matrices)
    own3, own5, own6, own7, theirs, far_made = lax.optimization_barrier((own3, own5, own6, own7, theirs, far_made))
    far = [own5, own7, own3, own6]
    far_crossed = cross(pack(far))
    last_made = expert([own7], matrices)
    far_crossed, last_made = lax.optimization_barrier((far_crossed, last_made))
    first_back, last_back = expert([far_crossed], matrices, 2)
    first_back = cross(first_back)
    near = [held, own1, own2, own4]
    weights = weigh(me, capacity, near + far + [first, crossed, far_crossed], top, tok_rows)
    weights, theirs, last_back = lax.optimization_barrier((weights, theirs, last_back))
    last_back = cross(last_back)

    def part(mine, back, block, place):
        return [(mine, block, place), (back, block, 8 + place)]

    send5, send7 = combine(
        [far_made, last_made, first_back], weights, [[(0, 1, 4), (2, 0, 12)], [(1, 0, 5), (2, 1, 13)]]
    )
    back7 = send(send7, ep, [-1])
    back5 = send(send5, ep, [-1])
    send3, send6 = combine(
        [far_made, last_back, back7],
        weights,
        [[(0, 0, 6), (1, 0, 14), (2, 0, None)], [(0, 2, 7), (1, 1, 15)]],
    )
    back3 = send(send3, ep, [-2])
    near_made = expert(near, matrices)
    near_made, send6 = lax.optimization_barrier((near_made, send6))
    back6 = send(send6, ep, [-1])
    near_back = cross(theirs)
    (send4,) = combine([near_made, near_back], weights, [part(0, 1, 3, 3)])
    back4 = send(send4, ep, [-1])
    back3, back5, send4 = lax.optimization_barrier((back3, back5, send4))
    (send1,) = combine([near_made, near_back, back3, back5], weights, [part(0, 1, 1, 1) + [(2, 0, None), (3, 0, None)]])
    back1 = send(send1, ep, [-3])
    back6, send1 = lax.optimization_barrier((back6, send1))
    (send2,) = combine([near_made, near_back, back6], weights, [part(0, 1, 2, 2) + [(2, 0, None)]])
    back2 = send(send2, ep, [-2])
    (total,) = combine([near_made, near_back, back4], weights, [part(0, 1, 0, 0) + [(2, 0, None)]], F32)
    back1, total = lax.optimization_barrier((back1, total))
    (total,) = combine([total, back1], weights, [[(0, 0, None), (1, 0, None)]], F32)
    back2, total = lax.optimization_barrier((back2, total))
    (total,) = combine([total, back2], weights, [[(0, 0, None), (1, 0, None)]])
    for step in range(steps - 3)[::-1]:
        half = total.shape[0] // 2
        total = add(total[:half], send(total[half:], ep, [step]))
    return total


def solution(mesh):
    in_specs = (
        P(("groups", "ep", "sub"), None),
        P(("groups", "ep", "sub"), None),
        P(("groups", "ep", "sub"), None),
        P(("groups", "ep", "sub")),
        P(),
        P(("ep", "sub"), None, None),
        P(("ep", "sub"), None, None),
        P(("ep", "sub"), None, None),
    )
    out_specs = P(("groups", "ep", "sub"), None)
    return jax.shard_map(
        functools.partial(on_device, mesh.shape["ep"]),
        mesh=mesh,
        in_specs=in_specs,
        out_specs=out_specs,
        check_vma=False,
    )
```

```python
import functools

import jax
import jax.numpy as jnp
from jax import lax
from jax.experimental import pallas as pl
from jax.experimental.pallas import tpu as pltpu
from jax.sharding import PartitionSpec as P

F32 = jnp.float32
BF16 = jnp.bfloat16
LANES = 128
BIG = 1e9
MIB = 1024 * 1024


def iota(shape, dim):
    return lax.broadcasted_iota(jnp.int32, shape, dim)


def prepare_kernel(me_ref, tokens_ref, routes_ref, gates_ref, prio_ref, rows_ref):
    rows, width = tokens_ref.shape
    top = routes_ref.shape[0]
    for block in range(width // LANES):
        lanes = slice(block * LANES, (block + 1) * LANES)
        x = tokens_ref[:, lanes].astype(F32)
        largest = jnp.max(jnp.abs(x), axis=1, keepdims=True)
        scale = ((largest + 1e-06) / 448.0).astype(BF16).astype(F32)
        quantized = (x / scale).astype(BF16)
        rows_ref[:, lanes] = (quantized.astype(F32) * scale).astype(BF16)
    gates = gates_ref[...]
    high = gates.astype(BF16)
    middle = (gates - high.astype(F32)).astype(BF16)
    low = (gates - high.astype(F32) - middle.astype(F32)).astype(BF16)
    place, token = iota((top, rows), 0), iota((top, rows), 1)
    other = jnp.where(place == 0, prio_ref[...], jnp.where(place == 1, me_ref[0], token))
    fields = [routes_ref[...].astype(F32), high.astype(F32), middle.astype(F32), low.astype(F32), other.astype(F32)]
    stacked = jnp.concatenate(fields, axis=0)
    place = iota((stacked.shape[0], LANES), 0) == iota((stacked.shape[0], LANES), 1)
    facts = lax.dot_general(
        stacked.astype(BF16), place.astype(F32).astype(BF16), (((0,), (0,)), ((), ())), preferred_element_type=F32
    )
    rows_ref[:, width:] = facts.astype(BF16)


def prepare(me, tokens, routes, gates, priority):
    rows, width = tokens.shape
    return pl.pallas_call(
        prepare_kernel,
        in_specs=[pl.BlockSpec(memory_space=pltpu.SMEM)] + [pl.BlockSpec(memory_space=pltpu.VMEM)] * 4,
        out_specs=pl.BlockSpec(memory_space=pltpu.VMEM),
        out_shape=jax.ShapeDtypeStruct((rows, width + LANES), BF16),
    )(me, tokens, routes.T, gates.T, priority.reshape(1, rows))


def weigh_kernel(top, tok_rows, me_ref, capacity_ref, *refs):
    fact_refs, out_ref, (all_ref, key_ref, row_ref) = refs[:-4], refs[-4], refs[-3:]
    total = all_ref.shape[0]
    at = 0
    for ref in fact_refs:
        rows, wide = ref.shape
        all_ref[at : at + rows, :] = ref[:, wide - LANES :]
        at += rows
    eye = iota((LANES, LANES), 0) == iota((LANES, LANES), 1)
    lane = iota((LANES, LANES), 1)
    tiles = total // LANES
    mine = tiles // 2
    experts = (me_ref[0], me_ref[0] + 1 - 2 * lax.rem(me_ref[0], 2))
    worth = jnp.where(lane == 4 * top, float(total), 0.0)
    worth = jnp.where(lane == 4 * top + 1, float(tok_rows), jnp.where(lane == 4 * top + 2, 1.0, worth))

    def read(i, _, own):
        facts = all_ref[pl.ds(pl.multiple_of(i * LANES, LANES), LANES), :].astype(F32)
        values = (
            pltpu.roll(facts, LANES - top, 1)
            + pltpu.roll(facts, LANES - 2 * top, 1)
            + pltpu.roll(facts, LANES - 3 * top, 1)
        )
        order = jnp.sum(facts * worth, axis=1, keepdims=True)
        for e, expert in enumerate(experts):
            named = (lane < top) & (facts == expert.astype(F32))
            gate = jnp.sum(jnp.where(named, values, 0.0), axis=1, keepdims=True)
            key = jnp.where(gate > 0.0, order, BIG)
            row_ref[e, pl.ds(i, 1), :] = jnp.sum(jnp.where(eye, key, 0.0), axis=0, keepdims=True)
            if own:
                key_ref[e, i] = jnp.broadcast_to(key, (LANES, LANES))
                held = pl.ds(pl.multiple_of((e * mine + i) * LANES, LANES), LANES)
                out_ref[held, :] = jnp.broadcast_to(gate, (LANES, LANES))
        return 0

    lax.fori_loop(0, mine, functools.partial(read, own=True), 0, unroll=min(mine, 4))
    lax.fori_loop(mine, tiles, functools.partial(read, own=False), 0, unroll=min(mine, 4))
    for e, expert in enumerate(experts):
        limit = capacity_ref[expert].astype(F32)

        def judge(i, _, e=e, limit=limit):
            held = pl.ds(pl.multiple_of((e * mine + i) * LANES, LANES), LANES)
            key = key_ref[e, i]

            def count(j, smaller):
                return smaller + (row_ref[e, pl.ds(j, 1), :] < key).astype(F32)

            smaller = lax.fori_loop(0, tiles, count, jnp.zeros((LANES, LANES), F32), unroll=min(tiles, 8))
            rank = jnp.sum(smaller, axis=1, keepdims=True)
            out_ref[held, :] = jnp.where(rank < limit, out_ref[held, :], 0.0)
            return 0

        lax.fori_loop(0, mine, judge, 0, unroll=min(mine, 4))


def weigh(me, capacity, facts, top, tok_rows):
    total = sum(f.shape[0] for f in facts)
    tiles = total // LANES
    return pl.pallas_call(
        functools.partial(weigh_kernel, top, tok_rows),
        in_specs=[pl.BlockSpec(memory_space=pltpu.SMEM)] * 2
        + [pl.BlockSpec(memory_space=pltpu.VMEM)] * len(facts),
        out_specs=pl.BlockSpec(memory_space=pltpu.VMEM),
        out_shape=jax.ShapeDtypeStruct((total, LANES), F32),
        scratch_shapes=[
            pltpu.VMEM((total, LANES), BF16),
            pltpu.VMEM((2, tiles // 2, LANES, LANES), F32),
            pltpu.VMEM((2, tiles, LANES), F32),
        ],
        compiler_params=pltpu.CompilerParams(vmem_limit_bytes=24 * MIB),
        cost_estimate=pl.CostEstimate(flops=1, bytes_accessed=1, transcendentals=0),
    )(me, capacity, *facts)


def pack_kernel(*refs):
    rows = refs[0].shape[0]
    for k, ref in enumerate(refs[:-1]):
        refs[-1][k * rows : (k + 1) * rows, :] = ref[...]


def pack(blocks):
    rows, wide = blocks[0].shape
    return pl.pallas_call(
        pack_kernel,
        in_specs=[pl.BlockSpec(memory_space=pltpu.VMEM)] * len(blocks),
        out_specs=pl.BlockSpec(memory_space=pltpu.VMEM),
        out_shape=jax.ShapeDtypeStruct((len(blocks) * rows, wide), BF16),
        compiler_params=pltpu.CompilerParams(vmem_limit_bytes=24 * MIB),
        cost_estimate=pl.CostEstimate(flops=1, bytes_accessed=1, transcendentals=0),
    )(*blocks)


def combine_kernel(rows, sums, weighted, *refs):
    ins, outs = refs[: -len(sums)], refs[-len(sums) :]
    width = outs[0].shape[1]
    for lanes in range(0, width, 256):
        for terms, out in zip(sums, outs):
            total = None
            for which, first, place in terms:
                value = ins[which][first : first + rows, lanes : lanes + 256].astype(F32)
                if place is not None:
                    value = value * ins[weighted][place : place + rows, :1]
                total = value if total is None else total + value
            out[:, lanes : lanes + 256] = total.astype(out.dtype)


def combine(arrays, weights, sums, kind=BF16):
    rows = weights.shape[0] // 16
    width = arrays[0].shape[1]
    sums = [[(a, b * rows, None if p is None else p * rows) for a, b, p in terms] for terms in sums]
    return pl.pallas_call(
        functools.partial(combine_kernel, rows, sums, len(arrays)),
        in_specs=[pl.BlockSpec(memory_space=pltpu.VMEM)] * (len(arrays) + 1),
        out_specs=[pl.BlockSpec(memory_space=pltpu.VMEM)] * len(sums),
        out_shape=[jax.ShapeDtypeStruct((rows, width), kind)] * len(sums),
        compiler_params=pltpu.CompilerParams(vmem_limit_bytes=24 * MIB),
        cost_estimate=pl.CostEstimate(flops=1, bytes_accessed=1, transcendentals=0),
    )(*arrays, weights)


def load_kernel(*refs):
    count = len(refs) // 2
    sems = refs[-1]
    copies = [pltpu.make_async_copy(refs[k], refs[count + k], sems.at[k]) for k in range(count)]
    for copy in copies:
        copy.start()
    for copy in copies:
        copy.wait()


def load(*arrays):
    size = sum(a.size * 2 for a in arrays)
    return pl.pallas_call(
        load_kernel,
        in_specs=[pl.BlockSpec(memory_space=pl.ANY)] * len(arrays),
        out_specs=[pl.BlockSpec(memory_space=pltpu.VMEM)] * len(arrays),
        out_shape=[jax.ShapeDtypeStruct(a.shape, a.dtype) for a in arrays],
        scratch_shapes=[pltpu.SemaphoreType.DMA((len(arrays),))],
        compiler_params=pltpu.CompilerParams(vmem_limit_bytes=size + 4 * MIB),
    )(*arrays)


FF_TILE, OUT_TILE = 256, 512


def expert_kernel(pieces, *refs):
    x_refs, (gate_ref, up_ref, down_ref) = refs[: -5 - pieces], refs[-5 - pieces : -2 - pieces]
    out_refs, (x, hidden) = refs[-2 - pieces : -2], refs[-2:]
    width, ff = x.shape[1], hidden.shape[1]
    at = 0
    for ref in x_refs:
        x[at : at + ref.shape[0], :] = ref[:, :width]
        at += ref.shape[0]
    for k in range(ff // FF_TILE):
        lanes = slice(k * FF_TILE, (k + 1) * FF_TILE)
        gated = jnp.dot(x[...], gate_ref[0, :, lanes], preferred_element_type=F32)
        upward = jnp.dot(x[...], up_ref[0, :, lanes], preferred_element_type=F32)
        hidden[:, lanes] = (gated / (1.0 + jnp.exp(-gated)) * upward).astype(BF16)
    for k in range(width // OUT_TILE):
        lanes = slice(k * OUT_TILE, (k + 1) * OUT_TILE)
        made = jnp.dot(hidden[...], down_ref[0, :, lanes], preferred_element_type=F32).astype(BF16)
        rows = made.shape[0] // pieces
        for k, out_ref in enumerate(out_refs):
            out_ref[:, lanes] = made[k * rows : (k + 1) * rows]


def expert(arrays, matrices, pieces=1, flops=1):
    ff, width = matrices[2].shape[1:]
    rows = sum(a.shape[0] for a in arrays)
    held = rows * 2 * (width + ff) + 4 * rows * (2 * FF_TILE + OUT_TILE)
    made = pl.pallas_call(
        functools.partial(expert_kernel, pieces),
        in_specs=[pl.BlockSpec(memory_space=pltpu.VMEM)] * (len(arrays) + 3),
        out_specs=[pl.BlockSpec(memory_space=pltpu.VMEM)] * pieces,
        out_shape=[jax.ShapeDtypeStruct((rows // pieces, width), BF16)] * pieces,
        scratch_shapes=[pltpu.VMEM((rows, width), BF16), pltpu.VMEM((rows, ff), BF16)],
        compiler_params=pltpu.CompilerParams(vmem_limit_bytes=held + 20 * MIB),
        cost_estimate=pl.CostEstimate(flops=flops, bytes_accessed=1, transcendentals=0),
    )(*arrays, *matrices)
    return made if pieces > 1 else made[0]


def orders(ep):
    bits = list(range(ep.bit_length() - 1))[::-1]
    return (bits, bits[:-2] + bits[:-3:-1])


def send(array, ep, flips):
    pairs = []
    for place in range(ep):
        for core, order in enumerate(orders(ep)):
            to = place
            for flip in flips:
                to ^= 1 << order[flip]
            pairs.append((2 * place + core, 2 * to + core))
    return lax.ppermute(array, ("ep", "sub"), pairs)


def cross(array):
    return lax.ppermute(array, "sub", [(0, 1), (1, 0)])


def add(*terms):
    return sum([t.astype(F32) for t in terms]).astype(BF16)


def on_device(ep, tokens, routes, gates, priority, capacity, w_gate, w_up, w_down):
    tok_rows, width = tokens.shape
    top = routes.shape[1]
    steps = ep.bit_length() - 1
    me = (lax.axis_index("ep") * 2 + lax.axis_index("sub")).astype(jnp.int32).reshape(1)
    held = prepare(me, tokens, routes, gates, priority)
    for step in range(steps - 3):
        held = jnp.concatenate([held, send(held, ep, [step])])
    base = held.shape[0]
    own1, own2, own4 = send(held, ep, [-3]), send(held, ep, [-2]), send(held, ep, [-1])
    first = cross(held)
    matrices = load(w_gate, w_up, w_down)
    own1, first, matrices = lax.optimization_barrier((own1, first, matrices))
    crossed = cross(pack([own1, own2, own4]))
    own3 = send(own1, ep, [-2])
    own5 = send(own1, ep, [-1])
    own6 = send(own2, ep, [-1])
    theirs = expert([first, crossed], matrices)
    own3, theirs = lax.optimization_barrier((own3, theirs))
    own7 = send(own3, ep, [-1])
    far_crossed = [cross(o) for o in (own3, own6, own5)]
    far_made = expert([own3, own5, own6], matrices)
    own3, own5, own6, own7, theirs, far_made = lax.optimization_barrier((own3, own5, own6, own7, theirs, far_made))
    far = [own5, own7, own3, own6]
    last_crossed = cross(own7)
    last_made = expert([own7], matrices)
    far_crossed, last_crossed, last_made = lax.optimization_barrier((far_crossed, last_crossed, last_made))
    last_back, first_back = expert([*far_crossed, last_crossed], matrices, 2)
    first_back = cross(first_back)
    near = [held, own1, own2, own4]
    weights = weigh(me, capacity, near + far + [first, crossed, *far_crossed, last_crossed], top, tok_rows)
    weights, theirs, last_back = lax.optimization_barrier((weights, theirs, last_back))
    last_back = cross(last_back)

    def part(mine, back, block, place):
        return [(mine, block, place), (back, block, 8 + place)]

    send5, send7 = combine(
        [far_made, last_made, first_back], weights, [[(0, 1, 4), (2, 0, 12)], [(1, 0, 5), (2, 1, 13)]]
    )
    back7 = send(send7, ep, [-1])
    back5 = send(send5, ep, [-1])
    send3, send6 = combine(
        [far_made, last_back, back7],
        weights,
        [[(0, 0, 6), (1, 0, 14), (2, 0, None)], [(0, 2, 7), (1, 1, 15)]],
    )
    back3 = send(send3, ep, [-2])
    near_made = expert(near, matrices)
    near_made, send6 = lax.optimization_barrier((near_made, send6))
    back6 = send(send6, ep, [-1])
    near_back = cross(theirs)
    (send4,) = combine([near_made, near_back], weights, [part(0, 1, 3, 3)])
    back4 = send(send4, ep, [-1])
    back3, back5, send4 = lax.optimization_barrier((back3, back5, send4))
    (send1,) = combine([near_made, near_back, back3, back5], weights, [part(0, 1, 1, 1) + [(2, 0, None), (3, 0, None)]])
    back1 = send(send1, ep, [-3])
    back6, send1 = lax.optimization_barrier((back6, send1))
    (send2,) = combine([near_made, near_back, back6], weights, [part(0, 1, 2, 2) + [(2, 0, None)]])
    back2 = send(send2, ep, [-2])
    (total,) = combine([near_made, near_back, back4], weights, [part(0, 1, 0, 0) + [(2, 0, None)]], F32)
    back1, total = lax.optimization_barrier((back1, total))
    (total,) = combine([total, back1], weights, [[(0, 0, None), (1, 0, None)]], F32)
    back2, total = lax.optimization_barrier((back2, total))
    (total,) = combine([total, back2], weights, [[(0, 0, None), (1, 0, None)]])
    for step in range(steps - 3)[::-1]:
        half = total.shape[0] // 2
        total = add(total[:half], send(total[half:], ep, [step]))
    return total


def solution(mesh):
    in_specs = (
        P(("groups", "ep", "sub"), None),
        P(("groups", "ep", "sub"), None),
        P(("groups", "ep", "sub"), None),
        P(("groups", "ep", "sub")),
        P(),
        P(("ep", "sub"), None, None),
        P(("ep", "sub"), None, None),
        P(("ep", "sub"), None, None),
    )
    out_specs = P(("groups", "ep", "sub"), None)
    return jax.shard_map(
        functools.partial(on_device, mesh.shape["ep"]),
        mesh=mesh,
        in_specs=in_specs,
        out_specs=out_specs,
        check_vma=False,
    )
```

```python
import functools

import jax
import jax.numpy as jnp
from jax import lax
from jax.experimental import pallas as pl
from jax.experimental.pallas import tpu as pltpu
from jax.sharding import PartitionSpec as P

F32 = jnp.float32
BF16 = jnp.bfloat16
LANES = 128
BIG = 1e9
MIB = 1024 * 1024


def iota(shape, dim):
    return lax.broadcasted_iota(jnp.int32, shape, dim)


def prepare_kernel(me_ref, tokens_ref, routes_ref, gates_ref, prio_ref, rows_ref):
    rows, width = tokens_ref.shape
    top = routes_ref.shape[0]
    for block in range(width // LANES):
        lanes = slice(block * LANES, (block + 1) * LANES)
        x = tokens_ref[:, lanes].astype(F32)
        largest = jnp.max(jnp.abs(x), axis=1, keepdims=True)
        scale = ((largest + 1e-06) / 448.0).astype(BF16).astype(F32)
        quantized = (x / scale).astype(BF16)
        rows_ref[:, lanes] = (quantized.astype(F32) * scale).astype(BF16)
    gates = gates_ref[...]
    high = gates.astype(BF16)
    middle = (gates - high.astype(F32)).astype(BF16)
    low = (gates - high.astype(F32) - middle.astype(F32)).astype(BF16)
    place, token = iota((top, rows), 0), iota((top, rows), 1)
    other = jnp.where(place == 0, prio_ref[...], jnp.where(place == 1, me_ref[0], token))
    fields = [routes_ref[...].astype(F32), high.astype(F32), middle.astype(F32), low.astype(F32), other.astype(F32)]
    stacked = jnp.concatenate(fields, axis=0)
    place = iota((stacked.shape[0], LANES), 0) == iota((stacked.shape[0], LANES), 1)
    facts = lax.dot_general(
        stacked.astype(BF16), place.astype(F32).astype(BF16), (((0,), (0,)), ((), ())), preferred_element_type=F32
    )
    rows_ref[:, width:] = facts.astype(BF16)


def prepare(me, tokens, routes, gates, priority):
    rows, width = tokens.shape
    return pl.pallas_call(
        prepare_kernel,
        in_specs=[pl.BlockSpec(memory_space=pltpu.SMEM)] + [pl.BlockSpec(memory_space=pltpu.VMEM)] * 4,
        out_specs=pl.BlockSpec(memory_space=pltpu.VMEM),
        out_shape=jax.ShapeDtypeStruct((rows, width + LANES), BF16),
    )(me, tokens, routes.T, gates.T, priority.reshape(1, rows))


def weigh_kernel(top, tok_rows, me_ref, capacity_ref, *refs):
    fact_refs, out_ref, (all_ref, key_ref, row_ref) = refs[:-4], refs[-4], refs[-3:]
    total = all_ref.shape[0]
    at = 0
    for ref in fact_refs:
        rows, wide = ref.shape
        all_ref[at : at + rows, :] = ref[:, wide - LANES :]
        at += rows
    eye = iota((LANES, LANES), 0) == iota((LANES, LANES), 1)
    lane = iota((LANES, LANES), 1)
    tiles = total // LANES
    mine = tiles // 2
    experts = (me_ref[0], me_ref[0] + 1 - 2 * lax.rem(me_ref[0], 2))
    worth = jnp.where(lane == 4 * top, float(total), 0.0)
    worth = jnp.where(lane == 4 * top + 1, float(tok_rows), jnp.where(lane == 4 * top + 2, 1.0, worth))

    def read(i, _, own):
        facts = all_ref[pl.ds(pl.multiple_of(i * LANES, LANES), LANES), :].astype(F32)
        values = (
            pltpu.roll(facts, LANES - top, 1)
            + pltpu.roll(facts, LANES - 2 * top, 1)
            + pltpu.roll(facts, LANES - 3 * top, 1)
        )
        order = jnp.sum(facts * worth, axis=1, keepdims=True)
        for e, expert in enumerate(experts):
            named = (lane < top) & (facts == expert.astype(F32))
            gate = jnp.sum(jnp.where(named, values, 0.0), axis=1, keepdims=True)
            key = jnp.where(gate > 0.0, order, BIG)
            row_ref[e, pl.ds(i, 1), :] = jnp.sum(jnp.where(eye, key, 0.0), axis=0, keepdims=True)
            if own:
                key_ref[e, i] = jnp.broadcast_to(key, (LANES, LANES))
                held = pl.ds(pl.multiple_of((e * mine + i) * LANES, LANES), LANES)
                out_ref[held, :] = jnp.broadcast_to(gate, (LANES, LANES))
        return 0

    lax.fori_loop(0, mine, functools.partial(read, own=True), 0, unroll=min(mine, 4))
    lax.fori_loop(mine, tiles, functools.partial(read, own=False), 0, unroll=min(mine, 4))
    for e, expert in enumerate(experts):
        limit = capacity_ref[expert].astype(F32)

        def judge(i, _, e=e, limit=limit):
            held = pl.ds(pl.multiple_of((e * mine + i) * LANES, LANES), LANES)
            key = key_ref[e, i]

            def count(j, smaller):
                return smaller + (row_ref[e, pl.ds(j, 1), :] < key).astype(F32)

            smaller = lax.fori_loop(0, tiles, count, jnp.zeros((LANES, LANES), F32), unroll=min(tiles, 8))
            rank = jnp.sum(smaller, axis=1, keepdims=True)
            out_ref[held, :] = jnp.where(rank < limit, out_ref[held, :], 0.0)
            return 0

        lax.fori_loop(0, mine, judge, 0, unroll=min(mine, 4))


def weigh(me, capacity, facts, top, tok_rows):
    total = sum(f.shape[0] for f in facts)
    tiles = total // LANES
    return pl.pallas_call(
        functools.partial(weigh_kernel, top, tok_rows),
        in_specs=[pl.BlockSpec(memory_space=pltpu.SMEM)] * 2
        + [pl.BlockSpec(memory_space=pltpu.VMEM)] * len(facts),
        out_specs=pl.BlockSpec(memory_space=pltpu.VMEM),
        out_shape=jax.ShapeDtypeStruct((total, LANES), F32),
        scratch_shapes=[
            pltpu.VMEM((total, LANES), BF16),
            pltpu.VMEM((2, tiles // 2, LANES, LANES), F32),
            pltpu.VMEM((2, tiles, LANES), F32),
        ],
        compiler_params=pltpu.CompilerParams(vmem_limit_bytes=24 * MIB),
        cost_estimate=pl.CostEstimate(flops=1, bytes_accessed=1, transcendentals=0),
    )(me, capacity, *facts)


def pack_kernel(*refs):
    rows = refs[0].shape[0]
    for k, ref in enumerate(refs[:-1]):
        refs[-1][k * rows : (k + 1) * rows, :] = ref[...]


def pack(blocks):
    rows, wide = blocks[0].shape
    return pl.pallas_call(
        pack_kernel,
        in_specs=[pl.BlockSpec(memory_space=pltpu.VMEM)] * len(blocks),
        out_specs=pl.BlockSpec(memory_space=pltpu.VMEM),
        out_shape=jax.ShapeDtypeStruct((len(blocks) * rows, wide), BF16),
        compiler_params=pltpu.CompilerParams(vmem_limit_bytes=24 * MIB),
        cost_estimate=pl.CostEstimate(flops=1, bytes_accessed=1, transcendentals=0),
    )(*blocks)


def combine_kernel(rows, sums, spans, offsets, weighted, *refs):
    ins, outs = refs[: -len(sums)], refs[-len(sums) :]
    for terms, (start, size), out in zip(sums, spans, outs):
        for lane in range(start, start + size, 256):
            total = None
            for which, first, place in terms:
                at = lane - offsets[which]
                value = ins[which][first : first + rows, at : at + 256].astype(F32)
                if place is not None:
                    value = value * ins[weighted][place : place + rows, :1]
                total = value if total is None else total + value
            out[:, lane - start : lane - start + 256] = total.astype(out.dtype)


def combine(arrays, weights, sums, kind=BF16, spans=None, offsets=None):
    rows = weights.shape[0] // 16
    spans = spans or [(0, arrays[0].shape[1])] * len(sums)
    offsets = offsets or [0] * len(arrays)
    sums = [[(a, b * rows, None if p is None else p * rows) for a, b, p in terms] for terms in sums]
    return pl.pallas_call(
        functools.partial(combine_kernel, rows, sums, spans, offsets, len(arrays)),
        in_specs=[pl.BlockSpec(memory_space=pltpu.VMEM)] * (len(arrays) + 1),
        out_specs=[pl.BlockSpec(memory_space=pltpu.VMEM)] * len(sums),
        out_shape=[jax.ShapeDtypeStruct((rows, size), kind) for start, size in spans],
        compiler_params=pltpu.CompilerParams(vmem_limit_bytes=24 * MIB),
        cost_estimate=pl.CostEstimate(flops=1, bytes_accessed=1, transcendentals=0),
    )(*arrays, weights)


def merge_kernel(low_ref, high_ref, low_last_ref, high_last_ref, out_ref):
    half = low_ref.shape[1]
    for ref, last, first in ((low_ref, low_last_ref, 0), (high_ref, high_last_ref, half)):
        for lane in range(0, half, 256):
            lanes = slice(lane, lane + 256)
            out_ref[:, first + lane : first + lane + 256] = (ref[:, lanes] + last[:, lanes].astype(F32)).astype(BF16)


def merge(halves, last):
    rows, half = last[0].shape
    return pl.pallas_call(
        merge_kernel,
        in_specs=[pl.BlockSpec(memory_space=pltpu.VMEM)] * 4,
        out_specs=pl.BlockSpec(memory_space=pltpu.VMEM),
        out_shape=jax.ShapeDtypeStruct((rows, 2 * half), BF16),
        compiler_params=pltpu.CompilerParams(vmem_limit_bytes=24 * MIB),
        cost_estimate=pl.CostEstimate(flops=1, bytes_accessed=1, transcendentals=0),
    )(*halves, *last)


def load_kernel(*refs):
    count = len(refs) // 2
    sems = refs[-1]
    copies = [pltpu.make_async_copy(refs[k], refs[count + k], sems.at[k]) for k in range(count)]
    for copy in copies:
        copy.start()
    for copy in copies:
        copy.wait()


def load(*arrays):
    size = sum(a.size * 2 for a in arrays)
    return pl.pallas_call(
        load_kernel,
        in_specs=[pl.BlockSpec(memory_space=pl.ANY)] * len(arrays),
        out_specs=[pl.BlockSpec(memory_space=pltpu.VMEM)] * len(arrays),
        out_shape=[jax.ShapeDtypeStruct(a.shape, a.dtype) for a in arrays],
        scratch_shapes=[pltpu.SemaphoreType.DMA((len(arrays),))],
        compiler_params=pltpu.CompilerParams(vmem_limit_bytes=size + 4 * MIB),
    )(*arrays)


FF_TILE, OUT_TILE = 256, 512


def expert_kernel(pieces, *refs):
    x_refs, (gate_ref, up_ref, down_ref) = refs[: -5 - pieces], refs[-5 - pieces : -2 - pieces]
    out_refs, (x, hidden) = refs[-2 - pieces : -2], refs[-2:]
    width, ff = x.shape[1], hidden.shape[1]
    at = 0
    for ref in x_refs:
        x[at : at + ref.shape[0], :] = ref[:, :width]
        at += ref.shape[0]
    for k in range(ff // FF_TILE):
        lanes = slice(k * FF_TILE, (k + 1) * FF_TILE)
        gated = jnp.dot(x[...], gate_ref[0, :, lanes], preferred_element_type=F32)
        upward = jnp.dot(x[...], up_ref[0, :, lanes], preferred_element_type=F32)
        hidden[:, lanes] = (gated / (1.0 + jnp.exp(-gated)) * upward).astype(BF16)
    for k in range(width // OUT_TILE):
        lanes = slice(k * OUT_TILE, (k + 1) * OUT_TILE)
        made = jnp.dot(hidden[...], down_ref[0, :, lanes], preferred_element_type=F32).astype(BF16)
        rows = made.shape[0] // pieces
        for k, out_ref in enumerate(out_refs):
            out_ref[:, lanes] = made[k * rows : (k + 1) * rows]


def expert(arrays, matrices, pieces=1, flops=1):
    ff, width = matrices[2].shape[1:]
    rows = sum(a.shape[0] for a in arrays)
    held = rows * 2 * (width + ff) + 4 * rows * (2 * FF_TILE + OUT_TILE)
    made = pl.pallas_call(
        functools.partial(expert_kernel, pieces),
        in_specs=[pl.BlockSpec(memory_space=pltpu.VMEM)] * (len(arrays) + 3),
        out_specs=[pl.BlockSpec(memory_space=pltpu.VMEM)] * pieces,
        out_shape=[jax.ShapeDtypeStruct((rows // pieces, width), BF16)] * pieces,
        scratch_shapes=[pltpu.VMEM((rows, width), BF16), pltpu.VMEM((rows, ff), BF16)],
        compiler_params=pltpu.CompilerParams(vmem_limit_bytes=held + 20 * MIB),
        cost_estimate=pl.CostEstimate(flops=flops, bytes_accessed=1, transcendentals=0),
    )(*arrays, *matrices)
    return made if pieces > 1 else made[0]


def orders(ep):
    bits = list(range(ep.bit_length() - 1))[::-1]
    return (bits, bits[:-2] + bits[:-3:-1])


def send(array, ep, flips):
    pairs = []
    for place in range(ep):
        for core, order in enumerate(orders(ep)):
            to = place
            for flip in flips:
                to ^= 1 << order[flip]
            pairs.append((2 * place + core, 2 * to + core))
    return lax.ppermute(array, ("ep", "sub"), pairs)


def cross(array):
    return lax.ppermute(array, "sub", [(0, 1), (1, 0)])


def add(*terms):
    return sum([t.astype(F32) for t in terms]).astype(BF16)


def on_device(ep, tokens, routes, gates, priority, capacity, w_gate, w_up, w_down):
    tok_rows, width = tokens.shape
    top = routes.shape[1]
    steps = ep.bit_length() - 1
    me = (lax.axis_index("ep") * 2 + lax.axis_index("sub")).astype(jnp.int32).reshape(1)
    held = prepare(me, tokens, routes, gates, priority)
    for step in range(steps - 3):
        held = jnp.concatenate([held, send(held, ep, [step])])
    base = held.shape[0]
    own1, own2, own4 = send(held, ep, [-3]), send(held, ep, [-2]), send(held, ep, [-1])
    first = cross(held)
    matrices = load(w_gate, w_up, w_down)
    own1, first, matrices = lax.optimization_barrier((own1, first, matrices))
    crossed = cross(pack([own1, own2, own4]))
    own3 = send(own1, ep, [-2])
    own5 = send(own1, ep, [-1])
    own6 = send(own2, ep, [-1])
    theirs = expert([first, crossed], matrices)
    own3, theirs = lax.optimization_barrier((own3, theirs))
    own7 = send(own3, ep, [-1])
    far_crossed = [cross(o) for o in (own3, own6, own5)]
    far_made = expert([own3, own5, own6], matrices)
    own3, own5, own6, own7, theirs, far_made = lax.optimization_barrier((own3, own5, own6, own7, theirs, far_made))
    far = [own5, own7, own3, own6]
    last_crossed = cross(own7)
    last_made = expert([own7], matrices)
    far_crossed, last_crossed, last_made = lax.optimization_barrier((far_crossed, last_crossed, last_made))
    last_back, first_back = expert([*far_crossed, last_crossed], matrices, 2)
    first_back = cross(first_back)
    near = [held, own1, own2, own4]
    weights = weigh(me, capacity, near + far + [first, crossed, *far_crossed, last_crossed], top, tok_rows)
    weights, theirs, last_back = lax.optimization_barrier((weights, theirs, last_back))
    last_back = cross(last_back)

    def part(mine, back, block, place):
        return [(mine, block, place), (back, block, 8 + place)]

    half = width // 2
    spans = [(0, half), (half, half)]
    sends = combine(
        [far_made, last_made, first_back],
        weights,
        [[(1, 0, 5), (2, 1, 13)]] * 2 + [[(0, 1, 4), (2, 0, 12)]] * 2,
        spans=spans * 2,
    )
    back7 = [send(s, ep, [-1]) for s in sends[:2]]
    back5 = [send(s, ep, [-1]) for s in sends[2:]]
    near_made = expert(near, matrices)
    near_made, back7[0] = lax.optimization_barrier((near_made, back7[0]))
    back3 = []
    for k, span in enumerate(spans):
        (send3,) = combine(
            [far_made, last_back, back7[k]],
            weights,
            [[(0, 0, 6), (1, 0, 14), (2, 0, None)]],
            spans=[span],
            offsets=[0, 0, span[0]],
        )
        back3.append(send(send3, ep, [-2]))
        if k == 0:
            back7[1], send3 = lax.optimization_barrier((back7[1], send3))
    send3, last_back = lax.optimization_barrier((send3, last_back))
    send6 = combine([far_made, last_back], weights, [[(0, 2, 7), (1, 1, 15)]] * 2, spans=spans)
    back6 = [send(s, ep, [-1]) for s in send6]
    near_back = cross(theirs)
    (send4,) = combine([near_made, near_back], weights, [part(0, 1, 3, 3)])
    back4 = send(send4, ep, [-1])
    back1 = []
    for k, span in enumerate(spans):
        (send1,) = combine(
            [near_made, near_back, back3[k], back5[k]],
            weights,
            [part(0, 1, 1, 1) + [(2, 0, None), (3, 0, None)]],
            spans=[span],
            offsets=[0, 0, span[0], span[0]],
        )
        back1.append(send(send1, ep, [-3]))
        if k == 0:
            back3[1], send1 = lax.optimization_barrier((back3[1], send1))
    back6, send1 = lax.optimization_barrier((back6, send1))
    send2 = combine(
        [near_made, near_back, *back6],
        weights,
        [part(0, 1, 2, 2) + [(2, 0, None)], part(0, 1, 2, 2) + [(3, 0, None)]],
        spans=spans,
        offsets=[0, 0, 0, half],
    )
    back2 = [send(s, ep, [-2]) for s in send2]
    (total,) = combine([near_made, near_back, back4], weights, [part(0, 1, 0, 0) + [(2, 0, None)]], F32)
    halves = []
    for k, span in enumerate(spans):
        back1[k], total = lax.optimization_barrier((back1[k], total))
        (sums,) = combine(
            [total, back1[k]], weights, [[(0, 0, None), (1, 0, None)]], F32, spans=[span], offsets=[0, span[0]]
        )
        halves.append(sums)
        if k == 0:
            total, sums = lax.optimization_barrier((total, sums))
    back2, halves = lax.optimization_barrier((back2, halves))
    total = merge(halves, back2)
    for step in range(steps - 3)[::-1]:
        count = total.shape[0] // 2
        total = add(total[:count], send(total[count:], ep, [step]))
    return total


def solution(mesh):
    in_specs = (
        P(("groups", "ep", "sub"), None),
        P(("groups", "ep", "sub"), None),
        P(("groups", "ep", "sub"), None),
        P(("groups", "ep", "sub")),
        P(),
        P(("ep", "sub"), None, None),
        P(("ep", "sub"), None, None),
        P(("ep", "sub"), None, None),
    )
    out_specs = P(("groups", "ep", "sub"), None)
    return jax.shard_map(
        functools.partial(on_device, mesh.shape["ep"]),
        mesh=mesh,
        in_specs=in_specs,
        out_specs=out_specs,
        check_vma=False,
    )
```

```python
import functools

import jax
import jax.numpy as jnp
from jax import lax
from jax.experimental import pallas as pl
from jax.experimental.pallas import tpu as pltpu
from jax.sharding import PartitionSpec as P

F32 = jnp.float32
BF16 = jnp.bfloat16
LANES = 128
BIG = 1e9
MIB = 1024 * 1024


def iota(shape, dim):
    return lax.broadcasted_iota(jnp.int32, shape, dim)


def prepare_kernel(me_ref, tokens_ref, routes_ref, gates_ref, prio_ref, rows_ref):
    rows, width = tokens_ref.shape
    top = routes_ref.shape[0]
    for block in range(width // LANES):
        lanes = slice(block * LANES, (block + 1) * LANES)
        x = tokens_ref[:, lanes].astype(F32)
        largest = jnp.max(jnp.abs(x), axis=1, keepdims=True)
        scale = ((largest + 1e-06) / 448.0).astype(BF16).astype(F32)
        quantized = (x / scale).astype(BF16)
        rows_ref[:, lanes] = (quantized.astype(F32) * scale).astype(BF16)
    gates = gates_ref[...]
    high = gates.astype(BF16)
    middle = (gates - high.astype(F32)).astype(BF16)
    low = (gates - high.astype(F32) - middle.astype(F32)).astype(BF16)
    place, token = iota((top, rows), 0), iota((top, rows), 1)
    other = jnp.where(place == 0, prio_ref[...], jnp.where(place == 1, me_ref[0], token))
    fields = [routes_ref[...].astype(F32), high.astype(F32), middle.astype(F32), low.astype(F32), other.astype(F32)]
    stacked = jnp.concatenate(fields, axis=0)
    place = iota((stacked.shape[0], LANES), 0) == iota((stacked.shape[0], LANES), 1)
    facts = lax.dot_general(
        stacked.astype(BF16), place.astype(F32).astype(BF16), (((0,), (0,)), ((), ())), preferred_element_type=F32
    )
    rows_ref[:, width:] = facts.astype(BF16)


def prepare(me, tokens, routes, gates, priority):
    rows, width = tokens.shape
    return pl.pallas_call(
        prepare_kernel,
        in_specs=[pl.BlockSpec(memory_space=pltpu.SMEM)] + [pl.BlockSpec(memory_space=pltpu.VMEM)] * 4,
        out_specs=pl.BlockSpec(memory_space=pltpu.VMEM),
        out_shape=jax.ShapeDtypeStruct((rows, width + LANES), BF16),
    )(me, tokens, routes.T, gates.T, priority.reshape(1, rows))


def weigh_kernel(top, tok_rows, me_ref, capacity_ref, *refs):
    fact_refs, out_ref, (all_ref, key_ref, row_ref) = refs[:-4], refs[-4], refs[-3:]
    total = all_ref.shape[0]
    at = 0
    for ref in fact_refs:
        rows, wide = ref.shape
        all_ref[at : at + rows, :] = ref[:, wide - LANES :]
        at += rows
    eye = iota((LANES, LANES), 0) == iota((LANES, LANES), 1)
    lane = iota((LANES, LANES), 1)
    tiles = total // LANES
    mine = tiles // 2
    experts = (me_ref[0], me_ref[0] + 1 - 2 * lax.rem(me_ref[0], 2))
    worth = jnp.where(lane == 4 * top, float(total), 0.0)
    worth = jnp.where(lane == 4 * top + 1, float(tok_rows), jnp.where(lane == 4 * top + 2, 1.0, worth))

    def read(i, _, own):
        facts = all_ref[pl.ds(pl.multiple_of(i * LANES, LANES), LANES), :].astype(F32)
        values = (
            pltpu.roll(facts, LANES - top, 1)
            + pltpu.roll(facts, LANES - 2 * top, 1)
            + pltpu.roll(facts, LANES - 3 * top, 1)
        )
        order = jnp.sum(facts * worth, axis=1, keepdims=True)
        for e, expert in enumerate(experts):
            named = (lane < top) & (facts == expert.astype(F32))
            gate = jnp.sum(jnp.where(named, values, 0.0), axis=1, keepdims=True)
            key = jnp.where(gate > 0.0, order, BIG)
            row_ref[e, pl.ds(i, 1), :] = jnp.sum(jnp.where(eye, key, 0.0), axis=0, keepdims=True)
            if own:
                key_ref[e, i] = jnp.broadcast_to(key, (LANES, LANES))
                held = pl.ds(pl.multiple_of((e * mine + i) * LANES, LANES), LANES)
                out_ref[held, :] = jnp.broadcast_to(gate, (LANES, LANES))
        return 0

    lax.fori_loop(0, mine, functools.partial(read, own=True), 0, unroll=min(mine, 4))
    lax.fori_loop(mine, tiles, functools.partial(read, own=False), 0, unroll=min(mine, 4))
    for e, expert in enumerate(experts):
        limit = capacity_ref[expert].astype(F32)

        def judge(i, _, e=e, limit=limit):
            held = pl.ds(pl.multiple_of((e * mine + i) * LANES, LANES), LANES)
            key = key_ref[e, i]

            def count(j, smaller):
                return smaller + (row_ref[e, pl.ds(j, 1), :] < key).astype(F32)

            smaller = lax.fori_loop(0, tiles, count, jnp.zeros((LANES, LANES), F32), unroll=min(tiles, 8))
            rank = jnp.sum(smaller, axis=1, keepdims=True)
            out_ref[held, :] = jnp.where(rank < limit, out_ref[held, :], 0.0)
            return 0

        lax.fori_loop(0, mine, judge, 0, unroll=min(mine, 4))


def weigh(me, capacity, facts, top, tok_rows):
    total = sum(f.shape[0] for f in facts)
    tiles = total // LANES
    return pl.pallas_call(
        functools.partial(weigh_kernel, top, tok_rows),
        in_specs=[pl.BlockSpec(memory_space=pltpu.SMEM)] * 2
        + [pl.BlockSpec(memory_space=pltpu.VMEM)] * len(facts),
        out_specs=pl.BlockSpec(memory_space=pltpu.VMEM),
        out_shape=jax.ShapeDtypeStruct((total, LANES), F32),
        scratch_shapes=[
            pltpu.VMEM((total, LANES), BF16),
            pltpu.VMEM((2, tiles // 2, LANES, LANES), F32),
            pltpu.VMEM((2, tiles, LANES), F32),
        ],
        compiler_params=pltpu.CompilerParams(vmem_limit_bytes=24 * MIB),
        cost_estimate=pl.CostEstimate(flops=1, bytes_accessed=1, transcendentals=0),
    )(me, capacity, *facts)


def pack_kernel(*refs):
    rows = refs[0].shape[0]
    for k, ref in enumerate(refs[:-1]):
        refs[-1][k * rows : (k + 1) * rows, :] = ref[...]


def pack(blocks):
    rows, wide = blocks[0].shape
    return pl.pallas_call(
        pack_kernel,
        in_specs=[pl.BlockSpec(memory_space=pltpu.VMEM)] * len(blocks),
        out_specs=pl.BlockSpec(memory_space=pltpu.VMEM),
        out_shape=jax.ShapeDtypeStruct((len(blocks) * rows, wide), BF16),
        compiler_params=pltpu.CompilerParams(vmem_limit_bytes=24 * MIB),
        cost_estimate=pl.CostEstimate(flops=1, bytes_accessed=1, transcendentals=0),
    )(*blocks)


def combine_kernel(rows, sums, weighted, *refs):
    ins, outs = refs[: -len(sums)], refs[-len(sums) :]
    width = outs[0].shape[1]
    for lanes in range(0, width, 256):
        for terms, out in zip(sums, outs):
            total = None
            for which, first, place in terms:
                value = ins[which][first : first + rows, lanes : lanes + 256].astype(F32)
                if place is not None:
                    value = value * ins[weighted][place : place + rows, :1]
                total = value if total is None else total + value
            out[:, lanes : lanes + 256] = total.astype(out.dtype)


def combine(arrays, weights, sums, kind=BF16):
    rows = weights.shape[0] // 16
    width = arrays[0].shape[1]
    sums = [[(a, b * rows, None if p is None else p * rows) for a, b, p in terms] for terms in sums]
    return pl.pallas_call(
        functools.partial(combine_kernel, rows, sums, len(arrays)),
        in_specs=[pl.BlockSpec(memory_space=pltpu.VMEM)] * (len(arrays) + 1),
        out_specs=[pl.BlockSpec(memory_space=pltpu.VMEM)] * len(sums),
        out_shape=[jax.ShapeDtypeStruct((rows, width), kind)] * len(sums),
        compiler_params=pltpu.CompilerParams(vmem_limit_bytes=24 * MIB),
        cost_estimate=pl.CostEstimate(flops=1, bytes_accessed=1, transcendentals=0),
    )(*arrays, weights)


def load_kernel(*refs):
    count = len(refs) // 2
    sems = refs[-1]
    copies = [pltpu.make_async_copy(refs[k], refs[count + k], sems.at[k]) for k in range(count)]
    for copy in copies:
        copy.start()
    for copy in copies:
        copy.wait()


def load(*arrays):
    size = sum(a.size * 2 for a in arrays)
    return pl.pallas_call(
        load_kernel,
        in_specs=[pl.BlockSpec(memory_space=pl.ANY)] * len(arrays),
        out_specs=[pl.BlockSpec(memory_space=pltpu.VMEM)] * len(arrays),
        out_shape=[jax.ShapeDtypeStruct(a.shape, a.dtype) for a in arrays],
        scratch_shapes=[pltpu.SemaphoreType.DMA((len(arrays),))],
        compiler_params=pltpu.CompilerParams(vmem_limit_bytes=size + 4 * MIB),
    )(*arrays)


FF_TILE, OUT_TILE = 256, 512


def expert_kernel(pieces, *refs):
    x_refs, (gate_ref, up_ref, down_ref) = refs[: -5 - pieces], refs[-5 - pieces : -2 - pieces]
    out_refs, (x, hidden) = refs[-2 - pieces : -2], refs[-2:]
    width, ff = x.shape[1], hidden.shape[1]
    at = 0
    for ref in x_refs:
        x[at : at + ref.shape[0], :] = ref[:, :width]
        at += ref.shape[0]
    for k in range(ff // FF_TILE):
        lanes = slice(k * FF_TILE, (k + 1) * FF_TILE)
        gated = jnp.dot(x[...], gate_ref[0, :, lanes], preferred_element_type=F32)
        upward = jnp.dot(x[...], up_ref[0, :, lanes], preferred_element_type=F32)
        hidden[:, lanes] = (gated / (1.0 + jnp.exp(-gated)) * upward).astype(BF16)
    for k in range(width // OUT_TILE):
        lanes = slice(k * OUT_TILE, (k + 1) * OUT_TILE)
        made = jnp.dot(hidden[...], down_ref[0, :, lanes], preferred_element_type=F32).astype(BF16)
        rows = made.shape[0] // pieces
        for k, out_ref in enumerate(out_refs):
            out_ref[:, lanes] = made[k * rows : (k + 1) * rows]


def expert(arrays, matrices, pieces=1, flops=1):
    ff, width = matrices[2].shape[1:]
    rows = sum(a.shape[0] for a in arrays)
    held = rows * 2 * (width + ff) + 4 * rows * (2 * FF_TILE + OUT_TILE)
    made = pl.pallas_call(
        functools.partial(expert_kernel, pieces),
        in_specs=[pl.BlockSpec(memory_space=pltpu.VMEM)] * (len(arrays) + 3),
        out_specs=[pl.BlockSpec(memory_space=pltpu.VMEM)] * pieces,
        out_shape=[jax.ShapeDtypeStruct((rows // pieces, width), BF16)] * pieces,
        scratch_shapes=[pltpu.VMEM((rows, width), BF16), pltpu.VMEM((rows, ff), BF16)],
        compiler_params=pltpu.CompilerParams(vmem_limit_bytes=held + 20 * MIB),
        cost_estimate=pl.CostEstimate(flops=flops, bytes_accessed=1, transcendentals=0),
    )(*arrays, *matrices)
    return made if pieces > 1 else made[0]


def orders(ep):
    bits = list(range(ep.bit_length() - 1))[::-1]
    return (bits, bits[:-2] + bits[:-3:-1])


def send(array, ep, flips):
    pairs = []
    for place in range(ep):
        for core, order in enumerate(orders(ep)):
            to = place
            for flip in flips:
                to ^= 1 << order[flip]
            pairs.append((2 * place + core, 2 * to + core))
    return lax.ppermute(array, ("ep", "sub"), pairs)


def cross(array):
    return lax.ppermute(array, "sub", [(0, 1), (1, 0)])


def add(*terms):
    return sum([t.astype(F32) for t in terms]).astype(BF16)


def on_device(ep, tokens, routes, gates, priority, capacity, w_gate, w_up, w_down):
    tok_rows, width = tokens.shape
    top = routes.shape[1]
    steps = ep.bit_length() - 1
    me = (lax.axis_index("ep") * 2 + lax.axis_index("sub")).astype(jnp.int32).reshape(1)
    held = prepare(me, tokens, routes, gates, priority)
    for step in range(steps - 3):
        held = jnp.concatenate([held, send(held, ep, [step])])
    base = held.shape[0]
    own1, own2, own4 = send(held, ep, [-3]), send(held, ep, [-2]), send(held, ep, [-1])
    first = cross(held)
    matrices = load(w_gate, w_up, w_down)
    first, own4, own2, own1, matrices = lax.optimization_barrier((first, own4, own2, own1, matrices))
    crossed = cross(pack([own1, own2, own4]))
    own3 = send(own1, ep, [-2])
    own5 = send(own1, ep, [-1])
    own6 = send(own2, ep, [-1])
    theirs = expert([first, crossed], matrices)
    own3, theirs = lax.optimization_barrier((own3, theirs))
    own7 = send(own3, ep, [-1])
    far_crossed = [cross(o) for o in (own3, own6, own5)]
    far_made = expert([own3, own5, own6], matrices)
    own3, own5, own6, own7, theirs, far_made = lax.optimization_barrier((own3, own5, own6, own7, theirs, far_made))
    far = [own5, own7, own3, own6]
    last_crossed = cross(own7)
    last_made = expert([own7], matrices)
    far_crossed, last_crossed, last_made = lax.optimization_barrier((far_crossed, last_crossed, last_made))
    last_back, first_back = expert([*far_crossed, last_crossed], matrices, 2)
    first_back = cross(first_back)
    near = [held, own1, own2, own4]
    weights = weigh(me, capacity, near + far + [first, crossed, *far_crossed, last_crossed], top, tok_rows)
    weights, theirs, last_back = lax.optimization_barrier((weights, theirs, last_back))
    last_back = cross(last_back)

    def part(mine, back, block, place):
        return [(mine, block, place), (back, block, 8 + place)]

    send5, send7 = combine(
        [far_made, last_made, first_back], weights, [[(0, 1, 4), (2, 0, 12)], [(1, 0, 5), (2, 1, 13)]]
    )
    back7 = send(send7, ep, [-1])
    back5 = send(send5, ep, [-1])
    send3, send6 = combine(
        [far_made, last_back, back7],
        weights,
        [[(0, 0, 6), (1, 0, 14), (2, 0, None)], [(0, 2, 7), (1, 1, 15)]],
    )
    back3 = send(send3, ep, [-2])
    near_made = expert(near, matrices)
    near_made, send6 = lax.optimization_barrier((near_made, send6))
    back6 = send(send6, ep, [-1])
    near_back = cross(theirs)
    (send4,) = combine([near_made, near_back], weights, [part(0, 1, 3, 3)])
    back4 = send(send4, ep, [-1])
    back3, back5, send4 = lax.optimization_barrier((back3, back5, send4))
    (send1,) = combine([near_made, near_back, back3, back5], weights, [part(0, 1, 1, 1) + [(2, 0, None), (3, 0, None)]])
    back1 = send(send1, ep, [-3])
    back6, send1 = lax.optimization_barrier((back6, send1))
    (send2,) = combine([near_made, near_back, back6], weights, [part(0, 1, 2, 2) + [(2, 0, None)]])
    back2 = send(send2, ep, [-2])
    (total,) = combine([near_made, near_back, back4], weights, [part(0, 1, 0, 0) + [(2, 0, None)]], F32)
    back1, total = lax.optimization_barrier((back1, total))
    (total,) = combine([total, back1], weights, [[(0, 0, None), (1, 0, None)]], F32)
    back2, total = lax.optimization_barrier((back2, total))
    (total,) = combine([total, back2], weights, [[(0, 0, None), (1, 0, None)]])
    for step in range(steps - 3)[::-1]:
        half = total.shape[0] // 2
        total = add(total[:half], send(total[half:], ep, [step]))
    return total


def solution(mesh):
    in_specs = (
        P(("groups", "ep", "sub"), None),
        P(("groups", "ep", "sub"), None),
        P(("groups", "ep", "sub"), None),
        P(("groups", "ep", "sub")),
        P(),
        P(("ep", "sub"), None, None),
        P(("ep", "sub"), None, None),
        P(("ep", "sub"), None, None),
    )
    out_specs = P(("groups", "ep", "sub"), None)
    return jax.shard_map(
        functools.partial(on_device, mesh.shape["ep"]),
        mesh=mesh,
        in_specs=in_specs,
        out_specs=out_specs,
        check_vma=False,
    )
```

```python
import functools

import jax
import jax.numpy as jnp
from jax import lax
from jax.experimental import pallas as pl
from jax.experimental.pallas import tpu as pltpu
from jax.sharding import PartitionSpec as P

F32 = jnp.float32
BF16 = jnp.bfloat16
LANES = 128
BIG = 1e9
MIB = 1024 * 1024


def iota(shape, dim):
    return lax.broadcasted_iota(jnp.int32, shape, dim)


def prepare_kernel(me_ref, tokens_ref, routes_ref, gates_ref, prio_ref, rows_ref):
    rows, width = tokens_ref.shape
    top = routes_ref.shape[0]
    for block in range(width // LANES):
        lanes = slice(block * LANES, (block + 1) * LANES)
        x = tokens_ref[:, lanes].astype(F32)
        largest = jnp.max(jnp.abs(x), axis=1, keepdims=True)
        scale = ((largest + 1e-06) / 448.0).astype(BF16).astype(F32)
        quantized = (x / scale).astype(BF16)
        rows_ref[:, lanes] = (quantized.astype(F32) * scale).astype(BF16)
    gates = gates_ref[...]
    high = gates.astype(BF16)
    middle = (gates - high.astype(F32)).astype(BF16)
    low = (gates - high.astype(F32) - middle.astype(F32)).astype(BF16)
    place, token = iota((top, rows), 0), iota((top, rows), 1)
    other = jnp.where(place == 0, prio_ref[...], jnp.where(place == 1, me_ref[0], token))
    fields = [routes_ref[...].astype(F32), high.astype(F32), middle.astype(F32), low.astype(F32), other.astype(F32)]
    stacked = jnp.concatenate(fields, axis=0)
    place = iota((stacked.shape[0], LANES), 0) == iota((stacked.shape[0], LANES), 1)
    facts = lax.dot_general(
        stacked.astype(BF16), place.astype(F32).astype(BF16), (((0,), (0,)), ((), ())), preferred_element_type=F32
    )
    rows_ref[:, width:] = facts.astype(BF16)


def prepare(me, tokens, routes, gates, priority):
    rows, width = tokens.shape
    return pl.pallas_call(
        prepare_kernel,
        in_specs=[pl.BlockSpec(memory_space=pltpu.SMEM)] + [pl.BlockSpec(memory_space=pltpu.VMEM)] * 4,
        out_specs=pl.BlockSpec(memory_space=pltpu.VMEM),
        out_shape=jax.ShapeDtypeStruct((rows, width + LANES), BF16),
    )(me, tokens, routes.T, gates.T, priority.reshape(1, rows))


def weigh_kernel(top, tok_rows, me_ref, capacity_ref, *refs):
    fact_refs, out_ref, (all_ref, key_ref, row_ref) = refs[:-4], refs[-4], refs[-3:]
    total = all_ref.shape[0]
    at = 0
    for ref in fact_refs:
        rows, wide = ref.shape
        all_ref[at : at + rows, :] = ref[:, wide - LANES :]
        at += rows
    eye = iota((LANES, LANES), 0) == iota((LANES, LANES), 1)
    lane = iota((LANES, LANES), 1)
    tiles = total // LANES
    mine = tiles // 2
    experts = (me_ref[0], me_ref[0] + 1 - 2 * lax.rem(me_ref[0], 2))
    worth = jnp.where(lane == 4 * top, float(total), 0.0)
    worth = jnp.where(lane == 4 * top + 1, float(tok_rows), jnp.where(lane == 4 * top + 2, 1.0, worth))

    def read(i, _, own):
        facts = all_ref[pl.ds(pl.multiple_of(i * LANES, LANES), LANES), :].astype(F32)
        values = (
            pltpu.roll(facts, LANES - top, 1)
            + pltpu.roll(facts, LANES - 2 * top, 1)
            + pltpu.roll(facts, LANES - 3 * top, 1)
        )
        order = jnp.sum(facts * worth, axis=1, keepdims=True)
        for e, expert in enumerate(experts):
            named = (lane < top) & (facts == expert.astype(F32))
            gate = jnp.sum(jnp.where(named, values, 0.0), axis=1, keepdims=True)
            key = jnp.where(gate > 0.0, order, BIG)
            row_ref[e, pl.ds(i, 1), :] = jnp.sum(jnp.where(eye, key, 0.0), axis=0, keepdims=True)
            if own:
                key_ref[e, i] = jnp.broadcast_to(key, (LANES, LANES))
                held = pl.ds(pl.multiple_of((e * mine + i) * LANES, LANES), LANES)
                out_ref[held, :] = jnp.broadcast_to(gate, (LANES, LANES))
        return 0

    lax.fori_loop(0, mine, functools.partial(read, own=True), 0, unroll=min(mine, 4))
    lax.fori_loop(mine, tiles, functools.partial(read, own=False), 0, unroll=min(mine, 4))
    for e, expert in enumerate(experts):
        limit = capacity_ref[expert].astype(F32)

        def judge(i, _, e=e, limit=limit):
            held = pl.ds(pl.multiple_of((e * mine + i) * LANES, LANES), LANES)
            key = key_ref[e, i]

            def count(j, smaller):
                return smaller + (row_ref[e, pl.ds(j, 1), :] < key).astype(F32)

            smaller = lax.fori_loop(0, tiles, count, jnp.zeros((LANES, LANES), F32), unroll=min(tiles, 8))
            rank = jnp.sum(smaller, axis=1, keepdims=True)
            out_ref[held, :] = jnp.where(rank < limit, out_ref[held, :], 0.0)
            return 0

        lax.fori_loop(0, mine, judge, 0, unroll=min(mine, 4))


def weigh(me, capacity, facts, top, tok_rows):
    total = sum(f.shape[0] for f in facts)
    tiles = total // LANES
    return pl.pallas_call(
        functools.partial(weigh_kernel, top, tok_rows),
        in_specs=[pl.BlockSpec(memory_space=pltpu.SMEM)] * 2
        + [pl.BlockSpec(memory_space=pltpu.VMEM)] * len(facts),
        out_specs=pl.BlockSpec(memory_space=pltpu.VMEM),
        out_shape=jax.ShapeDtypeStruct((total, LANES), F32),
        scratch_shapes=[
            pltpu.VMEM((total, LANES), BF16),
            pltpu.VMEM((2, tiles // 2, LANES, LANES), F32),
            pltpu.VMEM((2, tiles, LANES), F32),
        ],
        compiler_params=pltpu.CompilerParams(vmem_limit_bytes=24 * MIB),
        cost_estimate=pl.CostEstimate(flops=1, bytes_accessed=1, transcendentals=0),
    )(me, capacity, *facts)


def pack_kernel(*refs):
    rows = refs[0].shape[0]
    for k, ref in enumerate(refs[:-1]):
        refs[-1][k * rows : (k + 1) * rows, :] = ref[...]


def pack(blocks):
    rows, wide = blocks[0].shape
    return pl.pallas_call(
        pack_kernel,
        in_specs=[pl.BlockSpec(memory_space=pltpu.VMEM)] * len(blocks),
        out_specs=pl.BlockSpec(memory_space=pltpu.VMEM),
        out_shape=jax.ShapeDtypeStruct((len(blocks) * rows, wide), BF16),
        compiler_params=pltpu.CompilerParams(vmem_limit_bytes=24 * MIB),
        cost_estimate=pl.CostEstimate(flops=1, bytes_accessed=1, transcendentals=0),
    )(*blocks)


def combine_kernel(rows, sums, weighted, *refs):
    ins, outs = refs[: -len(sums)], refs[-len(sums) :]
    width = outs[0].shape[1]
    for lanes in range(0, width, 256):
        for terms, out in zip(sums, outs):
            total = None
            for which, first, place in terms:
                value = ins[which][first : first + rows, lanes : lanes + 256].astype(F32)
                if place is not None:
                    value = value * ins[weighted][place : place + rows, :1]
                total = value if total is None else total + value
            out[:, lanes : lanes + 256] = total.astype(out.dtype)


def combine(arrays, weights, sums, kind=BF16):
    rows = weights.shape[0] // 16
    width = arrays[0].shape[1]
    sums = [[(a, b * rows, None if p is None else p * rows) for a, b, p in terms] for terms in sums]
    return pl.pallas_call(
        functools.partial(combine_kernel, rows, sums, len(arrays)),
        in_specs=[pl.BlockSpec(memory_space=pltpu.VMEM)] * (len(arrays) + 1),
        out_specs=[pl.BlockSpec(memory_space=pltpu.VMEM)] * len(sums),
        out_shape=[jax.ShapeDtypeStruct((rows, width), kind)] * len(sums),
        compiler_params=pltpu.CompilerParams(vmem_limit_bytes=24 * MIB),
        cost_estimate=pl.CostEstimate(flops=1, bytes_accessed=1, transcendentals=0),
    )(*arrays, weights)


def load_kernel(*refs):
    count = len(refs) // 2
    sems = refs[-1]
    copies = [pltpu.make_async_copy(refs[k], refs[count + k], sems.at[k]) for k in range(count)]
    for copy in copies:
        copy.start()
    for copy in copies:
        copy.wait()


def load(*arrays):
    size = sum(a.size * 2 for a in arrays)
    return pl.pallas_call(
        load_kernel,
        in_specs=[pl.BlockSpec(memory_space=pl.ANY)] * len(arrays),
        out_specs=[pl.BlockSpec(memory_space=pltpu.VMEM)] * len(arrays),
        out_shape=[jax.ShapeDtypeStruct(a.shape, a.dtype) for a in arrays],
        scratch_shapes=[pltpu.SemaphoreType.DMA((len(arrays),))],
        compiler_params=pltpu.CompilerParams(vmem_limit_bytes=size + 4 * MIB),
    )(*arrays)


FF_TILE, OUT_TILE = 256, 512


def expert_kernel(pieces, *refs):
    x_refs, (gate_ref, up_ref, down_ref) = refs[: -5 - pieces], refs[-5 - pieces : -2 - pieces]
    out_refs, (x, hidden) = refs[-2 - pieces : -2], refs[-2:]
    width, ff = x.shape[1], hidden.shape[1]
    at = 0
    for ref in x_refs:
        x[at : at + ref.shape[0], :] = ref[:, :width]
        at += ref.shape[0]
    for k in range(ff // FF_TILE):
        lanes = slice(k * FF_TILE, (k + 1) * FF_TILE)
        gated = jnp.dot(x[...], gate_ref[0, :, lanes], preferred_element_type=F32)
        upward = jnp.dot(x[...], up_ref[0, :, lanes], preferred_element_type=F32)
        hidden[:, lanes] = (gated / (1.0 + jnp.exp(-gated)) * upward).astype(BF16)
    for k in range(width // OUT_TILE):
        lanes = slice(k * OUT_TILE, (k + 1) * OUT_TILE)
        made = jnp.dot(hidden[...], down_ref[0, :, lanes], preferred_element_type=F32).astype(BF16)
        rows = made.shape[0] // pieces
        for k, out_ref in enumerate(out_refs):
            out_ref[:, lanes] = made[k * rows : (k + 1) * rows]


def expert(arrays, matrices, pieces=1, flops=1):
    ff, width = matrices[2].shape[1:]
    rows = sum(a.shape[0] for a in arrays)
    held = rows * 2 * (width + ff) + 4 * rows * (2 * FF_TILE + OUT_TILE)
    made = pl.pallas_call(
        functools.partial(expert_kernel, pieces),
        in_specs=[pl.BlockSpec(memory_space=pltpu.VMEM)] * (len(arrays) + 3),
        out_specs=[pl.BlockSpec(memory_space=pltpu.VMEM)] * pieces,
        out_shape=[jax.ShapeDtypeStruct((rows // pieces, width), BF16)] * pieces,
        scratch_shapes=[pltpu.VMEM((rows, width), BF16), pltpu.VMEM((rows, ff), BF16)],
        compiler_params=pltpu.CompilerParams(vmem_limit_bytes=held + 20 * MIB),
        cost_estimate=pl.CostEstimate(flops=flops, bytes_accessed=1, transcendentals=0),
    )(*arrays, *matrices)
    return made if pieces > 1 else made[0]


def orders(ep):
    bits = list(range(ep.bit_length() - 1))[::-1]
    return (bits, bits[:-2] + bits[:-3:-1])


def send(array, ep, flips):
    pairs = []
    for place in range(ep):
        for core, order in enumerate(orders(ep)):
            to = place
            for flip in flips:
                to ^= 1 << order[flip]
            pairs.append((2 * place + core, 2 * to + core))
    return lax.ppermute(array, ("ep", "sub"), pairs)


def cross(array):
    return lax.ppermute(array, "sub", [(0, 1), (1, 0)])


def add(*terms):
    return sum([t.astype(F32) for t in terms]).astype(BF16)


def on_device(ep, tokens, routes, gates, priority, capacity, w_gate, w_up, w_down):
    tok_rows, width = tokens.shape
    top = routes.shape[1]
    steps = ep.bit_length() - 1
    me = (lax.axis_index("ep") * 2 + lax.axis_index("sub")).astype(jnp.int32).reshape(1)
    held = prepare(me, tokens, routes, gates, priority)
    for step in range(steps - 3):
        held = jnp.concatenate([held, send(held, ep, [step])])
    base = held.shape[0]
    own1, own2, own4 = send(held, ep, [-3]), send(held, ep, [-2]), send(held, ep, [-1])
    first = cross(held)
    matrices = load(w_gate, w_up, w_down)
    first, own1, matrices = lax.optimization_barrier((first, own1, matrices))
    crossed = cross(pack([own1, own2, own4]))
    own3 = send(own1, ep, [-2])
    own5 = send(own1, ep, [-1])
    own6 = send(own2, ep, [-1])
    theirs = expert([first, crossed], matrices)
    own3, theirs = lax.optimization_barrier((own3, theirs))
    own7 = send(own3, ep, [-1])
    far_crossed = [cross(o) for o in (own3, own6, own5)]
    far_made = expert([own3, own5, own6], matrices)
    own3, own5, own6, own7, theirs, far_made = lax.optimization_barrier((own3, own5, own6, own7, theirs, far_made))
    far = [own5, own7, own3, own6]
    last_crossed = cross(own7)
    last_made = expert([own7], matrices)
    far_crossed, last_crossed, last_made = lax.optimization_barrier((far_crossed, last_crossed, last_made))
    last_back, first_back = expert([*far_crossed, last_crossed], matrices, 2)
    first_back = cross(first_back)
    near = [held, own1, own2, own4]
    weights = weigh(me, capacity, near + far + [first, crossed, *far_crossed, last_crossed], top, tok_rows)
    weights, theirs, last_back = lax.optimization_barrier((weights, theirs, last_back))
    last_back = cross(last_back)

    def part(mine, back, block, place):
        return [(mine, block, place), (back, block, 8 + place)]

    send5, send7 = combine(
        [far_made, last_made, first_back], weights, [[(0, 1, 4), (2, 0, 12)], [(1, 0, 5), (2, 1, 13)]]
    )
    back7 = send(send7, ep, [-1])
    back5 = send(send5, ep, [-1])
    send3, send6 = combine(
        [far_made, last_back, back7],
        weights,
        [[(0, 0, 6), (1, 0, 14), (2, 0, None)], [(0, 2, 7), (1, 1, 15)]],
    )
    back3 = send(send3, ep, [-2])
    near_made = expert(near, matrices)
    near_made, send6 = lax.optimization_barrier((near_made, send6))
    back6 = send(send6, ep, [-1])
    near_back = cross(theirs)
    (send4,) = combine([near_made, near_back], weights, [part(0, 1, 3, 3)])
    back4 = send(send4, ep, [-1])
    back3, back5, send4 = lax.optimization_barrier((back3, back5, send4))
    (send1,) = combine([near_made, near_back, back3, back5], weights, [part(0, 1, 1, 1) + [(2, 0, None), (3, 0, None)]])
    back1 = send(send1, ep, [-3])
    back6, send1 = lax.optimization_barrier((back6, send1))
    (send2,) = combine([near_made, near_back, back6], weights, [part(0, 1, 2, 2) + [(2, 0, None)]])
    back2 = send(send2, ep, [-2])
    (total,) = combine([near_made, near_back, back4], weights, [part(0, 1, 0, 0) + [(2, 0, None)]], F32)
    back1, total = lax.optimization_barrier((back1, total))
    (total,) = combine([total, back1], weights, [[(0, 0, None), (1, 0, None)]], F32)
    back2, total = lax.optimization_barrier((back2, total))
    (total,) = combine([total, back2], weights, [[(0, 0, None), (1, 0, None)]])
    for step in range(steps - 3)[::-1]:
        half = total.shape[0] // 2
        total = add(total[:half], send(total[half:], ep, [step]))
    return total


def solution(mesh):
    in_specs = (
        P(("groups", "ep", "sub"), None),
        P(("groups", "ep", "sub"), None),
        P(("groups", "ep", "sub"), None),
        P(("groups", "ep", "sub")),
        P(),
        P(("ep", "sub"), None, None),
        P(("ep", "sub"), None, None),
        P(("ep", "sub"), None, None),
    )
    out_specs = P(("groups", "ep", "sub"), None)
    return jax.shard_map(
        functools.partial(on_device, mesh.shape["ep"]),
        mesh=mesh,
        in_specs=in_specs,
        out_specs=out_specs,
        check_vma=False,
    )
```

```python
import functools

import jax
import jax.numpy as jnp
from jax import lax
from jax.experimental import pallas as pl
from jax.experimental.pallas import tpu as pltpu
from jax.sharding import PartitionSpec as P

F32 = jnp.float32
BF16 = jnp.bfloat16
LANES = 128
BIG = 1e9
MIB = 1024 * 1024


def iota(shape, dim):
    return lax.broadcasted_iota(jnp.int32, shape, dim)


def prepare_kernel(me_ref, tokens_ref, routes_ref, gates_ref, prio_ref, rows_ref):
    rows, width = tokens_ref.shape
    top = routes_ref.shape[0]
    for block in range(width // LANES):
        lanes = slice(block * LANES, (block + 1) * LANES)
        x = tokens_ref[:, lanes].astype(F32)
        largest = jnp.max(jnp.abs(x), axis=1, keepdims=True)
        scale = ((largest + 1e-06) / 448.0).astype(BF16).astype(F32)
        quantized = (x / scale).astype(BF16)
        rows_ref[:, lanes] = (quantized.astype(F32) * scale).astype(BF16)
    gates = gates_ref[...]
    high = gates.astype(BF16)
    middle = (gates - high.astype(F32)).astype(BF16)
    low = (gates - high.astype(F32) - middle.astype(F32)).astype(BF16)
    place, token = iota((top, rows), 0), iota((top, rows), 1)
    other = jnp.where(place == 0, prio_ref[...], jnp.where(place == 1, me_ref[0], token))
    fields = [routes_ref[...].astype(F32), high.astype(F32), middle.astype(F32), low.astype(F32), other.astype(F32)]
    stacked = jnp.concatenate(fields, axis=0)
    place = iota((stacked.shape[0], LANES), 0) == iota((stacked.shape[0], LANES), 1)
    facts = lax.dot_general(
        stacked.astype(BF16), place.astype(F32).astype(BF16), (((0,), (0,)), ((), ())), preferred_element_type=F32
    )
    rows_ref[:, width:] = facts.astype(BF16)


def prepare(me, tokens, routes, gates, priority):
    rows, width = tokens.shape
    return pl.pallas_call(
        prepare_kernel,
        in_specs=[pl.BlockSpec(memory_space=pltpu.SMEM)] + [pl.BlockSpec(memory_space=pltpu.VMEM)] * 4,
        out_specs=pl.BlockSpec(memory_space=pltpu.VMEM),
        out_shape=jax.ShapeDtypeStruct((rows, width + LANES), BF16),
    )(me, tokens, routes.T, gates.T, priority.reshape(1, rows))


def weigh_kernel(top, tok_rows, me_ref, capacity_ref, *refs):
    fact_refs, out_ref, (all_ref, key_ref, row_ref) = refs[:-4], refs[-4], refs[-3:]
    total = all_ref.shape[0]
    at = 0
    for ref in fact_refs:
        rows, wide = ref.shape
        all_ref[at : at + rows, :] = ref[:, wide - LANES :]
        at += rows
    eye = iota((LANES, LANES), 0) == iota((LANES, LANES), 1)
    lane = iota((LANES, LANES), 1)
    tiles = total // LANES
    mine = tiles // 2
    experts = (me_ref[0], me_ref[0] + 1 - 2 * lax.rem(me_ref[0], 2))
    worth = jnp.where(lane == 4 * top, float(total), 0.0)
    worth = jnp.where(lane == 4 * top + 1, float(tok_rows), jnp.where(lane == 4 * top + 2, 1.0, worth))

    def read(i, _, own):
        facts = all_ref[pl.ds(pl.multiple_of(i * LANES, LANES), LANES), :].astype(F32)
        values = (
            pltpu.roll(facts, LANES - top, 1)
            + pltpu.roll(facts, LANES - 2 * top, 1)
            + pltpu.roll(facts, LANES - 3 * top, 1)
        )
        order = jnp.sum(facts * worth, axis=1, keepdims=True)
        for e, expert in enumerate(experts):
            named = (lane < top) & (facts == expert.astype(F32))
            gate = jnp.sum(jnp.where(named, values, 0.0), axis=1, keepdims=True)
            key = jnp.where(gate > 0.0, order, BIG)
            row_ref[e, pl.ds(i, 1), :] = jnp.sum(jnp.where(eye, key, 0.0), axis=0, keepdims=True)
            if own:
                key_ref[e, i] = jnp.broadcast_to(key, (LANES, LANES))
                held = pl.ds(pl.multiple_of((e * mine + i) * LANES, LANES), LANES)
                out_ref[held, :] = jnp.broadcast_to(gate, (LANES, LANES))
        return 0

    lax.fori_loop(0, mine, functools.partial(read, own=True), 0, unroll=min(mine, 4))
    lax.fori_loop(mine, tiles, functools.partial(read, own=False), 0, unroll=min(mine, 4))
    for e, expert in enumerate(experts):
        limit = capacity_ref[expert].astype(F32)

        def judge(i, _, e=e, limit=limit):
            held = pl.ds(pl.multiple_of((e * mine + i) * LANES, LANES), LANES)
            key = key_ref[e, i]

            def count(j, smaller):
                return smaller + (row_ref[e, pl.ds(j, 1), :] < key).astype(F32)

            smaller = lax.fori_loop(0, tiles, count, jnp.zeros((LANES, LANES), F32), unroll=min(tiles, 8))
            rank = jnp.sum(smaller, axis=1, keepdims=True)
            out_ref[held, :] = jnp.where(rank < limit, out_ref[held, :], 0.0)
            return 0

        lax.fori_loop(0, mine, judge, 0, unroll=min(mine, 4))


def weigh(me, capacity, facts, top, tok_rows):
    total = sum(f.shape[0] for f in facts)
    tiles = total // LANES
    return pl.pallas_call(
        functools.partial(weigh_kernel, top, tok_rows),
        in_specs=[pl.BlockSpec(memory_space=pltpu.SMEM)] * 2
        + [pl.BlockSpec(memory_space=pltpu.VMEM)] * len(facts),
        out_specs=pl.BlockSpec(memory_space=pltpu.VMEM),
        out_shape=jax.ShapeDtypeStruct((total, LANES), F32),
        scratch_shapes=[
            pltpu.VMEM((total, LANES), BF16),
            pltpu.VMEM((2, tiles // 2, LANES, LANES), F32),
            pltpu.VMEM((2, tiles, LANES), F32),
        ],
        compiler_params=pltpu.CompilerParams(vmem_limit_bytes=24 * MIB),
        cost_estimate=pl.CostEstimate(flops=1, bytes_accessed=1, transcendentals=0),
    )(me, capacity, *facts)


def pack_kernel(*refs):
    rows = refs[0].shape[0]
    for k, ref in enumerate(refs[:-1]):
        refs[-1][k * rows : (k + 1) * rows, :] = ref[...]


def pack(blocks):
    rows, wide = blocks[0].shape
    return pl.pallas_call(
        pack_kernel,
        in_specs=[pl.BlockSpec(memory_space=pltpu.VMEM)] * len(blocks),
        out_specs=pl.BlockSpec(memory_space=pltpu.VMEM),
        out_shape=jax.ShapeDtypeStruct((len(blocks) * rows, wide), BF16),
        compiler_params=pltpu.CompilerParams(vmem_limit_bytes=24 * MIB),
        cost_estimate=pl.CostEstimate(flops=1, bytes_accessed=1, transcendentals=0),
    )(*blocks)


def combine_kernel(rows, sums, weighted, *refs):
    ins, outs = refs[: -len(sums)], refs[-len(sums) :]
    width = outs[0].shape[1]
    for lanes in range(0, width, 256):
        for terms, out in zip(sums, outs):
            total = None
            for which, first, place in terms:
                value = ins[which][first : first + rows, lanes : lanes + 256].astype(F32)
                if place is not None:
                    value = value * ins[weighted][place : place + rows, :1]
                total = value if total is None else total + value
            out[:, lanes : lanes + 256] = total.astype(out.dtype)


def combine(arrays, weights, sums, kind=BF16):
    rows = weights.shape[0] // 16
    width = arrays[0].shape[1]
    sums = [[(a, b * rows, None if p is None else p * rows) for a, b, p in terms] for terms in sums]
    return pl.pallas_call(
        functools.partial(combine_kernel, rows, sums, len(arrays)),
        in_specs=[pl.BlockSpec(memory_space=pltpu.VMEM)] * (len(arrays) + 1),
        out_specs=[pl.BlockSpec(memory_space=pltpu.VMEM)] * len(sums),
        out_shape=[jax.ShapeDtypeStruct((rows, width), kind)] * len(sums),
        compiler_params=pltpu.CompilerParams(vmem_limit_bytes=24 * MIB),
        cost_estimate=pl.CostEstimate(flops=1, bytes_accessed=1, transcendentals=0),
    )(*arrays, weights)


def load_kernel(*refs):
    count = len(refs) // 2
    sems = refs[-1]
    copies = [pltpu.make_async_copy(refs[k], refs[count + k], sems.at[k]) for k in range(count)]
    for copy in copies:
        copy.start()
    for copy in copies:
        copy.wait()


def load(*arrays):
    size = sum(a.size * 2 for a in arrays)
    return pl.pallas_call(
        load_kernel,
        in_specs=[pl.BlockSpec(memory_space=pl.ANY)] * len(arrays),
        out_specs=[pl.BlockSpec(memory_space=pltpu.VMEM)] * len(arrays),
        out_shape=[jax.ShapeDtypeStruct(a.shape, a.dtype) for a in arrays],
        scratch_shapes=[pltpu.SemaphoreType.DMA((len(arrays),))],
        compiler_params=pltpu.CompilerParams(vmem_limit_bytes=size + 4 * MIB),
    )(*arrays)


FF_TILE, OUT_TILE = 256, 512


def expert_kernel(pieces, *refs):
    x_refs, (gate_ref, up_ref, down_ref) = refs[: -5 - pieces], refs[-5 - pieces : -2 - pieces]
    out_refs, (x, hidden) = refs[-2 - pieces : -2], refs[-2:]
    width, ff = x.shape[1], hidden.shape[1]
    at = 0
    for ref in x_refs:
        x[at : at + ref.shape[0], :] = ref[:, :width]
        at += ref.shape[0]
    for k in range(ff // FF_TILE):
        lanes = slice(k * FF_TILE, (k + 1) * FF_TILE)
        gated = jnp.dot(x[...], gate_ref[0, :, lanes], preferred_element_type=F32)
        upward = jnp.dot(x[...], up_ref[0, :, lanes], preferred_element_type=F32)
        hidden[:, lanes] = (gated / (1.0 + jnp.exp(-gated)) * upward).astype(BF16)
    for k in range(width // OUT_TILE):
        lanes = slice(k * OUT_TILE, (k + 1) * OUT_TILE)
        made = jnp.dot(hidden[...], down_ref[0, :, lanes], preferred_element_type=F32).astype(BF16)
        rows = made.shape[0] // pieces
        for k, out_ref in enumerate(out_refs):
            out_ref[:, lanes] = made[k * rows : (k + 1) * rows]


def expert(arrays, matrices, pieces=1, flops=1):
    ff, width = matrices[2].shape[1:]
    rows = sum(a.shape[0] for a in arrays)
    held = rows * 2 * (width + ff) + 4 * rows * (2 * FF_TILE + OUT_TILE)
    made = pl.pallas_call(
        functools.partial(expert_kernel, pieces),
        in_specs=[pl.BlockSpec(memory_space=pltpu.VMEM)] * (len(arrays) + 3),
        out_specs=[pl.BlockSpec(memory_space=pltpu.VMEM)] * pieces,
        out_shape=[jax.ShapeDtypeStruct((rows // pieces, width), BF16)] * pieces,
        scratch_shapes=[pltpu.VMEM((rows, width), BF16), pltpu.VMEM((rows, ff), BF16)],
        compiler_params=pltpu.CompilerParams(vmem_limit_bytes=held + 20 * MIB),
        cost_estimate=pl.CostEstimate(flops=flops, bytes_accessed=1, transcendentals=0),
    )(*arrays, *matrices)
    return made if pieces > 1 else made[0]


def orders(ep):
    bits = list(range(ep.bit_length() - 1))[::-1]
    return (bits, bits[:-2] + bits[:-3:-1])


def send(array, ep, flips):
    pairs = []
    for place in range(ep):
        for core, order in enumerate(orders(ep)):
            to = place
            for flip in flips:
                to ^= 1 << order[flip]
            pairs.append((2 * place + core, 2 * to + core))
    return lax.ppermute(array, ("ep", "sub"), pairs)


def cross(array):
    return lax.ppermute(array, "sub", [(0, 1), (1, 0)])


def add(*terms):
    return sum([t.astype(F32) for t in terms]).astype(BF16)


def on_device(ep, tokens, routes, gates, priority, capacity, w_gate, w_up, w_down):
    tok_rows, width = tokens.shape
    top = routes.shape[1]
    steps = ep.bit_length() - 1
    me = (lax.axis_index("ep") * 2 + lax.axis_index("sub")).astype(jnp.int32).reshape(1)
    held = prepare(me, tokens, routes, gates, priority)
    for step in range(steps - 3):
        held = jnp.concatenate([held, send(held, ep, [step])])
    base = held.shape[0]
    own1, own2, own4 = send(held, ep, [-3]), send(held, ep, [-2]), send(held, ep, [-1])
    first = cross(held)
    matrices = load(w_gate, w_up, w_down)
    own1, first, matrices = lax.optimization_barrier((own1, first, matrices))
    crossed = cross(pack([own1, own2, own4]))
    own3 = send(own1, ep, [-2])
    own5 = send(own1, ep, [-1])
    own6 = send(own2, ep, [-1])
    theirs = expert([first, crossed], matrices)
    own3, theirs = lax.optimization_barrier((own3, theirs))
    own7 = send(own3, ep, [-1])
    far_crossed = [cross(o) for o in (own3, own6, own5)]
    far_made = expert([own3, own5, own6], matrices)
    own3, own5, own6, own7, theirs, far_made = lax.optimization_barrier((own3, own5, own6, own7, theirs, far_made))
    far = [own5, own7, own3, own6]
    last_crossed = cross(own7)
    last_made = expert([own7], matrices)
    far_crossed, last_crossed, last_made = lax.optimization_barrier((far_crossed, last_crossed, last_made))
    last_back, first_back = expert([*far_crossed, last_crossed], matrices, 2)
    first_back = cross(first_back)
    near = [held, own1, own2, own4]
    weights = weigh(me, capacity, near + far + [first, crossed, *far_crossed, last_crossed], top, tok_rows)
    weights, theirs, last_back = lax.optimization_barrier((weights, theirs, last_back))
    last_back = cross(last_back)

    def part(mine, back, block, place):
        return [(mine, block, place), (back, block, 8 + place)]

    send5, send7 = combine(
        [far_made, last_made, first_back], weights, [[(0, 1, 4), (2, 0, 12)], [(1, 0, 5), (2, 1, 13)]]
    )
    back7 = send(send7, ep, [-1])
    back5 = send(send5, ep, [-1])
    near_made = expert(near, matrices)
    near_made, back7 = lax.optimization_barrier((near_made, back7))
    send3, send6 = combine(
        [far_made, last_back, back7],
        weights,
        [[(0, 0, 6), (1, 0, 14), (2, 0, None)], [(0, 2, 7), (1, 1, 15)]],
    )
    back3 = send(send3, ep, [-2])
    near_back = cross(theirs)
    near_made, send3 = lax.optimization_barrier((near_made, send3))
    (send4,) = combine([near_made, near_back], weights, [part(0, 1, 3, 3)])
    back4 = send(send4, ep, [-1])
    send6, send4 = lax.optimization_barrier((send6, send4))
    back6 = send(send6, ep, [-1])
    back3, back5, send4 = lax.optimization_barrier((back3, back5, send4))
    (send1,) = combine([near_made, near_back, back3, back5], weights, [part(0, 1, 1, 1) + [(2, 0, None), (3, 0, None)]])
    back1 = send(send1, ep, [-3])
    back6, send1 = lax.optimization_barrier((back6, send1))
    (send2,) = combine([near_made, near_back, back6], weights, [part(0, 1, 2, 2) + [(2, 0, None)]])
    back2 = send(send2, ep, [-2])
    (total,) = combine([near_made, near_back, back4], weights, [part(0, 1, 0, 0) + [(2, 0, None)]], F32)
    back1, total = lax.optimization_barrier((back1, total))
    (total,) = combine([total, back1], weights, [[(0, 0, None), (1, 0, None)]], F32)
    back2, total = lax.optimization_barrier((back2, total))
    (total,) = combine([total, back2], weights, [[(0, 0, None), (1, 0, None)]])
    for step in range(steps - 3)[::-1]:
        half = total.shape[0] // 2
        total = add(total[:half], send(total[half:], ep, [step]))
    return total


def solution(mesh):
    in_specs = (
        P(("groups", "ep", "sub"), None),
        P(("groups", "ep", "sub"), None),
        P(("groups", "ep", "sub"), None),
        P(("groups", "ep", "sub")),
        P(),
        P(("ep", "sub"), None, None),
        P(("ep", "sub"), None, None),
        P(("ep", "sub"), None, None),
    )
    out_specs = P(("groups", "ep", "sub"), None)
    return jax.shard_map(
        functools.partial(on_device, mesh.shape["ep"]),
        mesh=mesh,
        in_specs=in_specs,
        out_specs=out_specs,
        check_vma=False,
    )
```

```python
import functools

import jax
import jax.numpy as jnp
from jax import lax
from jax.experimental import pallas as pl
from jax.experimental.pallas import tpu as pltpu
from jax.sharding import PartitionSpec as P

F32 = jnp.float32
BF16 = jnp.bfloat16
LANES = 128
BIG = 1e9
MIB = 1024 * 1024


def iota(shape, dim):
    return lax.broadcasted_iota(jnp.int32, shape, dim)


def prepare_kernel(me_ref, tokens_ref, routes_ref, gates_ref, prio_ref, rows_ref):
    rows, width = tokens_ref.shape
    top = routes_ref.shape[0]
    for block in range(width // LANES):
        lanes = slice(block * LANES, (block + 1) * LANES)
        x = tokens_ref[:, lanes].astype(F32)
        largest = jnp.max(jnp.abs(x), axis=1, keepdims=True)
        scale = ((largest + 1e-06) / 448.0).astype(BF16).astype(F32)
        quantized = (x / scale).astype(BF16)
        rows_ref[:, lanes] = (quantized.astype(F32) * scale).astype(BF16)
    gates = gates_ref[...]
    high = gates.astype(BF16)
    middle = (gates - high.astype(F32)).astype(BF16)
    low = (gates - high.astype(F32) - middle.astype(F32)).astype(BF16)
    place, token = iota((top, rows), 0), iota((top, rows), 1)
    other = jnp.where(place == 0, prio_ref[...], jnp.where(place == 1, me_ref[0], token))
    fields = [routes_ref[...].astype(F32), high.astype(F32), middle.astype(F32), low.astype(F32), other.astype(F32)]
    stacked = jnp.concatenate(fields, axis=0)
    place = iota((stacked.shape[0], LANES), 0) == iota((stacked.shape[0], LANES), 1)
    facts = lax.dot_general(
        stacked.astype(BF16), place.astype(F32).astype(BF16), (((0,), (0,)), ((), ())), preferred_element_type=F32
    )
    rows_ref[:, width:] = facts.astype(BF16)


def prepare(me, tokens, routes, gates, priority):
    rows, width = tokens.shape
    return pl.pallas_call(
        prepare_kernel,
        in_specs=[pl.BlockSpec(memory_space=pltpu.SMEM)] + [pl.BlockSpec(memory_space=pltpu.VMEM)] * 4,
        out_specs=pl.BlockSpec(memory_space=pltpu.VMEM),
        out_shape=jax.ShapeDtypeStruct((rows, width + LANES), BF16),
    )(me, tokens, routes.T, gates.T, priority.reshape(1, rows))


def weigh_kernel(top, tok_rows, me_ref, capacity_ref, *refs):
    fact_refs, out_ref, (all_ref, key_ref, row_ref) = refs[:-4], refs[-4], refs[-3:]
    total = all_ref.shape[0]
    at = 0
    for ref in fact_refs:
        rows, wide = ref.shape
        all_ref[at : at + rows, :] = ref[:, wide - LANES :]
        at += rows
    eye = iota((LANES, LANES), 0) == iota((LANES, LANES), 1)
    lane = iota((LANES, LANES), 1)
    tiles = total // LANES
    mine = tiles // 2
    experts = (me_ref[0], me_ref[0] + 1 - 2 * lax.rem(me_ref[0], 2))
    worth = jnp.where(lane == 4 * top, float(total), 0.0)
    worth = jnp.where(lane == 4 * top + 1, float(tok_rows), jnp.where(lane == 4 * top + 2, 1.0, worth))

    def read(i, _, own):
        facts = all_ref[pl.ds(pl.multiple_of(i * LANES, LANES), LANES), :].astype(F32)
        values = (
            pltpu.roll(facts, LANES - top, 1)
            + pltpu.roll(facts, LANES - 2 * top, 1)
            + pltpu.roll(facts, LANES - 3 * top, 1)
        )
        order = jnp.sum(facts * worth, axis=1, keepdims=True)
        for e, expert in enumerate(experts):
            named = (lane < top) & (facts == expert.astype(F32))
            gate = jnp.sum(jnp.where(named, values, 0.0), axis=1, keepdims=True)
            key = jnp.where(gate > 0.0, order, BIG)
            row_ref[e, pl.ds(i, 1), :] = jnp.sum(jnp.where(eye, key, 0.0), axis=0, keepdims=True)
            if own:
                key_ref[e, i] = jnp.broadcast_to(key, (LANES, LANES))
                held = pl.ds(pl.multiple_of((e * mine + i) * LANES, LANES), LANES)
                out_ref[held, :] = jnp.broadcast_to(gate, (LANES, LANES))
        return 0

    lax.fori_loop(0, mine, functools.partial(read, own=True), 0, unroll=min(mine, 4))
    lax.fori_loop(mine, tiles, functools.partial(read, own=False), 0, unroll=min(mine, 4))
    for e, expert in enumerate(experts):
        limit = capacity_ref[expert].astype(F32)

        def judge(i, _, e=e, limit=limit):
            held = pl.ds(pl.multiple_of((e * mine + i) * LANES, LANES), LANES)
            key = key_ref[e, i]

            def count(j, smaller):
                return smaller + (row_ref[e, pl.ds(j, 1), :] < key).astype(F32)

            smaller = lax.fori_loop(0, tiles, count, jnp.zeros((LANES, LANES), F32), unroll=min(tiles, 8))
            rank = jnp.sum(smaller, axis=1, keepdims=True)
            out_ref[held, :] = jnp.where(rank < limit, out_ref[held, :], 0.0)
            return 0

        lax.fori_loop(0, mine, judge, 0, unroll=min(mine, 4))


def weigh(me, capacity, facts, top, tok_rows):
    total = sum(f.shape[0] for f in facts)
    tiles = total // LANES
    return pl.pallas_call(
        functools.partial(weigh_kernel, top, tok_rows),
        in_specs=[pl.BlockSpec(memory_space=pltpu.SMEM)] * 2
        + [pl.BlockSpec(memory_space=pltpu.VMEM)] * len(facts),
        out_specs=pl.BlockSpec(memory_space=pltpu.VMEM),
        out_shape=jax.ShapeDtypeStruct((total, LANES), F32),
        scratch_shapes=[
            pltpu.VMEM((total, LANES), BF16),
            pltpu.VMEM((2, tiles // 2, LANES, LANES), F32),
            pltpu.VMEM((2, tiles, LANES), F32),
        ],
        compiler_params=pltpu.CompilerParams(vmem_limit_bytes=24 * MIB),
        cost_estimate=pl.CostEstimate(flops=1, bytes_accessed=1, transcendentals=0),
    )(me, capacity, *facts)


def pack_kernel(*refs):
    rows = refs[0].shape[0]
    for k, ref in enumerate(refs[:-1]):
        refs[-1][k * rows : (k + 1) * rows, :] = ref[...]


def pack(blocks):
    rows, wide = blocks[0].shape
    return pl.pallas_call(
        pack_kernel,
        in_specs=[pl.BlockSpec(memory_space=pltpu.VMEM)] * len(blocks),
        out_specs=pl.BlockSpec(memory_space=pltpu.VMEM),
        out_shape=jax.ShapeDtypeStruct((len(blocks) * rows, wide), BF16),
        compiler_params=pltpu.CompilerParams(vmem_limit_bytes=24 * MIB),
        cost_estimate=pl.CostEstimate(flops=1, bytes_accessed=1, transcendentals=0),
    )(*blocks)


def combine_kernel(rows, sums, weighted, *refs):
    ins, outs = refs[: -len(sums)], refs[-len(sums) :]
    width = outs[0].shape[1]
    for lanes in range(0, width, 256):
        for terms, out in zip(sums, outs):
            total = None
            for which, first, place in terms:
                value = ins[which][first : first + rows, lanes : lanes + 256].astype(F32)
                if place is not None:
                    value = value * ins[weighted][place : place + rows, :1]
                total = value if total is None else total + value
            out[:, lanes : lanes + 256] = total.astype(out.dtype)


def combine(arrays, weights, sums, kind=BF16):
    rows = weights.shape[0] // 16
    width = arrays[0].shape[1]
    sums = [[(a, b * rows, None if p is None else p * rows) for a, b, p in terms] for terms in sums]
    return pl.pallas_call(
        functools.partial(combine_kernel, rows, sums, len(arrays)),
        in_specs=[pl.BlockSpec(memory_space=pltpu.VMEM)] * (len(arrays) + 1),
        out_specs=[pl.BlockSpec(memory_space=pltpu.VMEM)] * len(sums),
        out_shape=[jax.ShapeDtypeStruct((rows, width), kind)] * len(sums),
        compiler_params=pltpu.CompilerParams(vmem_limit_bytes=24 * MIB),
        cost_estimate=pl.CostEstimate(flops=1, bytes_accessed=1, transcendentals=0),
    )(*arrays, weights)


def load_kernel(*refs):
    count = len(refs) // 2
    sems = refs[-1]
    copies = [pltpu.make_async_copy(refs[k], refs[count + k], sems.at[k]) for k in range(count)]
    for copy in copies:
        copy.start()
    for copy in copies:
        copy.wait()


def load(*arrays):
    size = sum(a.size * 2 for a in arrays)
    return pl.pallas_call(
        load_kernel,
        in_specs=[pl.BlockSpec(memory_space=pl.ANY)] * len(arrays),
        out_specs=[pl.BlockSpec(memory_space=pltpu.VMEM)] * len(arrays),
        out_shape=[jax.ShapeDtypeStruct(a.shape, a.dtype) for a in arrays],
        scratch_shapes=[pltpu.SemaphoreType.DMA((len(arrays),))],
        compiler_params=pltpu.CompilerParams(vmem_limit_bytes=size + 4 * MIB),
    )(*arrays)


FF_TILE, OUT_TILE = 256, 512


def expert_kernel(pieces, *refs):
    x_refs, (gate_ref, up_ref, down_ref) = refs[: -5 - pieces], refs[-5 - pieces : -2 - pieces]
    out_refs, (x, hidden) = refs[-2 - pieces : -2], refs[-2:]
    width, ff = x.shape[1], hidden.shape[1]
    at = 0
    for ref in x_refs:
        x[at : at + ref.shape[0], :] = ref[:, :width]
        at += ref.shape[0]
    for k in range(ff // FF_TILE):
        lanes = slice(k * FF_TILE, (k + 1) * FF_TILE)
        gated = jnp.dot(x[...], gate_ref[0, :, lanes], preferred_element_type=F32)
        upward = jnp.dot(x[...], up_ref[0, :, lanes], preferred_element_type=F32)
        hidden[:, lanes] = (gated / (1.0 + jnp.exp(-gated)) * upward).astype(BF16)
    for k in range(width // OUT_TILE):
        lanes = slice(k * OUT_TILE, (k + 1) * OUT_TILE)
        made = jnp.dot(hidden[...], down_ref[0, :, lanes], preferred_element_type=F32).astype(BF16)
        rows = made.shape[0] // pieces
        for k, out_ref in enumerate(out_refs):
            out_ref[:, lanes] = made[k * rows : (k + 1) * rows]


def expert(arrays, matrices, pieces=1, flops=1):
    ff, width = matrices[2].shape[1:]
    rows = sum(a.shape[0] for a in arrays)
    held = rows * 2 * (width + ff) + 4 * rows * (2 * FF_TILE + OUT_TILE)
    made = pl.pallas_call(
        functools.partial(expert_kernel, pieces),
        in_specs=[pl.BlockSpec(memory_space=pltpu.VMEM)] * (len(arrays) + 3),
        out_specs=[pl.BlockSpec(memory_space=pltpu.VMEM)] * pieces,
        out_shape=[jax.ShapeDtypeStruct((rows // pieces, width), BF16)] * pieces,
        scratch_shapes=[pltpu.VMEM((rows, width), BF16), pltpu.VMEM((rows, ff), BF16)],
        compiler_params=pltpu.CompilerParams(vmem_limit_bytes=held + 20 * MIB),
        cost_estimate=pl.CostEstimate(flops=flops, bytes_accessed=1, transcendentals=0),
    )(*arrays, *matrices)
    return made if pieces > 1 else made[0]


def orders(ep):
    bits = list(range(ep.bit_length() - 1))[::-1]
    return (bits, bits[:-2] + bits[:-3:-1])


def send(array, ep, flips):
    pairs = []
    for place in range(ep):
        for core, order in enumerate(orders(ep)):
            to = place
            for flip in flips:
                to ^= 1 << order[flip]
            pairs.append((2 * place + core, 2 * to + core))
    return lax.ppermute(array, ("ep", "sub"), pairs)


def cross(array):
    return lax.ppermute(array, "sub", [(0, 1), (1, 0)])


def add(*terms):
    return sum([t.astype(F32) for t in terms]).astype(BF16)


def on_device(ep, tokens, routes, gates, priority, capacity, w_gate, w_up, w_down):
    tok_rows, width = tokens.shape
    top = routes.shape[1]
    steps = ep.bit_length() - 1
    me = (lax.axis_index("ep") * 2 + lax.axis_index("sub")).astype(jnp.int32).reshape(1)
    held = prepare(me, tokens, routes, gates, priority)
    for step in range(steps - 3):
        held = jnp.concatenate([held, send(held, ep, [step])])
    base = held.shape[0]
    own1, own2, own4 = send(held, ep, [-3]), send(held, ep, [-2]), send(held, ep, [-1])
    first = cross(held)
    matrices = load(w_gate, w_up, w_down)
    own1, first, matrices = lax.optimization_barrier((own1, first, matrices))
    crossed = cross(pack([own1, own2, own4]))
    own3 = send(own1, ep, [-2])
    own5 = send(own1, ep, [-1])
    own6 = send(own2, ep, [-1])
    theirs = expert([first, crossed], matrices)
    own3, theirs = lax.optimization_barrier((own3, theirs))
    own7 = send(own3, ep, [-1])
    far_crossed = [cross(o) for o in (own3, own6, own5)]
    far_made = expert([own3, own5, own6], matrices)
    own3, own5, own6, own7, theirs, far_made = lax.optimization_barrier((own3, own5, own6, own7, theirs, far_made))
    far = [own5, own7, own3, own6]
    last_crossed = cross(own7)
    last_made = expert([own7], matrices)
    far_crossed, last_crossed, last_made = lax.optimization_barrier((far_crossed, last_crossed, last_made))
    last_back, first_back = expert([*far_crossed, last_crossed], matrices, 2)
    first_back = cross(first_back)
    near = [held, own1, own2, own4]
    weights = weigh(me, capacity, near + far + [first, crossed, *far_crossed, last_crossed], top, tok_rows)
    weights, last_back = lax.optimization_barrier((weights, last_back))
    last_back = cross(last_back)

    def part(mine, back, block, place):
        return [(mine, block, place), (back, block, 8 + place)]

    send5, send7 = combine(
        [far_made, last_made, first_back], weights, [[(0, 1, 4), (2, 0, 12)], [(1, 0, 5), (2, 1, 13)]]
    )
    back7 = send(send7, ep, [-1])
    back5 = send(send5, ep, [-1])
    send3, send6 = combine(
        [far_made, last_back, back7],
        weights,
        [[(0, 0, 6), (1, 0, 14), (2, 0, None)], [(0, 2, 7), (1, 1, 15)]],
    )
    send3, theirs = lax.optimization_barrier((send3, theirs))
    back3 = send(send3, ep, [-2])
    near_made = expert(near, matrices)
    near_made, send6 = lax.optimization_barrier((near_made, send6))
    back6 = send(send6, ep, [-1])
    near_back = cross(theirs)
    (send4,) = combine([near_made, near_back], weights, [part(0, 1, 3, 3)])
    back4 = send(send4, ep, [-1])
    back3, back5, send4 = lax.optimization_barrier((back3, back5, send4))
    (send1,) = combine([near_made, near_back, back3, back5], weights, [part(0, 1, 1, 1) + [(2, 0, None), (3, 0, None)]])
    back1 = send(send1, ep, [-3])
    back6, send1 = lax.optimization_barrier((back6, send1))
    (send2,) = combine([near_made, near_back, back6], weights, [part(0, 1, 2, 2) + [(2, 0, None)]])
    back2 = send(send2, ep, [-2])
    (total,) = combine([near_made, near_back, back4], weights, [part(0, 1, 0, 0) + [(2, 0, None)]], F32)
    back1, total = lax.optimization_barrier((back1, total))
    (total,) = combine([total, back1], weights, [[(0, 0, None), (1, 0, None)]], F32)
    back2, total = lax.optimization_barrier((back2, total))
    (total,) = combine([total, back2], weights, [[(0, 0, None), (1, 0, None)]])
    for step in range(steps - 3)[::-1]:
        half = total.shape[0] // 2
        total = add(total[:half], send(total[half:], ep, [step]))
    return total


def solution(mesh):
    in_specs = (
        P(("groups", "ep", "sub"), None),
        P(("groups", "ep", "sub"), None),
        P(("groups", "ep", "sub"), None),
        P(("groups", "ep", "sub")),
        P(),
        P(("ep", "sub"), None, None),
        P(("ep", "sub"), None, None),
        P(("ep", "sub"), None, None),
    )
    out_specs = P(("groups", "ep", "sub"), None)
    return jax.shard_map(
        functools.partial(on_device, mesh.shape["ep"]),
        mesh=mesh,
        in_specs=in_specs,
        out_specs=out_specs,
        check_vma=False,
    )
```

```python
import functools

import jax
import jax.numpy as jnp
from jax import lax
from jax.experimental import pallas as pl
from jax.experimental.pallas import tpu as pltpu
from jax.sharding import PartitionSpec as P

F32 = jnp.float32
BF16 = jnp.bfloat16
LANES = 128
BIG = 1e9
MIB = 1024 * 1024


def iota(shape, dim):
    return lax.broadcasted_iota(jnp.int32, shape, dim)


def prepare_kernel(me_ref, tokens_ref, routes_ref, gates_ref, prio_ref, rows_ref):
    rows, width = tokens_ref.shape
    top = routes_ref.shape[0]
    for block in range(width // LANES):
        lanes = slice(block * LANES, (block + 1) * LANES)
        x = tokens_ref[:, lanes].astype(F32)
        largest = jnp.max(jnp.abs(x), axis=1, keepdims=True)
        scale = ((largest + 1e-06) / 448.0).astype(BF16).astype(F32)
        quantized = (x / scale).astype(BF16)
        rows_ref[:, lanes] = (quantized.astype(F32) * scale).astype(BF16)
    gates = gates_ref[...]
    high = gates.astype(BF16)
    middle = (gates - high.astype(F32)).astype(BF16)
    low = (gates - high.astype(F32) - middle.astype(F32)).astype(BF16)
    place, token = iota((top, rows), 0), iota((top, rows), 1)
    other = jnp.where(place == 0, prio_ref[...], jnp.where(place == 1, me_ref[0], token))
    fields = [routes_ref[...].astype(F32), high.astype(F32), middle.astype(F32), low.astype(F32), other.astype(F32)]
    stacked = jnp.concatenate(fields, axis=0)
    place = iota((stacked.shape[0], LANES), 0) == iota((stacked.shape[0], LANES), 1)
    facts = lax.dot_general(
        stacked.astype(BF16), place.astype(F32).astype(BF16), (((0,), (0,)), ((), ())), preferred_element_type=F32
    )
    rows_ref[:, width:] = facts.astype(BF16)


def prepare(me, tokens, routes, gates, priority):
    rows, width = tokens.shape
    return pl.pallas_call(
        prepare_kernel,
        in_specs=[pl.BlockSpec(memory_space=pltpu.SMEM)] + [pl.BlockSpec(memory_space=pltpu.VMEM)] * 4,
        out_specs=pl.BlockSpec(memory_space=pltpu.VMEM),
        out_shape=jax.ShapeDtypeStruct((rows, width + LANES), BF16),
    )(me, tokens, routes.T, gates.T, priority.reshape(1, rows))


def weigh_kernel(top, tok_rows, me_ref, capacity_ref, *refs):
    fact_refs, out_ref, (all_ref, key_ref, row_ref) = refs[:-4], refs[-4], refs[-3:]
    total = all_ref.shape[0]
    at = 0
    for ref in fact_refs:
        rows, wide = ref.shape
        all_ref[at : at + rows, :] = ref[:, wide - LANES :]
        at += rows
    eye = iota((LANES, LANES), 0) == iota((LANES, LANES), 1)
    lane = iota((LANES, LANES), 1)
    tiles = total // LANES
    mine = tiles // 2
    experts = (me_ref[0], me_ref[0] + 1 - 2 * lax.rem(me_ref[0], 2))
    worth = jnp.where(lane == 4 * top, float(total), 0.0)
    worth = jnp.where(lane == 4 * top + 1, float(tok_rows), jnp.where(lane == 4 * top + 2, 1.0, worth))

    def read(i, _, own):
        facts = all_ref[pl.ds(pl.multiple_of(i * LANES, LANES), LANES), :].astype(F32)
        values = (
            pltpu.roll(facts, LANES - top, 1)
            + pltpu.roll(facts, LANES - 2 * top, 1)
            + pltpu.roll(facts, LANES - 3 * top, 1)
        )
        order = jnp.sum(facts * worth, axis=1, keepdims=True)
        for e, expert in enumerate(experts):
            named = (lane < top) & (facts == expert.astype(F32))
            gate = jnp.sum(jnp.where(named, values, 0.0), axis=1, keepdims=True)
            key = jnp.where(gate > 0.0, order, BIG)
            row_ref[e, pl.ds(i, 1), :] = jnp.sum(jnp.where(eye, key, 0.0), axis=0, keepdims=True)
            if own:
                key_ref[e, i] = jnp.broadcast_to(key, (LANES, LANES))
                held = pl.ds(pl.multiple_of((e * mine + i) * LANES, LANES), LANES)
                out_ref[held, :] = jnp.broadcast_to(gate, (LANES, LANES))
        return 0

    lax.fori_loop(0, mine, functools.partial(read, own=True), 0, unroll=min(mine, 4))
    lax.fori_loop(mine, tiles, functools.partial(read, own=False), 0, unroll=min(mine, 4))
    for e, expert in enumerate(experts):
        limit = capacity_ref[expert].astype(F32)

        def judge(i, _, e=e, limit=limit):
            held = pl.ds(pl.multiple_of((e * mine + i) * LANES, LANES), LANES)
            key = key_ref[e, i]

            def count(j, smaller):
                return smaller + (row_ref[e, pl.ds(j, 1), :] < key).astype(F32)

            smaller = lax.fori_loop(0, tiles, count, jnp.zeros((LANES, LANES), F32), unroll=min(tiles, 8))
            rank = jnp.sum(smaller, axis=1, keepdims=True)
            out_ref[held, :] = jnp.where(rank < limit, out_ref[held, :], 0.0)
            return 0

        lax.fori_loop(0, mine, judge, 0, unroll=min(mine, 4))


def weigh(me, capacity, facts, top, tok_rows):
    total = sum(f.shape[0] for f in facts)
    tiles = total // LANES
    return pl.pallas_call(
        functools.partial(weigh_kernel, top, tok_rows),
        in_specs=[pl.BlockSpec(memory_space=pltpu.SMEM)] * 2
        + [pl.BlockSpec(memory_space=pltpu.VMEM)] * len(facts),
        out_specs=pl.BlockSpec(memory_space=pltpu.VMEM),
        out_shape=jax.ShapeDtypeStruct((total, LANES), F32),
        scratch_shapes=[
            pltpu.VMEM((total, LANES), BF16),
            pltpu.VMEM((2, tiles // 2, LANES, LANES), F32),
            pltpu.VMEM((2, tiles, LANES), F32),
        ],
        compiler_params=pltpu.CompilerParams(vmem_limit_bytes=24 * MIB),
        cost_estimate=pl.CostEstimate(flops=1, bytes_accessed=1, transcendentals=0),
    )(me, capacity, *facts)


def pack_kernel(*refs):
    rows = refs[0].shape[0]
    for k, ref in enumerate(refs[:-1]):
        refs[-1][k * rows : (k + 1) * rows, :] = ref[...]


def pack(blocks):
    rows, wide = blocks[0].shape
    return pl.pallas_call(
        pack_kernel,
        in_specs=[pl.BlockSpec(memory_space=pltpu.VMEM)] * len(blocks),
        out_specs=pl.BlockSpec(memory_space=pltpu.VMEM),
        out_shape=jax.ShapeDtypeStruct((len(blocks) * rows, wide), BF16),
        compiler_params=pltpu.CompilerParams(vmem_limit_bytes=24 * MIB),
        cost_estimate=pl.CostEstimate(flops=1, bytes_accessed=1, transcendentals=0),
    )(*blocks)


def combine_kernel(rows, sums, weighted, *refs):
    ins, outs = refs[: -len(sums)], refs[-len(sums) :]
    width = outs[0].shape[1]
    for lanes in range(0, width, 256):
        for terms, out in zip(sums, outs):
            total = None
            for which, first, place in terms:
                value = ins[which][first : first + rows, lanes : lanes + 256].astype(F32)
                if place is not None:
                    value = value * ins[weighted][place : place + rows, :1]
                total = value if total is None else total + value
            out[:, lanes : lanes + 256] = total.astype(out.dtype)


def combine(arrays, weights, sums, kind=BF16):
    rows = weights.shape[0] // 16
    width = arrays[0].shape[1]
    sums = [[(a, b * rows, None if p is None else p * rows) for a, b, p in terms] for terms in sums]
    return pl.pallas_call(
        functools.partial(combine_kernel, rows, sums, len(arrays)),
        in_specs=[pl.BlockSpec(memory_space=pltpu.VMEM)] * (len(arrays) + 1),
        out_specs=[pl.BlockSpec(memory_space=pltpu.VMEM)] * len(sums),
        out_shape=[jax.ShapeDtypeStruct((rows, width), kind)] * len(sums),
        compiler_params=pltpu.CompilerParams(vmem_limit_bytes=24 * MIB),
        cost_estimate=pl.CostEstimate(flops=1, bytes_accessed=1, transcendentals=0),
    )(*arrays, weights)


def load_kernel(*refs):
    count = len(refs) // 2
    sems = refs[-1]
    copies = [pltpu.make_async_copy(refs[k], refs[count + k], sems.at[k]) for k in range(count)]
    for copy in copies:
        copy.start()
    for copy in copies:
        copy.wait()


def load(*arrays):
    size = sum(a.size * 2 for a in arrays)
    return pl.pallas_call(
        load_kernel,
        in_specs=[pl.BlockSpec(memory_space=pl.ANY)] * len(arrays),
        out_specs=[pl.BlockSpec(memory_space=pltpu.VMEM)] * len(arrays),
        out_shape=[jax.ShapeDtypeStruct(a.shape, a.dtype) for a in arrays],
        scratch_shapes=[pltpu.SemaphoreType.DMA((len(arrays),))],
        compiler_params=pltpu.CompilerParams(vmem_limit_bytes=size + 4 * MIB),
    )(*arrays)


FF_TILE, OUT_TILE = 768, 1024


def expert_kernel(pieces, *refs):
    x_refs, (gate_ref, up_ref, down_ref) = refs[: -5 - pieces], refs[-5 - pieces : -2 - pieces]
    out_refs, (x, hidden) = refs[-2 - pieces : -2], refs[-2:]
    width, ff = x.shape[1], hidden.shape[1]
    at = 0
    for ref in x_refs:
        x[at : at + ref.shape[0], :] = ref[:, :width]
        at += ref.shape[0]
    for k in range(ff // FF_TILE):
        lanes = slice(k * FF_TILE, (k + 1) * FF_TILE)
        gated = jnp.dot(x[...], gate_ref[0, :, lanes], preferred_element_type=F32)
        upward = jnp.dot(x[...], up_ref[0, :, lanes], preferred_element_type=F32)
        hidden[:, lanes] = (gated / (1.0 + jnp.exp(-gated)) * upward).astype(BF16)
    for k in range(width // OUT_TILE):
        lanes = slice(k * OUT_TILE, (k + 1) * OUT_TILE)
        made = jnp.dot(hidden[...], down_ref[0, :, lanes], preferred_element_type=F32).astype(BF16)
        rows = made.shape[0] // pieces
        for k, out_ref in enumerate(out_refs):
            out_ref[:, lanes] = made[k * rows : (k + 1) * rows]


def expert(arrays, matrices, pieces=1, flops=1):
    ff, width = matrices[2].shape[1:]
    rows = sum(a.shape[0] for a in arrays)
    held = rows * 2 * (width + ff) + 4 * rows * (2 * FF_TILE + OUT_TILE)
    made = pl.pallas_call(
        functools.partial(expert_kernel, pieces),
        in_specs=[pl.BlockSpec(memory_space=pltpu.VMEM)] * (len(arrays) + 3),
        out_specs=[pl.BlockSpec(memory_space=pltpu.VMEM)] * pieces,
        out_shape=[jax.ShapeDtypeStruct((rows // pieces, width), BF16)] * pieces,
        scratch_shapes=[pltpu.VMEM((rows, width), BF16), pltpu.VMEM((rows, ff), BF16)],
        compiler_params=pltpu.CompilerParams(vmem_limit_bytes=held + 20 * MIB),
        cost_estimate=pl.CostEstimate(flops=flops, bytes_accessed=1, transcendentals=0),
    )(*arrays, *matrices)
    return made if pieces > 1 else made[0]


def orders(ep):
    bits = list(range(ep.bit_length() - 1))[::-1]
    return (bits, bits[:-2] + bits[:-3:-1])


def send(array, ep, flips):
    pairs = []
    for place in range(ep):
        for core, order in enumerate(orders(ep)):
            to = place
            for flip in flips:
                to ^= 1 << order[flip]
            pairs.append((2 * place + core, 2 * to + core))
    return lax.ppermute(array, ("ep", "sub"), pairs)


def cross(array):
    return lax.ppermute(array, "sub", [(0, 1), (1, 0)])


def add(*terms):
    return sum([t.astype(F32) for t in terms]).astype(BF16)


def on_device(ep, tokens, routes, gates, priority, capacity, w_gate, w_up, w_down):
    tok_rows, width = tokens.shape
    top = routes.shape[1]
    steps = ep.bit_length() - 1
    me = (lax.axis_index("ep") * 2 + lax.axis_index("sub")).astype(jnp.int32).reshape(1)
    held = prepare(me, tokens, routes, gates, priority)
    for step in range(steps - 3):
        held = jnp.concatenate([held, send(held, ep, [step])])
    base = held.shape[0]
    own1, own2, own4 = send(held, ep, [-3]), send(held, ep, [-2]), send(held, ep, [-1])
    first = cross(held)
    matrices = load(w_gate, w_up, w_down)
    own1, first, matrices = lax.optimization_barrier((own1, first, matrices))
    crossed = cross(pack([own1, own2, own4]))
    own3 = send(own1, ep, [-2])
    own5 = send(own1, ep, [-1])
    own6 = send(own2, ep, [-1])
    theirs = expert([first, crossed], matrices)
    own3, theirs = lax.optimization_barrier((own3, theirs))
    own7 = send(own3, ep, [-1])
    far_crossed = [cross(o) for o in (own3, own6, own5)]
    far_made = expert([own3, own5, own6], matrices)
    own3, own5, own6, own7, theirs, far_made = lax.optimization_barrier((own3, own5, own6, own7, theirs, far_made))
    far = [own5, own7, own3, own6]
    last_crossed = cross(own7)
    last_made = expert([own7], matrices)
    far_crossed, last_crossed, last_made = lax.optimization_barrier((far_crossed, last_crossed, last_made))
    last_back, first_back = expert([*far_crossed, last_crossed], matrices, 2)
    first_back = cross(first_back)
    near = [held, own1, own2, own4]
    weights = weigh(me, capacity, near + far + [first, crossed, *far_crossed, last_crossed], top, tok_rows)
    weights, theirs, last_back = lax.optimization_barrier((weights, theirs, last_back))
    last_back = cross(last_back)

    def part(mine, back, block, place):
        return [(mine, block, place), (back, block, 8 + place)]

    send5, send7 = combine(
        [far_made, last_made, first_back], weights, [[(0, 1, 4), (2, 0, 12)], [(1, 0, 5), (2, 1, 13)]]
    )
    back7 = send(send7, ep, [-1])
    back5 = send(send5, ep, [-1])
    send3, send6 = combine(
        [far_made, last_back, back7],
        weights,
        [[(0, 0, 6), (1, 0, 14), (2, 0, None)], [(0, 2, 7), (1, 1, 15)]],
    )
    back3 = send(send3, ep, [-2])
    near_made = expert(near, matrices)
    near_made, send6 = lax.optimization_barrier((near_made, send6))
    back6 = send(send6, ep, [-1])
    near_back = cross(theirs)
    (send4,) = combine([near_made, near_back], weights, [part(0, 1, 3, 3)])
    back4 = send(send4, ep, [-1])
    back3, back5, send4 = lax.optimization_barrier((back3, back5, send4))
    (send1,) = combine([near_made, near_back, back3, back5], weights, [part(0, 1, 1, 1) + [(2, 0, None), (3, 0, None)]])
    back1 = send(send1, ep, [-3])
    back6, send1 = lax.optimization_barrier((back6, send1))
    (send2,) = combine([near_made, near_back, back6], weights, [part(0, 1, 2, 2) + [(2, 0, None)]])
    back2 = send(send2, ep, [-2])
    (total,) = combine([near_made, near_back, back4], weights, [part(0, 1, 0, 0) + [(2, 0, None)]], F32)
    back1, total = lax.optimization_barrier((back1, total))
    (total,) = combine([total, back1], weights, [[(0, 0, None), (1, 0, None)]], F32)
    back2, total = lax.optimization_barrier((back2, total))
    (total,) = combine([total, back2], weights, [[(0, 0, None), (1, 0, None)]])
    for step in range(steps - 3)[::-1]:
        half = total.shape[0] // 2
        total = add(total[:half], send(total[half:], ep, [step]))
    return total


def solution(mesh):
    in_specs = (
        P(("groups", "ep", "sub"), None),
        P(("groups", "ep", "sub"), None),
        P(("groups", "ep", "sub"), None),
        P(("groups", "ep", "sub")),
        P(),
        P(("ep", "sub"), None, None),
        P(("ep", "sub"), None, None),
        P(("ep", "sub"), None, None),
    )
    out_specs = P(("groups", "ep", "sub"), None)
    return jax.shard_map(
        functools.partial(on_device, mesh.shape["ep"]),
        mesh=mesh,
        in_specs=in_specs,
        out_specs=out_specs,
        check_vma=False,
    )
```
